128 devices in a mesh: dp: 8 (over y, core), seq: 16 (over z, x).
Axes of the slice: x: 4, y: 4, z: 4, core: 2. Of those that a mesh axis runs over, the one named last changes fastest.
Arguments:
- x_branch: bfloat16 [8, 2048, 8192], P('dp', 'seq'), may hold values from -6 to 6
- z_branch: bfloat16 [8, 2048, 8192], P('dp', 'seq'), may hold values from -6 to 6
- out_grad: bfloat16 [8, 2048, 8192], P('dp', 'seq'), may hold values from -6 to 6
- x_weight: bfloat16 [8192, 288], P('seq', 'dp'), may hold values from -0.0625 to 0.0625
- dt_weight: bfloat16 [256, 8192], P('dp', 'seq'), may hold values from -0.375 to 0.375
- conv_weight: float32 [4, 8192], replicated, may hold values from -3 to 3
- conv_bias: float32 [8192], replicated, may hold values from -0.5 to 0.5
- dt_bias: float32 [8192], replicated, may hold values from -4.5 to -3.5
- a_log: float32 [16, 8192], replicated, may hold values from -12 to 1
- d_skip: float32 [8192], replicated, may hold values from 0.5 to 1.5
Outputs:
- mixer_out: bfloat16 [8, 2048, 8192], P('dp', 'seq')
- grad_x_branch: bfloat16 [8, 2048, 8192], P('dp', 'seq')
- grad_z_branch: bfloat16 [8, 2048, 8192], P('dp', 'seq')
- grad_x_weight: float32 [8192, 288], P('seq', 'dp')
- grad_dt_weight: float32 [256, 8192], P('dp', 'seq')
- grad_conv_weight: float32 [4, 8192], replicated
- grad_conv_bias: float32 [8192], replicated
- grad_dt_bias: float32 [8192], replicated
- grad_a_log: float32 [16, 8192], replicated
- grad_d_skip: float32 [8192], replicated
The draws below stay inside these ranges and needn't reach their ends.
All inputs are finite; a program needn't handle non-finite values.
Results may differ from the reference program's by a relative error of at most 0.007.
Values may be sent and summed in bfloat16 or wider, within the bound.
A program may use at most 256 MiB of HBM per device.

```python
import jax
import jax.numpy as jnp
from jax import lax

E = 8192
N = 16
R = 256
TAPS = 4
LEN = 2048
SEQS = 8
PROJ = 288


def draw_a_log(key, part):
    key = jax.random.fold_in(key, 7)
    key_span, key_kind, key_fast = jax.random.split(key, 3)
    slow_span = jnp.exp(jax.random.uniform(key_span, (N, E), jnp.float32, jnp.log(0.2), jnp.log(2.0)))
    slow_rate = slow_span / (0.03 * LEN)
    fast_rate = jnp.exp(jax.random.uniform(key_fast, (N, E), jnp.float32, jnp.log(1.0 / 50.0), jnp.log(1.0 / 30.0))) / 0.03
    fast_share = 0.5
    is_fast = jax.random.bernoulli(key_kind, fast_share, (1, E))
    return jnp.log(jnp.where(is_fast, fast_rate, slow_rate)).astype(jnp.float32)


def with_spikes(result, own_key, source, target, shards_of, factor):
    def block_of(axis_at):
        return (jnp.arange(result.shape[axis_at]) // (result.shape[axis_at] // shards_of)).reshape((-1,) + (1,) * (result.ndim - 1 - axis_at))

    near = jax.random.permutation(own_key, shards_of)[block_of(target)]
    second = (block_of(target) + shards_of // 2) % shards_of
    return jnp.where((block_of(source) == near) | (block_of(source) == second), factor * result, result)


def steps_of(key, shape, cuts, smallest, high):
    def one(position, parts):
        heights = jax.random.uniform(jax.random.fold_in(jax.random.fold_in(key, 6), position), (parts,), jnp.float32, smallest / len(cuts), high / len(cuts))
        return jnp.repeat(jnp.exp(heights), shape[position] // parts).reshape((-1,) + (1,) * (len(shape) - position - 1))

    gain = one(*cuts[0])
    for cut in cuts[1:]:
        gain = gain * one(*cut)
    return gain


def scatter_about(own_key, dims, deviation, reach, cuts=(), kind=jnp.bfloat16):
    array = jax.random.normal(own_key, dims, jnp.float32) * deviation
    if len(cuts) > 0:
        array = steps_of(own_key, dims, cuts, -0.22, 0.18) * array
    return jnp.clip(array, min=-reach, max=reach).astype(kind)


def heavy_noise(own_key, dims, scale, limit, cuts, heavy, kind=jnp.bfloat16):
    drawn = scale * jax.random.normal(own_key, dims, jnp.float32)
    if cuts:
        drawn = drawn * steps_of(own_key, dims, cuts, -0.22, 0.18)
    return jnp.clip(with_spikes(drawn, jax.random.fold_in(own_key, 3), *heavy), -limit, limit).astype(kind)


def setup_inputs(seed: int = 0) -> dict:
    seeds = jax.random.split(jax.random.key(seed), 11)
    return {
        "x_branch": heavy_noise(seeds[0], (SEQS, LEN, E), 1.0, 6.0, ((0, 8), (1, 16)), (1, 2, 16, 2.0)),
        "z_branch": scatter_about(seeds[1], (SEQS, LEN, E), 1.0, 6.0, ((0, 8), (1, 16))),
        "out_grad": heavy_noise(seeds[2], (SEQS, LEN, E), 1.0, 6.0, ((0, 8), (1, 16)), (1, 2, 16, 2.0)),
        "x_weight": scatter_about(seeds[3], (E, PROJ), E ** -0.5, 0.0625, ((0, 16), (1, 8))),
        "dt_weight": scatter_about(seeds[4], (R, E), R ** -0.5, 0.375, ((0, 8), (1, 16))),
        "conv_weight": scatter_about(seeds[5], (TAPS, E), TAPS ** -0.5, 3.0, (), jnp.float32),
        "conv_bias": jnp.clip(jax.random.uniform(seeds[6], (E,), jnp.float32, -0.5, 0.5), -0.5, 0.5),
        "dt_bias": jnp.clip(jax.random.uniform(seeds[7], (E,), jnp.float32, -4.5, -3.5), -4.5, -3.5),
        "a_log": draw_a_log(jax.random.fold_in(seeds[10], 71), 0),
        "d_skip": jnp.clip(jax.random.uniform(seeds[9], (E,), jnp.float32, 0.5, 1.5), 0.5, 1.5),
    }


def silu_slope(values):
    logistic = jax.nn.sigmoid(values)
    return logistic * (1.0 + values * (1.0 - logistic))


def forward_pass(a_mat, start_state, step_size, drive_term, b_mat, c_mat, block_len):
    block_count = step_size.shape[0] // block_len

    def shaped(source):
        return source.reshape((block_count, block_len) + source.shape[1:])

    def advance(carried, pieces):
        step_blk, drive_blk, b_blk, c_blk = pieces
        first_state = carried
        outputs = []
        for offset in range(block_len):
            carried = jnp.exp(step_blk[offset][None, :] * a_mat) * carried + b_blk[offset][:, None] * drive_blk[offset][None, :]
            outputs.append(jnp.sum(c_blk[offset][:, None] * carried, axis=0))
        return carried, (first_state, jnp.stack(outputs))

    final_state, (checks, scanned) = lax.scan(advance, start_state, (shaped(step_size), shaped(drive_term), shaped(b_mat), shaped(c_mat)))
    return checks, scanned.reshape(step_size.shape)


def backward_pass(a_mat, checks, entering, step_size, drive_term, b_mat, c_mat, g_state, block_len):
    block_count = step_size.shape[0] // block_len

    def shaped(source):
        return source.reshape((block_count, block_len) + source.shape[1:])

    def retreat(carried, pieces):
        adjoint_next, rate_grad = carried
        first_state, step_blk, drive_blk, b_blk, c_blk, g_blk = pieces
        history = []
        current = first_state
        for offset in range(block_len):
            factor = jnp.exp(step_blk[offset][None, :] * a_mat)
            updated = factor * current + b_blk[offset][:, None] * drive_blk[offset][None, :]
            history.append((factor, current, updated))
            current = updated
        drive_grads, rate_grads, b_grads, c_grads = [], [], [], []
        for offset in range(block_len - 1, -1, -1):
            factor, earlier, updated = history[offset]
            adjoint = c_blk[offset][:, None] * g_blk[offset][None, :] + adjoint_next
            drive_grads.append(jnp.sum(adjoint * b_blk[offset][:, None], axis=0))
            b_grads.append(jnp.sum(adjoint * drive_blk[offset][None, :], axis=1))
            c_grads.append(jnp.sum(updated * g_blk[offset][None, :], axis=1))
            moment = adjoint * factor * earlier
            rate_grads.append(jnp.sum(moment * a_mat, axis=0))
            rate_grad = rate_grad + moment * step_blk[offset][None, :]
            adjoint_next = factor * adjoint
        stacked = tuple(jnp.stack(collected[::-1]) for collected in (drive_grads, rate_grads, b_grads, c_grads))
        return (adjoint_next, rate_grad), stacked

    pieces_all = (checks, shaped(step_size), shaped(drive_term), shaped(b_mat), shaped(c_mat), shaped(g_state))
    carried, stacked = lax.scan(retreat, (entering, jnp.zeros(a_mat.shape, jnp.float32)), pieces_all, reverse=True)
    flattened = tuple(stacked_part.reshape((step_size.shape[0],) + stacked_part.shape[2:]) for stacked_part in stacked)
    return carried[1], flattened


def one_sequence(x_tok, z_tok, g_tok, x_weight, dt_weight, conv_weight, conv_bias, dt_bias, a_log, d_skip):
    tap_count = conv_weight.shape[0]
    length = x_tok.shape[0]
    width = x_tok.shape[1]
    extended = jnp.concatenate([jnp.zeros((tap_count - 1, width), x_tok.dtype), x_tok], axis=0).astype(jnp.float32)
    conv_pre = jnp.zeros((length, width), jnp.float32) + conv_bias[None, :]
    for tap_index in range(tap_count):
        conv_pre = conv_pre + conv_weight[tap_index][None, :] * extended[tap_index:tap_index + length]
    x_conv = jax.nn.silu(conv_pre).astype(jnp.bfloat16)
    x_wide = x_conv.astype(jnp.float32)
    projected = jnp.dot(x_conv, x_weight, preferred_element_type=jnp.float32)
    low_part = projected[:, :R].astype(jnp.bfloat16)
    b_mat = projected[:, R:R + N]
    c_mat = projected[:, R + N:]
    rate_pre = jnp.dot(low_part, dt_weight, preferred_element_type=jnp.float32) + dt_bias[None, :]
    step_size = jax.nn.softplus(rate_pre)
    a_mat = -jnp.exp(a_log)
    drive_term = step_size * x_wide
    zero_state = jnp.zeros(a_mat.shape, jnp.float32)
    checks, scanned = forward_pass(a_mat, zero_state, step_size, drive_term, b_mat, c_mat, 16)
    z_wide = z_tok.astype(jnp.float32)
    gate_act = jax.nn.silu(z_wide)
    inner_sum = scanned + d_skip[None, :] * x_wide
    mixer_out = (gate_act * inner_sum).astype(jnp.bfloat16)
    g_wide = g_tok.astype(jnp.float32)
    g_state = g_wide * gate_act
    grad_z = (g_wide * inner_sum * silu_slope(z_wide)).astype(jnp.bfloat16)
    g_amat, (g_drive, g_rate, g_bmat, g_cmat) = backward_pass(a_mat, checks, zero_state, step_size, drive_term, b_mat, c_mat, g_state, 16)
    g_pre = (g_drive * x_wide + g_rate) * jax.nn.sigmoid(rate_pre)
    g_pre_b = g_pre.astype(jnp.bfloat16)
    grad_dt_weight = jnp.dot(low_part.T, g_pre_b, preferred_element_type=jnp.float32)
    g_low = jnp.dot(g_pre_b, dt_weight.T, preferred_element_type=jnp.float32)
    g_proj = jnp.concatenate([g_low, g_bmat, g_cmat], axis=1).astype(jnp.bfloat16)
    grad_x_weight = jnp.dot(x_conv.T, g_proj, preferred_element_type=jnp.float32)
    g_conv_x = g_drive * step_size + g_state * d_skip[None, :] + jnp.dot(g_proj, x_weight.T, preferred_element_type=jnp.float32)
    g_conv = g_conv_x * silu_slope(conv_pre)
    g_extended = jnp.concatenate([g_conv, jnp.zeros((tap_count - 1, width), jnp.float32)], axis=0)
    grad_x = jnp.zeros((length, width), jnp.float32)
    for tap_index in range(tap_count):
        begin = tap_count - 1 - tap_index
        grad_x = grad_x + conv_weight[tap_index][None, :] * g_extended[begin:begin + length]
    grad_conv_w = jnp.stack([jnp.sum(g_conv * extended[tap_index:tap_index + length], axis=0) for tap_index in range(tap_count)])
    grad_conv_b = jnp.sum(g_conv, axis=0)
    grad_bias = jnp.sum(g_pre, axis=0)
    grad_skip = jnp.sum(g_state * x_wide, axis=0)
    return (mixer_out, grad_x.astype(jnp.bfloat16), grad_z, grad_x_weight, grad_dt_weight, grad_conv_w, grad_conv_b, grad_bias, g_amat, grad_skip)


def reference(x_branch, z_branch, out_grad, x_weight, dt_weight, conv_weight, conv_bias, dt_bias, a_log, d_skip):
    def single(slices):
        return one_sequence(slices[0], slices[1], slices[2], x_weight, dt_weight, conv_weight, conv_bias, dt_bias, a_log, d_skip)

    results = lax.map(single, (x_branch, z_branch, out_grad))
    a_mat = -jnp.exp(a_log)
    return (results[0], results[1], results[2], jnp.sum(results[3], axis=0), jnp.sum(results[4], axis=0), jnp.sum(results[5], axis=0), jnp.sum(results[6], axis=0), jnp.sum(results[7], axis=0), jnp.sum(results[8], axis=0) * a_mat, jnp.sum(results[9], axis=0))
```

```python
import functools

import jax
import jax.numpy as jnp
from jax import lax
from jax.experimental import pallas as pl
from jax.experimental.pallas import tpu as pltpu
from jax.sharding import PartitionSpec as P

T = 128
N = 16
LN2 = 0.6931471805599453
LOG2E = 1.4426950408889634


def local_scan_kernel(low_ref, w_ref, x_ref, z_ref, g_ref, bias_ref, a2_ref, bc_ref,
              step_ref, drive_ref, gs_ref, sig_ref, ends_ref, tot_ref, scr):
    low = low_ref[...]
    for half in range(2):
        dt = w_ref[half, :, 48:, :].reshape(256, 512)
        cols = pl.ds(512 * half, 512)
        rate = jnp.dot(low, dt, preferred_element_type=jnp.float32) + bias_ref[:, cols]
        e = jnp.exp(-jnp.abs(rate))
        step = jnp.maximum(rate, 0.0) + jnp.log1p(e)
        sig_ref[:, cols] = jnp.where(rate >= 0, 1.0, e) / (1.0 + e)
        xw = x_ref[:, cols].astype(jnp.float32)
        z = z_ref[:, cols].astype(jnp.float32)
        gs = g_ref[:, cols].astype(jnp.float32) * (z * jax.nn.sigmoid(z))
        drive = step * xw
        for s in range(4):
            part = slice(128 * s, 128 * s + 128)
            step_ref[:, 4 * half + s, :] = step[:, part]
            drive_ref[:, 4 * half + s, :] = drive[:, part]
            gs_ref[:, 4 * half + s, :] = gs[:, part]

    def body(t, carry):
        tot, ends, prods, lams = carry
        st = step_ref[t]
        dr = drive_ref[t]
        gv = gs_ref[t]
        ne, np_, nl = [], [], []
        for n in range(N):
            f = jnp.exp2(st * a2_ref[n])
            b = bc_ref[n, pl.ds(t, 1), :]
            c = bc_ref[N + n, pl.ds(t, 1), :]
            ne.append(f * ends[n] + b * dr)
            p = prods[n] * f
            np_.append(p)
            nl.append(lams[n] + p * (c * gv))
        return tot + st, tuple(ne), tuple(np_), tuple(nl)

    zero = jnp.zeros((8, 128), jnp.float32)
    one = jnp.ones((8, 128), jnp.float32)
    tot, ends, prods, lams = lax.fori_loop(0, T, body, (zero, (zero,) * N, (one,) * N, (zero,) * N))
    for n in range(N):
        for half in range(2):
            scr[half, 4 * n:4 * n + 4, :] = ends[n][4 * half:4 * half + 4]
            scr[half, 64 + 4 * n:64 + 4 * n + 4, :] = lams[n][4 * half:4 * half + 4]
    ends_ref[...] = scr[...].astype(jnp.bfloat16)
    for half in range(2):
        tot_ref[half, 0:4, :] = tot[4 * half:4 * half + 4]
        tot_ref[half, 4:8, :] = jnp.zeros((4, 128), jnp.float32)

def local_scan(low, wg, x_conv, z, g, bias, a2, bc):
    E = x_conv.shape[1]; C = E // 1024
    nat = pl.BlockSpec((T, 1024), lambda i: (0, i))
    tri = pl.BlockSpec((T, 8, 128), lambda i: (0, i, 0))
    full = lambda shape: pl.BlockSpec(shape, lambda i: (0,) * len(shape))
    f32 = jnp.float32
    return pl.pallas_call(
        local_scan_kernel, grid=(C,), name="local_scan",
        in_specs=[full((T, 256)), pl.BlockSpec((2, 8, 80, 512), lambda i: (i, 0, 0, 0)), nat, nat, nat,
                  pl.BlockSpec((1, 1024), lambda i: (0, i)), pl.BlockSpec((N, 8, 128), lambda i: (0, i, 0)),
                  full((32, T, 128))],
        out_specs=[tri, tri, tri, nat, pl.BlockSpec((2, 128, 128), lambda i: (i, 0, 0)), pl.BlockSpec((2, 8, 128), lambda i: (i, 0, 0))],
        out_shape=[jax.ShapeDtypeStruct((T, E // 128, 128), f32)] * 3 + [jax.ShapeDtypeStruct((T, E), f32),
                   jax.ShapeDtypeStruct((2 * C, 128, 128), jnp.bfloat16), jax.ShapeDtypeStruct((2 * C, 8, 128), f32)],
        scratch_shapes=[pltpu.VMEM((2, 128, 128), f32)],
        compiler_params=pltpu.CompilerParams(vmem_limit_bytes=60 * 2**20),
    )(low, wg, x_conv, z, g, bias, a2, bc)

def main_scan_kernel(step_ref, drive_ref, gs_ref, sig_ref, x_ref, z_ref, g_ref, dskip_ref, a2_ref, bc_ref, ent_ref, w_ref, low_ref,
              mix_ref, gz_ref, gcx_ref, gdt_ref, par_ref, ga_ref, glow_ref, gbc_ref,
              es, us, fs, y3, gd3, gr3, accb, accc, alow):
    i = pl.program_id(0)
    f32 = jnp.float32

    @pl.when(i == 0)
    def _():
        accb[...] = jnp.zeros(accb.shape, f32)
        accc[...] = jnp.zeros(accc.shape, f32)
        alow[...] = jnp.zeros(alow.shape, f32)

    es[...] = ent_ref[...].astype(f32)

    def state(base, n):
        return jnp.concatenate([es[0, base + 4 * n:base + 4 * n + 4, :], es[1, base + 4 * n:base + 4 * n + 4, :]], axis=0)

    def forward(t, hs):
        st, dr, gv = step_ref[t], drive_ref[t], gs_ref[t]
        new = []
        y = None
        for n in range(N):
            f = jnp.exp2(st * a2_ref[n])
            u = f * hs[n]
            fs[t, n] = f
            us[t, n] = u
            h = u + bc_ref[n, pl.ds(t, 1), :] * dr
            new.append(h)
            ch = bc_ref[N + n, pl.ds(t, 1), :] * h
            y = ch if y is None else y + ch
            accc[t, n] += h * gv
        y3[t] = y
        return tuple(new)

    lax.fori_loop(0, T, forward, tuple(state(0, n) for n in range(N)))

    def backward(k, carry):
        adj, ra = carry
        t = T - 1 - k
        st, dr, gv = step_ref[t], drive_ref[t], gs_ref[t]
        na, nr = [], []
        gd = gr = None
        for n in range(N):
            lam = bc_ref[N + n, pl.ds(t, 1), :] * gv + adj[n]
            lb = lam * bc_ref[n, pl.ds(t, 1), :]
            accb[t, n] += lam * dr
            na.append(fs[t, n] * lam)
            m = lam * us[t, n]
            ma = m * a2_ref[n]
            nr.append(ra[n] + m * st)
            gd = lb if gd is None else gd + lb
            gr = ma if gr is None else gr + ma
        gd3[t] = gd
        gr3[t] = gr
        return tuple(na), tuple(nr)

    zero = jnp.zeros((8, 128), f32)
    adj, ra = lax.fori_loop(0, T, backward, (tuple(state(64, n) for n in range(N)), (zero,) * N))
    for n in range(N):
        ga_ref[n] = ra[n] * a2_ref[n] * LN2

    for half in range(2):
        dt = w_ref[half, :, 48:, :].reshape(256, 512)
        gpb = []
        for s4 in range(4):
            s = 4 * half + s4
            cols = slice(128 * s, 128 * s + 128)
            xw = x_ref[:, cols].astype(f32)
            z = z_ref[:, cols].astype(f32)
            gw = g_ref[:, cols].astype(f32)
            dsk = dskip_ref[:, cols]
            sz = jax.nn.sigmoid(z)
            inner = y3[:, s, :] + dsk * xw
            mix_ref[:, cols] = (z * sz * inner).astype(jnp.bfloat16)
            gz_ref[:, cols] = (gw * inner * (sz * (1.0 + z * (1.0 - sz)))).astype(jnp.bfloat16)
            gsn = gw * (z * sz)
            gd = gd3[:, s, :]
            gpre = (gd * xw + gr3[:, s, :] * LN2) * sig_ref[:, cols]
            gcx_ref[:, cols] = gd * step_ref[:, s, :] + gsn * dsk
            par_ref[0:1, cols] = jnp.sum(gpre, axis=0, keepdims=True)
            par_ref[1:2, cols] = jnp.sum(gsn * xw, axis=0, keepdims=True)
            gpb.append(gpre.astype(jnp.bfloat16))
        gp = jnp.concatenate(gpb, axis=1)
        alow[...] += lax.dot_general(gp, dt, (((1,), (1,)), ((), ())), preferred_element_type=f32)
        gdt_ref[half] = lax.dot_general(low_ref[...], gp, (((0,), (0,)), ((), ())),
                                        preferred_element_type=f32).reshape(8, 32, 512).astype(jnp.bfloat16)

    @pl.when(i == pl.num_programs(0) - 1)
    def _():
        glow_ref[...] = alow[...]

        def fold(t, _):
            gbc_ref[t, 0:16, :] = jnp.sum(accb[t], axis=1)
            gbc_ref[t, 16:32, :] = jnp.sum(accc[t], axis=1)
            return 0
        lax.fori_loop(0, T, fold, 0)

def main_scan(step3, drive3, gs3, sig, x_conv, z, g, dskip, a2, bc, ent, wg, low):
    E = x_conv.shape[1]; C = E // 1024
    f32 = jnp.float32
    nat = pl.BlockSpec((T, 1024), lambda i: (0, i))
    tri = pl.BlockSpec((T, 8, 128), lambda i: (0, i, 0))
    full = lambda shape: pl.BlockSpec(shape, lambda i: (0,) * len(shape))
    S = jax.ShapeDtypeStruct
    return pl.pallas_call(
        main_scan_kernel, grid=(C,), name="main_scan",
        in_specs=[tri, tri, tri, nat, nat, nat, nat, pl.BlockSpec((1, 1024), lambda i: (0, i)),
                  pl.BlockSpec((N, 8, 128), lambda i: (0, i, 0)), full((32, T, 128)),
                  pl.BlockSpec((2, 128, 128), lambda i: (i, 0, 0)),
                  pl.BlockSpec((2, 8, 80, 512), lambda i: (i, 0, 0, 0)), full((T, 256))],
        out_specs=[nat, nat, nat, pl.BlockSpec((2, 8, 32, 512), lambda i: (i, 0, 0, 0)),
                   pl.BlockSpec((8, 1024), lambda i: (0, i)), pl.BlockSpec((N, 8, 128), lambda i: (0, i, 0)),
                   full((T, 256)), full((T, 32, 128))],
        out_shape=[S((T, E), jnp.bfloat16), S((T, E), jnp.bfloat16), S((T, E), f32), S((2 * C, 8, 32, 512), jnp.bfloat16),
                   S((8, E), f32), S((N, E // 128, 128), f32), S((T, 256), f32), S((T, 32, 128), f32)],
        scratch_shapes=[pltpu.VMEM((2, 128, 128), f32), pltpu.VMEM((T, N, 8, 128), f32), pltpu.VMEM((T, N, 8, 128), f32),
                        pltpu.VMEM((T, 8, 128), f32), pltpu.VMEM((T, 8, 128), f32), pltpu.VMEM((T, 8, 128), f32),
                        pltpu.VMEM((T, N, 8, 128), f32), pltpu.VMEM((T, N, 8, 128), f32), pltpu.VMEM((T, 256), f32)],
        compiler_params=pltpu.CompilerParams(vmem_limit_bytes=62 * 2**20),
    )(step3, drive3, gs3, sig, x_conv, z, g, dskip, a2, bc, ent, wg, low)


MESH = pl.DeviceIdType.MESH
ORDERS = (("x", "y", "z"), ("y", "z", "x"), ("z", "x", "y"))
ROWS = ((0, 32), (32, 32), (64, 16))
DIMS = {"z": 0, "x": 1, "y": 2}


def place():
    d, j = lax.axis_index("dp"), lax.axis_index("seq")
    return d, j, {"z": lax.div(j, 4), "x": lax.rem(j, 4), "y": lax.div(d, 2)}, lax.rem(d, 2)


def peer(pos, core, axis, hop):
    at = dict(pos)
    at[axis] = lax.rem(at[axis] + hop + 4, 4)
    return (at["y"] * 2 + core, at["z"] * 4 + at["x"])


def greet(devices):
    barrier = pltpu.get_barrier_semaphore()
    for device in devices:
        pl.semaphore_signal(barrier, inc=1, device_id=device, device_id_type=MESH)
    pl.semaphore_wait(barrier, len(devices))


def remote(src, dst, send_sem, recv_sem, device):
    return pltpu.make_async_remote_copy(
        src_ref=src, dst_ref=dst, send_sem=send_sem, recv_sem=recv_sem, device_id=device, device_id_type=MESH
    )


def slab(ref, fixed, tail):
    index = [slice(None)] * 3
    for axis, value in fixed.items():
        index[DIMS[axis]] = value
    return ref.at[tuple(index) + tail]


def gather_kernel(parts, with_tail, *refs):
    if with_tail:
        shard, tail_ref, out, halo, local_sem, ssem, rsem, csend, crecv, hsend, hrecv = refs
    else:
        shard, out, local_sem, ssem, rsem, csend, crecv = refs
    d, j, pos, core = place()
    sibling = (pos["y"] * 2 + 1 - core, j)
    following, previous = (d, lax.rem(j + 1, 16)), (d, lax.rem(j + 15, 16))
    near = [peer(pos, core, axis, hop) for axis in "xyz" for hop in (1, -1)]
    greet(near + [sibling] + ([previous] if with_tail else []))
    sent = []

    def go(copy):
        copy.start()
        sent.append(copy)

    if with_tail:
        tail_copy = remote(tail_ref, halo, hsend, hrecv, following)
        go(tail_copy)
    own = out.at[pos["z"], pos["x"], pos["y"], core]
    local = pltpu.make_async_copy(shard, own, local_sem)
    local.start()
    local.wait()

    def step(p, stage):
        order, (row, count) = parts[p]
        axis = order[stage]
        done = order[:stage]
        fixed = {a: pos[a] for a in "xyz" if a not in done}
        rows = pl.ds(row, count)
        half = out.shape[-1] // 2
        columns = (pl.ds(0, half), pl.ds(half, half))
        right, left = peer(pos, core, axis, 1), peer(pos, core, axis, -1)

        def at(hop, cols=slice(None)):
            return slab(out, {**fixed, axis: lax.rem(pos[axis] + hop + 4, 4)}, (core, rows, cols))

        def copy(which):
            hop, cols, device = ((0, slice(None), right), (0, slice(None), left),
                                 (-1, columns[0], right), (1, columns[1], left))[which]
            return remote(at(hop, cols), at(hop, cols), ssem.at[p, stage, which], rsem.at[p, stage, which], device)

        def landed(which):
            hop, cols, device = ((-1, slice(None), right), (1, slice(None), left),
                                 (2, columns[0], right), (2, columns[1], left))[which]
            remote(at(hop, cols), at(hop, cols), ssem.at[p, stage, which], rsem.at[p, stage, which], device).wait_recv()

        def across(which):
            hop = (0, -1, 1, 2)[which]
            return remote(at(hop), at(hop), csend.at[p, which], crecv.at[p, which], sibling)

        def crossed(which):
            hop = (0, -1, 1, 2)[which]
            there = slab(out, {**fixed, axis: lax.rem(pos[axis] + hop + 4, 4)}, (1 - core, rows, slice(None)))
            remote(there, there, csend.at[p, which], crecv.at[p, which], sibling).wait_recv()

        return copy, landed, across, crossed

    count = len(parts)
    for stage in range(3):
        steps = [step(p, stage) for p in range(count)]
        for copy, landed, across, crossed in steps:
            go(copy(0))
            go(copy(1))
            if stage == 2:
                go(across(0))
        for which in (0, 1):
            for copy, landed, across, crossed in steps:
                landed(which)
                go(copy(2 + which))
                if stage == 2:
                    go(across(1 + which))
        for copy, landed, across, crossed in steps:
            landed(2)
            landed(3)
            if stage == 2:
                go(across(3))
    for copy, landed, across, crossed in steps:
        for which in range(4):
            crossed(which)
    if with_tail:
        tail_copy.wait_recv()
    for copy in sent:
        copy.wait_send()


def gather(shard, tail, parts, collective_id):
    rows, columns = shard.shape
    count = len(parts)
    anyspace = pl.BlockSpec(memory_space=pl.ANY)
    dma = pltpu.SemaphoreType.DMA
    out_shape = [jax.ShapeDtypeStruct((4, 4, 4, 2, rows, columns), shard.dtype)]
    sems = [dma, dma((count, 3, 4)), dma((count, 3, 4)), dma((count, 4)), dma((count, 4))]
    operands = [shard]
    if tail is not None:
        out_shape.append(jax.ShapeDtypeStruct(tail.shape, tail.dtype))
        sems += [dma, dma]
        operands.append(tail)
    return pl.pallas_call(
        functools.partial(gather_kernel, parts, tail is not None),
        name="gather_shards",
        out_shape=out_shape,
        in_specs=[anyspace] * len(operands),
        out_specs=[anyspace] * len(out_shape),
        scratch_shapes=sems,
        compiler_params=pltpu.CompilerParams(collective_id=collective_id, has_side_effects=True),
    )(*operands)


def carry_kernel(ends, tot, a2, out, got, got_tot, back, ssem, rsem, tsend, trecv, bsend, brecv):
    d, j, pos, core = place()
    peers = [(d, lax.rem(j + k, 16)) for k in range(1, 16)]
    greet(peers)
    sent = []
    for k in range(1, 16):
        to = lax.rem(j + k, 16)
        one = remote(ends.at[to], got.at[j], ssem.at[k], rsem.at[k], peers[k - 1])
        two = remote(tot.at[to], got_tot.at[j], tsend.at[k], trecv.at[k], peers[k - 1])
        one.start()
        two.start()
        sent += [one, two]
    got[j] = ends[j]
    got_tot[j] = tot[j]
    for k in range(1, 16):
        source = lax.rem(j + 16 - k, 16)
        remote(got.at[source], got.at[source], ssem.at[k], rsem.at[k], peers[k - 1]).wait_recv()
        remote(got_tot.at[source], got_tot.at[source], tsend.at[k], trecv.at[k], peers[k - 1]).wait_recv()
    rates = a2[j]

    def decay(i):
        return jnp.exp2(rates * jnp.concatenate([got_tot[i, 0:4, :]] * 16, axis=0))

    enter = jnp.zeros((64, 128), jnp.float32)
    leave = jnp.zeros((64, 128), jnp.float32)
    for i in range(16):
        back[i, 0:64, :] = enter.astype(jnp.bfloat16)
        enter = decay(i) * enter + got[i, 0:64, :].astype(jnp.float32)
        r = 15 - i
        back[r, 64:128, :] = leave.astype(jnp.bfloat16)
        leave = decay(r) * leave + got[r, 64:128, :].astype(jnp.float32)
    for k in range(1, 16):
        to = lax.rem(j + k, 16)
        one = remote(back.at[to], out.at[j], bsend.at[k], brecv.at[k], peers[k - 1])
        one.start()
        sent.append(one)
    out[j] = back[j]
    for k in range(1, 16):
        source = lax.rem(j + 16 - k, 16)
        remote(out.at[source], out.at[source], bsend.at[k], brecv.at[k], peers[k - 1]).wait_recv()
    for copy in sent:
        copy.wait_send()


def carry(ends, tot, a2):
    vmem = pl.BlockSpec(memory_space=pltpu.VMEM)
    dma = pltpu.SemaphoreType.DMA((16,))
    return pl.pallas_call(
        carry_kernel,
        name="carry_exchange",
        out_shape=jax.ShapeDtypeStruct((16, 128, 128), jnp.bfloat16),
        in_specs=[vmem] * 3,
        out_specs=vmem,
        scratch_shapes=[
            pltpu.VMEM((16, 128, 128), jnp.bfloat16),
            pltpu.VMEM((16, 8, 128), jnp.float32),
            pltpu.VMEM((16, 128, 128), jnp.bfloat16),
            dma, dma, dma, dma, dma, dma,
        ],
        compiler_params=pltpu.CompilerParams(
            collective_id=1, has_side_effects=True, vmem_limit_bytes=32 * 2**20
        ),
    )(ends, tot, a2)


def reduce_kernel(part_ref, edge, out, all_params, halo, sums, cross, *scratch):
    buffers, scratch = scratch[:36], scratch[36:]
    packed, csend, crecv, ssem, rsem, psend, precv, pcs, pcr, hsend, hrecv = scratch
    d, j, pos, core = place()
    sibling = (pos["y"] * 2 + 1 - core, j)
    following, previous = (d, lax.rem(j + 1, 16)), (d, lax.rem(j + 15, 16))
    near = [peer(pos, core, axis, hop) for axis in "xyz" for hop in (1, -1)]
    greet(near + [sibling, following])
    sent = []

    def go(copy):
        copy.start()
        sent.append(copy)

    def across(p):
        row, count = ROWS[p]
        there = cross.at[:, :, :, pl.ds(row, count), :]
        return remote(part_ref.at[:, :, :, 1 - core, pl.ds(row, count), :], there, csend.at[p], crecv.at[p], sibling)

    for p in range(3):
        go(across(p))
    edge_copy = remote(edge, halo, hsend, hrecv, previous)
    go(edge_copy)
    for p in range(3):
        row, count = ROWS[p]
        rows = pl.ds(row, count)
        across(p).wait_recv()

        def add_core(i, _):
            a, b, c = lax.div(i, 16), lax.rem(lax.div(i, 4), 4), lax.rem(i, 4)
            sums[a, b, c, rows, :] = (
                part_ref[a, b, c, core, rows, :].astype(jnp.float32) + cross[a, b, c, rows, :].astype(jnp.float32)
            ).astype(jnp.bfloat16)
            return 0

        lax.fori_loop(0, 64, add_core, 0)

    def step(p, stage):
        order, (row, count) = ORDERS[p], ROWS[p]
        axis = order[2 - stage]
        fixed = {a: pos[a] for a in order[3 - stage:]}
        rows = pl.ds(row, count)
        half = 256
        columns = (slice(0, half), slice(half, 2 * half))
        right, left = peer(pos, core, axis, 1), peer(pos, core, axis, -1)
        bufs = buffers[(p * 3 + stage) * 4:(p * 3 + stage) * 4 + 4]
        free = [a for a in ("z", "x", "y") if a not in fixed and a != axis]

        def spot(hop):
            return lax.rem(pos[axis] + hop + 4, 4)

        def copy(which):
            hop, cols, device = ((2, columns[0], right), (2, columns[1], left),
                                 (1, slice(None), right), (-1, slice(None), left))[which]
            source = slab(sums, {**fixed, axis: spot(hop)}, (rows, cols))
            return remote(source, bufs[which], ssem.at[p, stage, which], rsem.at[p, stage, which], device)

        def add(hop, cols, terms):
            def at(values):
                index = [None] * 3
                for a, v in {**fixed, axis: spot(hop), **dict(zip(free, values))}.items():
                    index[DIMS[a]] = v
                return tuple(index) + (rows, cols)

            def one(i, _):
                values = (lax.div(i, 4), lax.rem(i, 4))[2 - len(free):] if free else ()
                total = sums[at(values)].astype(jnp.float32)
                for term in terms:
                    total = total + term[tuple(values)].astype(jnp.float32)
                sums[at(values)] = total.astype(jnp.bfloat16)
                return 0

            if free:
                lax.fori_loop(0, 4 ** len(free), one, 0)
            else:
                total = sums[at(())].astype(jnp.float32)
                for term in terms:
                    total = total + term[...].astype(jnp.float32)
                out[rows, :] = total

        def add_half(which):
            cols, hop = columns[which], (1, -1)[which]

            def at(values):
                index = [None] * 3
                for a, v in {**fixed, axis: spot(hop), **dict(zip(free, values))}.items():
                    index[DIMS[a]] = v
                return tuple(index) + (rows, cols)

            def one(i, _):
                values = (lax.div(i, 4), lax.rem(i, 4))[2 - len(free):] if free else ()
                mine = sums[at(values)].astype(jnp.float32)
                sums[at(values)] = (mine + bufs[which][tuple(values) if free else ...].astype(jnp.float32)).astype(jnp.bfloat16)
                return 0

            if free:
                lax.fori_loop(0, 4 ** len(free), one, 0)
            else:
                one(0, 0)

        return copy, (lambda which: copy(which).wait_recv()), add_half, (lambda: add(0, slice(None), bufs[2:]))

    for stage in range(3):
        steps = [step(p, stage) for p in range(3)]
        for copy, landed, add_half, finish in steps:
            go(copy(0))
            go(copy(1))
        for which in (0, 1):
            for copy, landed, add_half, finish in steps:
                landed(which)
                add_half(which)
                go(copy(2 + which))
        for copy, landed, add_half, finish in steps:
            landed(2)
            landed(3)
            finish()

    packed[...] = jnp.zeros((16, 128), jnp.bfloat16)
    rowsum = jnp.concatenate(
        [out[36 + q:37 + q, 128 * s:128 * s + 128] for q in range(3) for s in range(4)] + [jnp.zeros((4, 128), jnp.float32)], axis=0
    )
    packed[...] = rowsum.astype(jnp.bfloat16)
    all_params[pos["z"], pos["x"], pos["y"], core] = packed[...]
    order = ("y", "z", "x")
    for stage in range(3):
        axis = order[stage]
        fixed = {a: pos[a] for a in order[stage:]}

        def block(hop):
            return slab(all_params, {**fixed, axis: lax.rem(pos[axis] + hop + 4, 4)}, (core,))

        def send(which):
            hop, device = ((0, peer(pos, core, axis, 1)), (0, peer(pos, core, axis, -1)), (-1, peer(pos, core, axis, 1)))[which]
            return remote(block(hop), block(hop), psend.at[stage, which], precv.at[stage, which], device)

        def arrive(which):
            hop, device = ((-1, peer(pos, core, axis, 1)), (1, peer(pos, core, axis, -1)), (2, peer(pos, core, axis, 1)))[which]
            remote(block(hop), block(hop), psend.at[stage, which], precv.at[stage, which], device).wait_recv()

        go(send(0))
        go(send(1))
        arrive(0)
        go(send(2))
        arrive(1)
        arrive(2)
    mine, theirs = all_params.at[:, :, :, core], all_params.at[:, :, :, 1 - core]
    go(remote(mine, mine, pcs, pcr, sibling))
    remote(theirs, theirs, pcs, pcr, sibling).wait_recv()
    edge_copy.wait_recv()
    for copy in sent:
        copy.wait_send()


def reduce_all(part, edge):
    vmem = pl.BlockSpec(memory_space=pltpu.VMEM)
    anyspace = pl.BlockSpec(memory_space=pl.ANY)
    dma = pltpu.SemaphoreType.DMA
    bf16 = jnp.bfloat16
    buffers = []
    for row, count in ROWS:
        for stage in range(3):
            lead = (4,) * (2 - stage)
            buffers += [pltpu.VMEM(lead + (count, 256), bf16)] * 2 + [pltpu.VMEM(lead + (count, 512), bf16)] * 2
    return pl.pallas_call(
        reduce_kernel,
        name="reduce_shards",
        out_shape=[
            jax.ShapeDtypeStruct((80, 512), jnp.float32),
            jax.ShapeDtypeStruct((4, 4, 4, 2, 16, 128), bf16),
            jax.ShapeDtypeStruct(edge.shape, edge.dtype),
        ],
        in_specs=[vmem, anyspace],
        out_specs=[vmem, vmem, anyspace],
        scratch_shapes=[pltpu.VMEM((4, 4, 4, 80, 512), bf16)] * 2 + buffers + [
            pltpu.VMEM((16, 128), bf16),
            dma((3,)), dma((3,)), dma((3, 3, 4)), dma((3, 3, 4)), dma((3, 3)), dma((3, 3)), dma, dma, dma, dma,
        ],
        compiler_params=pltpu.CompilerParams(
            collective_id=2, has_side_effects=True, vmem_limit_bytes=48 * 2**20
        ),
    )(part, edge)


def tile_specs(width):
    nat = pl.BlockSpec((T, width), lambda i: (0, i))
    row = lambda count: pl.BlockSpec((count, width), lambda i: (0, i))
    full = lambda *shape: pl.BlockSpec(shape, lambda i: (0,) * len(shape))
    return nat, row, full


def spread(rows, columns, row_is_plain):
    plain = lax.broadcasted_iota(jnp.int32, (rows, columns), 0 if row_is_plain else 1)
    padded = lax.broadcasted_iota(jnp.int32, (rows, columns), 1 if row_is_plain else 0)
    device = lax.div(padded, 48)
    inside = padded - 48 * device
    return jnp.where((inside < 36) & (36 * device + inside == plain), 1.0, 0.0).astype(jnp.bfloat16)


def conv_kernel(x_ref, halo_ref, cw_ref, cb_ref, w_ref, xc_ref, slope_ref, low_ref, bc_ref, ext, acc):
    i = pl.program_id(0)

    @pl.when(i == 0)
    def _():
        acc[...] = jnp.zeros(acc.shape, jnp.float32)

    first = lax.axis_index("seq") == 0
    tail = halo_ref[...].astype(jnp.float32)
    ext[0:8, :] = jnp.where(first, 0.0, tail[8:16])
    ext[8:T + 8, :] = x_ref[...].astype(jnp.float32)
    for half in range(2):
        cols = slice(512 * half, 512 * half + 512)
        pre = cb_ref[:, cols] + cw_ref[0:1, cols] * ext[5:5 + T, cols]
        for k in range(1, 4):
            pre = pre + cw_ref[k:k + 1, cols] * ext[5 + k:5 + k + T, cols]
        logistic = jax.nn.sigmoid(pre)
        slope_ref[:, cols] = logistic * (1.0 + pre * (1.0 - logistic))
        xc = (pre * logistic).astype(jnp.bfloat16)
        xc_ref[:, cols] = xc
        acc[...] += lax.dot_general(
            xc, w_ref[half, :, 0:48, :].reshape(384, 512), (((1,), (1,)), ((), ())), preferred_element_type=jnp.float32
        )

    @pl.when(i == pl.num_programs(0) - 1)
    def _():
        low_ref[...] = jnp.dot(
            acc[...].astype(jnp.bfloat16), spread(384, 256, False), preferred_element_type=jnp.float32
        ).astype(jnp.bfloat16)
        for n in range(32):
            bc_ref[n] = jnp.broadcast_to(acc[:, 340 + n:341 + n], (T, 128))


def conv_project(x, halo, cw, cb, wg):
    E = x.shape[1]
    nat, row, full = tile_specs(1024)
    S = jax.ShapeDtypeStruct
    return pl.pallas_call(
        conv_kernel, grid=(E // 1024,), name="conv_project",
        in_specs=[nat, row(16), row(4), row(1), pl.BlockSpec((2, 8, 80, 512), lambda i: (i, 0, 0, 0))],
        out_specs=[nat, nat, full(T, 256), full(32, T, 128)],
        out_shape=[S((T, E), jnp.bfloat16), S((T, E), jnp.float32), S((T, 256), jnp.bfloat16), S((32, T, 128), jnp.float32)],
        scratch_shapes=[pltpu.VMEM((T + 8, 1024), jnp.float32), pltpu.VMEM((T, 384), jnp.float32)],
        compiler_params=pltpu.CompilerParams(vmem_limit_bytes=48 * 2**20),
    )(x, halo, cw, cb, wg)


def grads_kernel(glow_ref, gbc_ref, gcx_ref, slope_ref, xc_ref, x_ref, halo_ref, w_ref, gdt_ref, par_ref, ga_ref,
                 gconv_ref, part_ref, gproj, ext, wide):
    i = pl.program_id(0)
    f32 = jnp.float32

    @pl.when(i == 0)
    def _():
        plain = jnp.concatenate([glow_ref[...], gbc_ref[...]], axis=1).astype(jnp.bfloat16)
        gproj[...] = jnp.dot(plain, spread(288, 384, True), preferred_element_type=f32).astype(jnp.bfloat16)

    first = lax.axis_index("seq") == 0
    tail = halo_ref[...].astype(f32)
    ext[0:8, :] = jnp.where(first, 0.0, tail[8:16])
    ext[8:T + 8, :] = x_ref[...].astype(f32)
    for half in range(2):
        cols = slice(512 * half, 512 * half + 512)
        weights = w_ref[half, :, 0:48, :].reshape(384, 512)
        g_conv = (gcx_ref[:, cols] + jnp.dot(gproj[...], weights, preferred_element_type=f32)) * slope_ref[:, cols]
        gconv_ref[:, cols] = g_conv
        wide[...] = lax.dot_general(gproj[...], xc_ref[:, cols], (((0,), (0,)), ((), ())), preferred_element_type=f32)

        def put(r, value):
            wide[48 * (r // 3) + 36 + r % 3:48 * (r // 3) + 37 + r % 3, :] = value

        for k in range(4):
            put(k, jnp.sum(g_conv * ext[5 + k:5 + k + T, cols], axis=0, keepdims=True))
        put(4, jnp.sum(g_conv, axis=0, keepdims=True))
        put(5, par_ref[0:1, cols])
        put(6, par_ref[1:2, cols])
        for n in range(N):
            put(7 + n, jnp.concatenate([ga_ref[n, 4 * half + s:4 * half + s + 1, :] for s in range(4)], axis=1))
        part_ref[half, :, 0:48, :] = wide[...].reshape(8, 48, 512).astype(jnp.bfloat16)
        part_ref[half, :, 48:80, :] = gdt_ref[half]


def weight_grads(glow, gbc, gcx, slope, xc, x, halo, wg, gdt, par, ga):
    E = x.shape[1]
    nat, row, full = tile_specs(1024)
    S = jax.ShapeDtypeStruct
    block = pl.BlockSpec((2, 8, 80, 512), lambda i: (i, 0, 0, 0))
    return pl.pallas_call(
        grads_kernel, grid=(E // 1024,), name="weight_grads",
        in_specs=[full(T, 256), full(T, 32), nat, nat, nat, nat, row(16), block,
                  pl.BlockSpec((2, 8, 32, 512), lambda i: (i, 0, 0, 0)), row(8), pl.BlockSpec((N, 8, 128), lambda i: (0, i, 0))],
        out_specs=[nat, block],
        out_shape=[S((T, E), jnp.float32), S((E // 512, 8, 80, 512), jnp.bfloat16)],
        scratch_shapes=[pltpu.VMEM((T, 384), jnp.bfloat16), pltpu.VMEM((T + 8, 1024), jnp.float32), pltpu.VMEM((384, 512), jnp.float32)],
        compiler_params=pltpu.CompilerParams(vmem_limit_bytes=48 * 2**20),
    )(glow, gbc, gcx, slope, xc, x, halo, wg, gdt, par, ga)


def input_grad_kernel(g_ref, edge_ref, cw_ref, out_ref, ext):
    last = lax.axis_index("seq") == 15
    ext[0:T, :] = g_ref[...]
    ext[T:T + 8, :] = jnp.where(last, 0.0, edge_ref[...])
    total = cw_ref[0:1, :] * ext[3:3 + T, :]
    for k in range(1, 4):
        total = total + cw_ref[k:k + 1, :] * ext[3 - k:3 - k + T, :]
    out_ref[...] = total.astype(jnp.bfloat16)


def input_grad(g_conv, edge, cw):
    E = g_conv.shape[1]
    nat, row, full = tile_specs(1024)
    return pl.pallas_call(
        input_grad_kernel, grid=(E // 1024,), name="input_grad",
        in_specs=[nat, row(8), row(4)], out_specs=nat,
        out_shape=jax.ShapeDtypeStruct((T, E), jnp.bfloat16),
        scratch_shapes=[pltpu.VMEM((T + 8, 1024), jnp.float32)],
        compiler_params=pltpu.CompilerParams(vmem_limit_bytes=48 * 2**20),
    )(g_conv, edge, cw)


def local(x_branch, z_branch, out_grad, x_weight, dt_weight, conv_weight, conv_bias, dt_bias, a_log, d_skip):
    x, z, g = x_branch[0], z_branch[0], out_grad[0]
    E = x.shape[1]
    shard = jnp.concatenate([x_weight.T, jnp.zeros((12, 512), jnp.bfloat16), dt_weight], axis=0)
    gathered, halo = gather(shard, x[T - 16:], tuple(zip(ORDERS, ROWS)), 0)
    wg = gathered.reshape(16, 8, 80, 512)
    a2_wide = -jnp.exp(a_log) * LOG2E
    a2 = a2_wide.reshape(N, E // 128, 128)
    a2_blocks = a2_wide.reshape(N, 16, 4, 128).transpose(1, 0, 2, 3).reshape(16, 64, 128)
    xc, slope, low, bc = conv_project(x, halo, conv_weight, conv_bias[None], wg)
    step3, drive3, gs3, sig, ends, tot = local_scan(low, wg, xc, z, g, dt_bias[None], a2, bc)
    carried = carry(ends, tot, a2_blocks)
    mixer_out, grad_z, gcx, gdt, par, ga, glow, gbc = main_scan(
        step3, drive3, gs3, sig, xc, z, g, d_skip[None], a2, bc, carried, wg, low
    )
    g_conv, part = weight_grads(glow, jnp.sum(gbc, axis=2), gcx, slope, xc, x, halo, wg, gdt, par, ga)
    reduced, params, edge = reduce_all(part.reshape(4, 4, 4, 2, 80, 512), g_conv[:8])
    grad_x = input_grad(g_conv, edge, conv_weight)
    params = params.reshape(16, 8, 16, 128)[:, :, :12].reshape(16, 8, 3, 4, 128)
    params = params.transpose(1, 2, 0, 3, 4).reshape(24, E).astype(jnp.float32)
    return (
        mixer_out[None], grad_x[None], grad_z[None], reduced[:36].T, reduced[48:80],
        params[0:4], params[4], params[5], params[7:23], params[6],
    )


def solution(mesh):
    tokens, weights, whole = P("dp", "seq", None), P("seq", "dp"), P()
    in_specs = (tokens,) * 3 + (weights, P("dp", "seq")) + (whole,) * 5
    out_specs = (tokens,) * 3 + (weights, P("dp", "seq")) + (whole,) * 5
    return jax.shard_map(local, mesh=mesh, in_specs=in_specs, out_specs=out_specs, check_vma=False)
```

```python
import functools

import jax
import jax.numpy as jnp
from jax import lax
from jax.experimental import pallas as pl
from jax.experimental.pallas import tpu as pltpu
from jax.sharding import PartitionSpec as P

T = 128
N = 16
LN2 = 0.6931471805599453
LOG2E = 1.4426950408889634
VMEM_LIMIT = 62 * 2**20
LOCAL_GROUP, LOCAL_UNROLL = 4, 16
CHUNKS = 1
FWD_GROUP, FWD_UNROLL = 8, 8
BWD_GROUP, BWD_UNROLL = 8, 8


def logistic(values):
    return 0.5 * jnp.tanh(0.5 * values) + 0.5


def tile_specs(width):
    nat = pl.BlockSpec((T, width), lambda i: (0, i))
    row = lambda count: pl.BlockSpec((count, width), lambda i: (0, i))
    full = lambda *shape: pl.BlockSpec(shape, lambda i: (0,) * len(shape))
    return nat, row, full


def local_scan_kernel(low_ref, wa_ref, wb_ref, x_ref, z_ref, g_ref, bias_ref, a2_ref, bc_ref,
                      step_ref, drive_ref, gs_ref, sig_ref, ends_ref, tot_ref, scr):
    low = low_ref[...]
    rows = [ref.reshape(T * 8, 128) for ref in (step_ref, drive_ref, gs_ref)]
    for half in range(2):
        dt = jnp.concatenate([wa_ref[half].reshape(128, 512), wb_ref[half].reshape(128, 512)], axis=0)
        cols = pl.ds(512 * half, 512)
        rate = jnp.dot(low, dt, preferred_element_type=jnp.float32) + bias_ref[:, cols]
        step = jnp.maximum(rate, 0.0) + jnp.log1p(jnp.exp(-jnp.abs(rate)))
        sig_ref[:, cols] = jnp.exp(rate - step)
        z = z_ref[:, cols].astype(jnp.float32)
        gs = g_ref[:, cols].astype(jnp.float32) * (z * logistic(z))
        drive = step * x_ref[:, cols].astype(jnp.float32)
        for s in range(4):
            for ref, value in zip(rows, (step, drive, gs)):
                ref[pl.ds(4 * half + s, T, stride=8), :] = value[:, 128 * s:128 * s + 128]

    zero = jnp.zeros((8, 128), jnp.float32)
    one = jnp.ones((8, 128), jnp.float32)
    ends, lams = [], []
    for first in range(0, N, LOCAL_GROUP):
        group = range(first, first + LOCAL_GROUP)

        def body(k, carry):
            tot, ends, prods, lams = carry
            for unrolled in range(LOCAL_UNROLL):
                t = k * LOCAL_UNROLL + unrolled
                st, dr, gv = step_ref[t], drive_ref[t], gs_ref[t]
                new_ends, new_prods, new_lams = [], [], []
                for q, n in enumerate(group):
                    f = jnp.exp2(st * a2_ref[n])
                    new_ends.append(f * ends[q] + bc_ref[n, pl.ds(t, 1), :] * dr)
                    p = prods[q] * f
                    new_prods.append(p)
                    new_lams.append(lams[q] + p * (bc_ref[N + n, pl.ds(t, 1), :] * gv))
                tot, ends, prods, lams = tot + st, tuple(new_ends), tuple(new_prods), tuple(new_lams)
            return tot, ends, prods, lams

        many = LOCAL_GROUP
        tot, e, _, l = lax.fori_loop(0, T // LOCAL_UNROLL, body, (zero, (zero,) * many, (one,) * many, (zero,) * many))
        ends += e
        lams += l
    for n in range(N):
        for half in range(2):
            scr[half, 4 * n:4 * n + 4, :] = ends[n][4 * half:4 * half + 4]
            scr[half, 64 + 4 * n:64 + 4 * n + 4, :] = lams[n][4 * half:4 * half + 4]
    ends_ref[...] = scr[...].astype(jnp.bfloat16)
    for half in range(2):
        tot_ref[half, 0:4, :] = tot[4 * half:4 * half + 4]
        tot_ref[half, 4:8, :] = jnp.zeros((4, 128), jnp.float32)


def local_scan(low, wg, x_conv, z, g, bias, a2, bc):
    E = x_conv.shape[1]
    C = E // 1024
    f32 = jnp.float32
    nat, row, full = tile_specs(1024)
    tri = pl.BlockSpec((T, 8, 128), lambda i: (0, i, 0))
    return pl.pallas_call(
        local_scan_kernel, grid=(C,), name="local_scan",
        in_specs=[full(T, 256), pl.BlockSpec((2, 8, 16, 512), lambda i: (i, 0, 3, 0)),
                  pl.BlockSpec((2, 8, 16, 512), lambda i: (i, 0, 4, 0)), nat, nat, nat,
                  row(1), pl.BlockSpec((N, 8, 128), lambda i: (0, i, 0)), full(32, T, 128)],
        out_specs=[tri, tri, tri, nat, pl.BlockSpec((2, 128, 128), lambda i: (i, 0, 0)),
                   pl.BlockSpec((2, 8, 128), lambda i: (i, 0, 0))],
        out_shape=[jax.ShapeDtypeStruct((T, E // 128, 128), f32)] * 3 + [
            jax.ShapeDtypeStruct((T, E), f32), jax.ShapeDtypeStruct((2 * C, 128, 128), jnp.bfloat16),
            jax.ShapeDtypeStruct((2 * C, 8, 128), f32)],
        scratch_shapes=[pltpu.VMEM((2, 128, 128), f32)],
        compiler_params=pltpu.CompilerParams(vmem_limit_bytes=VMEM_LIMIT),
    )(low, wg, wg, x_conv, z, g, bias, a2, bc)


def main_scan_kernel(step_ref, drive_ref, gs_ref, sig_ref, x_ref, z_ref, g_ref, dskip_ref, a2_ref, bc_ref, ent_ref, wa_ref, wb_ref, low_ref,
              mix_ref, gz_ref, gcx_ref, gdt_ref, par_ref, ga_ref, glow_ref, gbc_ref,
              es, us, y3, gd3, gr3, accb, accc, alow, turned):
    i = pl.program_id(0)
    f32 = jnp.float32
    span = [slice(8 * q, 8 * q + 8) for q in range(CHUNKS)]

    @pl.when(i == 0)
    def _():
        accb[...] = jnp.zeros(accb.shape, f32)
        accc[...] = jnp.zeros(accc.shape, f32)
        alow[...] = jnp.zeros(alow.shape, f32)
        turned[...] = low_ref[...].T

    es[...] = ent_ref[...].astype(f32)

    def state(base, n, q):
        rows = slice(base + 4 * n, base + 4 * n + 4)
        return jnp.concatenate([es[2 * q, rows, :], es[2 * q + 1, rows, :]], axis=0)

    def add(total, term):
        return term if total is None else total + term

    def inputs(t):
        return tuple([ref[t, rows] for rows in span] for ref in (step_ref, drive_ref, gs_ref))

    zero = jnp.zeros((8, 128), f32)
    for first in range(0, N, FWD_GROUP):
        group = range(first, first + FWD_GROUP)

        def forward(k, hs):
            for unrolled in range(FWD_UNROLL):
                t = k * FWD_UNROLL + unrolled
                st, dr, gv = inputs(t)
                ys = [None if first == 0 else y3[t, rows] for rows in span]
                new = []
                for p, n in enumerate(group):
                    b, c = bc_ref[n, pl.ds(t, 1), :], bc_ref[N + n, pl.ds(t, 1), :]
                    total = accc[t, n]
                    for q in range(CHUNKS):
                        u = jnp.exp2(st[q] * a2_ref[n, span[q]]) * hs[p * CHUNKS + q]
                        us[t, n, span[q]] = u
                        h = u + b * dr[q]
                        new.append(h)
                        ys[q] = add(ys[q], c * h)
                        total = total + h * gv[q]
                    accc[t, n] = total
                for q in range(CHUNKS):
                    y3[t, span[q]] = ys[q]
                hs = tuple(new)
            return hs

        lax.fori_loop(0, T // FWD_UNROLL, forward, tuple(state(0, n, q) for n in group for q in range(CHUNKS)))

    for first in range(0, N, BWD_GROUP):
        group = range(first, first + BWD_GROUP)

        def backward(k, carry):
            adj, ra = carry
            for unrolled in range(BWD_UNROLL):
                t = T - 1 - (k * BWD_UNROLL + unrolled)
                st, dr, gv = inputs(t)
                gd = [None if first == 0 else gd3[t, rows] for rows in span]
                gr = [None if first == 0 else gr3[t, rows] for rows in span]
                na, nr = [], []
                for p, n in enumerate(group):
                    b, c = bc_ref[n, pl.ds(t, 1), :], bc_ref[N + n, pl.ds(t, 1), :]
                    total = accb[t, n]
                    for q in range(CHUNKS):
                        rate = a2_ref[n, span[q]]
                        lam = c * gv[q] + adj[p * CHUNKS + q]
                        gd[q] = add(gd[q], lam * b)
                        total = total + lam * dr[q]
                        na.append(jnp.exp2(st[q] * rate) * lam)
                        m = lam * us[t, n, span[q]]
                        gr[q] = add(gr[q], m * rate)
                        nr.append(ra[p * CHUNKS + q] + m * st[q])
                    accb[t, n] = total
                for q in range(CHUNKS):
                    gd3[t, span[q]] = gd[q]
                    gr3[t, span[q]] = gr[q]
                adj, ra = tuple(na), tuple(nr)
            return adj, ra

        _, ra = lax.fori_loop(0, T // BWD_UNROLL, backward, (tuple(state(64, n, q) for n in group for q in range(CHUNKS)), (zero,) * (BWD_GROUP * CHUNKS)))
        for p, n in enumerate(group):
            for q in range(CHUNKS):
                ga_ref[n, span[q]] = ra[p * CHUNKS + q] * a2_ref[n, span[q]] * LN2

    for half in range(2 * CHUNKS):
        dt = jnp.concatenate([wa_ref[half].reshape(128, 512), wb_ref[half].reshape(128, 512)], axis=0)
        gpb = []
        for s in range(4 * half, 4 * half + 4):
            cols = slice(128 * s, 128 * s + 128)
            xw = x_ref[:, cols].astype(f32)
            z = z_ref[:, cols].astype(f32)
            gw = g_ref[:, cols].astype(f32)
            dsk = dskip_ref[:, cols]
            sz = logistic(z)
            act = z * sz
            inner = y3.reshape(T * 8 * CHUNKS, 128)[pl.ds(s, T, stride=8 * CHUNKS), :] + dsk * xw
            mix_ref[:, cols] = (act * inner).astype(jnp.bfloat16)
            gz_ref[:, cols] = (gw * inner * (sz + act * (1.0 - sz))).astype(jnp.bfloat16)
            gsn = gw * act
            gd = gd3.reshape(T * 8 * CHUNKS, 128)[pl.ds(s, T, stride=8 * CHUNKS), :]
            gpre = (gd * xw + gr3.reshape(T * 8 * CHUNKS, 128)[pl.ds(s, T, stride=8 * CHUNKS), :] * LN2) * sig_ref[:, cols]
            gcx_ref[:, cols] = gd * step_ref.reshape(T * 8 * CHUNKS, 128)[pl.ds(s, T, stride=8 * CHUNKS), :] + gsn * dsk
            par_ref[0:1, cols] = jnp.sum(gpre, axis=0, keepdims=True)
            par_ref[1:2, cols] = jnp.sum(gsn * xw, axis=0, keepdims=True)
            gpb.append(gpre.astype(jnp.bfloat16))
        gp = jnp.concatenate(gpb, axis=1)
        alow[...] += lax.dot_general(gp, dt, (((1,), (1,)), ((), ())), preferred_element_type=f32)
        gdt = jnp.dot(turned[...], gp, preferred_element_type=f32).astype(jnp.bfloat16)
        for h in range(2):
            gdt_ref[half, :, 16 * h:16 * h + 16, :] = gdt[128 * h:128 * h + 128].reshape(8, 16, 512)

    @pl.when(i == pl.num_programs(0) - 1)
    def _():
        glow_ref[...] = alow[...]

        def fold(t, _):
            gbc_ref[t, 0:16, :] = jnp.sum(accb[t], axis=1)
            gbc_ref[t, 16:32, :] = jnp.sum(accc[t], axis=1)
            return 0
        lax.fori_loop(0, T, fold, 0)

def main_scan(step3, drive3, gs3, sig, x_conv, z, g, dskip, a2, bc, ent, wg, low):
    E = x_conv.shape[1]
    C = E // (1024 * CHUNKS)
    f32 = jnp.float32
    nat = pl.BlockSpec((T, 1024 * CHUNKS), lambda i: (0, i))
    tri = pl.BlockSpec((T, 8 * CHUNKS, 128), lambda i: (0, i, 0))
    row = lambda count: pl.BlockSpec((count, 1024 * CHUNKS), lambda i: (0, i))
    once = lambda *shape: pl.BlockSpec(shape, lambda i: (0,) * len(shape), pipeline_mode=pl.Buffered(1))
    full = lambda *shape: pl.BlockSpec(shape, lambda i: (0,) * len(shape))
    rate = pl.BlockSpec((N, 8 * CHUNKS, 128), lambda i: (0, i, 0))
    S = jax.ShapeDtypeStruct
    return pl.pallas_call(
        main_scan_kernel, grid=(C,), name="main_scan",
        in_specs=[tri, tri, tri, nat, nat, nat, nat, row(1), rate, once(32, T, 128),
                  pl.BlockSpec((2 * CHUNKS, 128, 128), lambda i: (i, 0, 0)),
                  pl.BlockSpec((2 * CHUNKS, 8, 16, 512), lambda i: (i, 0, 3, 0)),
                  pl.BlockSpec((2 * CHUNKS, 8, 16, 512), lambda i: (i, 0, 4, 0)), once(T, 256)],
        out_specs=[nat, nat, nat, pl.BlockSpec((2 * CHUNKS, 8, 32, 512), lambda i: (i, 0, 0, 0)),
                   row(8), rate, full(T, 256), full(T, 32, 128)],
        out_shape=[S((T, E), jnp.bfloat16), S((T, E), jnp.bfloat16), S((T, E), f32), S((E // 512, 8, 32, 512), jnp.bfloat16),
                   S((8, E), f32), S((N, E // 128, 128), f32), S((T, 256), f32), S((T, 32, 128), f32)],
        scratch_shapes=[pltpu.VMEM((2 * CHUNKS, 128, 128), f32), pltpu.VMEM((T, N, 8 * CHUNKS, 128), f32)]
        + [pltpu.VMEM((T, 8 * CHUNKS, 128), f32)] * 3 + [pltpu.VMEM((T, N, 8, 128), f32)] * 2 + [pltpu.VMEM((T, 256), f32), pltpu.VMEM((256, T), jnp.bfloat16)],
        compiler_params=pltpu.CompilerParams(vmem_limit_bytes=VMEM_LIMIT),
    )(step3, drive3, gs3, sig, x_conv, z, g, dskip, a2, bc, ent, wg, wg, low)


MESH = pl.DeviceIdType.MESH
ORDERS = (("x", "y", "z"), ("y", "z", "x"), ("z", "x", "y"))
GATHER_ROWS = ((0, 32), (32, 32), (64, 16))
ROWS = ((0, 32), (32, 16), (48, 32))
DIMS = {"z": 0, "x": 1, "y": 2}


def place():
    d, j = lax.axis_index("dp"), lax.axis_index("seq")
    return d, j, {"z": lax.div(j, 4), "x": lax.rem(j, 4), "y": lax.div(d, 2)}, lax.rem(d, 2)


def peer(pos, core, axis, hop):
    at = dict(pos)
    at[axis] = lax.rem(at[axis] + hop + 4, 4)
    return (at["y"] * 2 + core, at["z"] * 4 + at["x"])


OTHERS = [(a, b) for a in range(4) for b in range(4) if (a, b) != (0, 0)]


def peer2(pos, core, axes, hops):
    at = {a: lax.rem(pos[a] + h, 4) for a, h in zip(axes, hops)}
    at = {**pos, **at}
    return (at["y"] * 2 + core, at["z"] * 4 + at["x"])


def planes(pos, core):
    near = [peer(pos, core, axis, hop) for axis in "xyz" for hop in (1, 2, 3)]
    return near + [peer2(pos, core, axes, (a, b)) for axes in ("xy", "yz", "zx") for a, b in OTHERS if a and b]


def greet(devices):
    barrier = pltpu.get_barrier_semaphore()
    for device in devices:
        pl.semaphore_signal(barrier, inc=1, device_id=device, device_id_type=MESH)
    pl.semaphore_wait(barrier, len(devices))


def remote(src, dst, send_sem, recv_sem, device):
    return pltpu.make_async_remote_copy(
        src_ref=src, dst_ref=dst, send_sem=send_sem, recv_sem=recv_sem, device_id=device, device_id_type=MESH
    )


def slab(ref, fixed, tail):
    index = [slice(None)] * 3
    for axis, value in fixed.items():
        index[DIMS[axis]] = value
    return ref.at[tuple(index) + tail]


def gather_kernel(parts, with_tail, *refs):
    if with_tail:
        shard, tail_ref, out, halo, local_sem, ssem, rsem, fsend, frecv, csend, crecv, hsend, hrecv = refs
    else:
        shard, out, local_sem, ssem, rsem, fsend, frecv, csend, crecv = refs
    d, j, pos, core = place()
    sibling = (pos["y"] * 2 + 1 - core, j)
    following, previous = (d, lax.rem(j + 1, 16)), (d, lax.rem(j + 15, 16))
    greet(planes(pos, core) + [sibling] + ([previous] if with_tail else []))
    sent = []

    def go(copy):
        copy.start()
        sent.append(copy)

    own = out.at[pos["z"], pos["x"], pos["y"], core]
    local = pltpu.make_async_copy(shard, own, local_sem)
    local.start()
    half = out.shape[-1] // 2
    columns = (pl.ds(0, half), pl.ds(half, half))
    whole = slice(None)
    hops = (0, -1, 1, 2)

    def step(p, slot, axis, fixed):
        row, count = parts[p][1]
        rows = pl.ds(row, count)
        right, left = peer(pos, core, axis, 1), peer(pos, core, axis, -1)

        def at(hop, cols=whole, which=core):
            return slab(out, {**fixed, axis: lax.rem(pos[axis] + hop + 4, 4)}, (which, rows, cols))

        def ring(hop, cols, which, device):
            return remote(at(hop, cols), at(hop, cols), ssem.at[p, slot, which], rsem.at[p, slot, which], device)

        def send(which):
            hop, cols, device = ((0, whole, right), (0, whole, left), (-1, columns[0], right), (1, columns[1], left))[which]
            go(ring(hop, cols, which, device))

        def landed(which):
            hop, cols, device = ((-1, whole, right), (1, whole, left), (2, columns[0], right), (2, columns[1], left))[which]
            ring(hop, cols, which, device).wait_recv()

        def across(which):
            there = at(hops[which])
            go(remote(there, there, csend.at[p, slot, which], crecv.at[p, slot, which], sibling))

        def crossed(which):
            there = at(hops[which], whole, 1 - core)
            remote(there, there, csend.at[p, slot, which], crecv.at[p, slot, which], sibling).wait_recv()

        return send, landed, across, crossed

    count = range(len(parts))

    def spot(axis, hop):
        return lax.rem(pos[axis] + hop + 4, 4)

    def direct(p, k):
        (one, two, three), (row, rows) = parts[p]
        device = peer2(pos, core, (one, two), OTHERS[k])
        return remote(shard.at[pl.ds(row, rows), :], own.at[pl.ds(row, rows), :], fsend.at[p, k], frecv.at[p, k], device)

    def arrived(p, k):
        (one, two, three), (row, rows) = parts[p]
        a, b = OTHERS[k]
        there = slab(out, {one: spot(one, -a), two: spot(two, -b), three: pos[three]}, (core, pl.ds(row, rows), whole))
        remote(there, there, fsend.at[p, k], frecv.at[p, k], peer2(pos, core, (one, two), OTHERS[k])).wait_recv()

    third = []
    for p in count:
        one, two, three = parts[p][0]
        third.append([step(p, i, three, {two: spot(two, hops[i])}) for i in range(4)])
    turn = [[k for k, (a, b) in enumerate(OTHERS) if (-b) % 4 == hops[i] % 4] for i in range(4)]
    for i in range(4):
        for k in turn[i]:
            for p in count:
                go(direct(p, k))
    if with_tail:
        tail_copy = remote(tail_ref.at[pl.ds(T - 16, 16), :], halo, hsend, hrecv, following)
        go(tail_copy)
    local.wait()
    for i in range(4):
        for p in count:
            for k in turn[i]:
                arrived(p, k)
            send, _, across, _ = third[p][i]
            send(0)
            send(1)
            across(0)
    for i in range(4):
        for which in (0, 1):
            for p in count:
                send, landed, across, _ = third[p][i]
                landed(which)
                send(2 + which)
                across(1 + which)
    for i in range(4):
        for p in count:
            _, landed, across, _ = third[p][i]
            landed(2)
            landed(3)
            across(3)
    for i in range(4):
        for p in count:
            for which in range(4):
                third[p][i][3](which)
    if with_tail:
        tail_copy.wait_recv()
    for copy in sent:
        copy.wait_send()


def gather(shard, tail, parts, collective_id):
    rows, columns = shard.shape
    count = len(parts)
    anyspace = pl.BlockSpec(memory_space=pl.ANY)
    dma = pltpu.SemaphoreType.DMA
    out_shape = [jax.ShapeDtypeStruct((4, 4, 4, 2, rows, columns), shard.dtype)]
    sems = [dma, dma((count, 4, 4)), dma((count, 4, 4)), dma((count, 15)), dma((count, 15)), dma((count, 4, 4)), dma((count, 4, 4))]
    operands = [shard]
    if tail is not None:
        out_shape.append(jax.ShapeDtypeStruct((16, tail.shape[1]), tail.dtype))
        sems += [dma, dma]
        operands.append(tail)
    return pl.pallas_call(
        functools.partial(gather_kernel, parts, tail is not None),
        name="gather_shards",
        out_shape=out_shape,
        in_specs=[anyspace] * len(operands),
        out_specs=[anyspace] * len(out_shape),
        scratch_shapes=sems,
        compiler_params=pltpu.CompilerParams(collective_id=collective_id, has_side_effects=True, vmem_limit_bytes=VMEM_LIMIT),
    )(*operands)


def carry_kernel(ends, tot, a2, out, got, got_tot, back, ssem, rsem, tsend, trecv, bsend, brecv):
    d, j, pos, core = place()
    peers = [(d, lax.rem(j + k, 16)) for k in range(1, 16)]
    greet(peers)
    sent = []
    for k in range(1, 16):
        to = lax.rem(j + k, 16)
        one = remote(ends.at[to], got.at[j], ssem.at[k], rsem.at[k], peers[k - 1])
        two = remote(tot.at[to], got_tot.at[j], tsend.at[k], trecv.at[k], peers[k - 1])
        one.start()
        two.start()
        sent += [one, two]
    got[j] = ends[j]
    got_tot[j] = tot[j]
    for k in range(1, 16):
        source = lax.rem(j + 16 - k, 16)
        remote(got.at[source], got.at[source], ssem.at[k], rsem.at[k], peers[k - 1]).wait_recv()
        remote(got_tot.at[source], got_tot.at[source], tsend.at[k], trecv.at[k], peers[k - 1]).wait_recv()
    rates = a2[j]

    def decay(i):
        return jnp.exp2(rates * jnp.concatenate([got_tot[i, 0:4, :]] * 16, axis=0))

    enter = jnp.zeros((64, 128), jnp.float32)
    leave = jnp.zeros((64, 128), jnp.float32)
    for i in range(16):
        back[i, 0:64, :] = enter.astype(jnp.bfloat16)
        enter = decay(i) * enter + got[i, 0:64, :].astype(jnp.float32)
        r = 15 - i
        back[r, 64:128, :] = leave.astype(jnp.bfloat16)
        leave = decay(r) * leave + got[r, 64:128, :].astype(jnp.float32)
    for k in range(1, 16):
        to = lax.rem(j + k, 16)
        one = remote(back.at[to], out.at[j], bsend.at[k], brecv.at[k], peers[k - 1])
        one.start()
        sent.append(one)
    out[j] = back[j]
    for k in range(1, 16):
        source = lax.rem(j + 16 - k, 16)
        remote(out.at[source], out.at[source], bsend.at[k], brecv.at[k], peers[k - 1]).wait_recv()
    for copy in sent:
        copy.wait_send()


def carry(ends, tot, a2):
    vmem = pl.BlockSpec(memory_space=pltpu.VMEM)
    dma = pltpu.SemaphoreType.DMA((16,))
    return pl.pallas_call(
        carry_kernel,
        name="carry_exchange",
        out_shape=jax.ShapeDtypeStruct((16, 128, 128), jnp.bfloat16),
        in_specs=[vmem] * 3,
        out_specs=vmem,
        scratch_shapes=[
            pltpu.VMEM((16, 128, 128), jnp.bfloat16),
            pltpu.VMEM((16, 8, 128), jnp.float32),
            pltpu.VMEM((16, 128, 128), jnp.bfloat16),
            dma, dma, dma, dma, dma, dma,
        ],
        compiler_params=pltpu.CompilerParams(
            collective_id=1, has_side_effects=True, vmem_limit_bytes=VMEM_LIMIT
        ),
    )(ends, tot, a2)


def reduce_kernel(xpart, dpart, edge, out, all_params, halo, sums, cross, *scratch):
    buffers, plane, scratch = scratch[:48], scratch[48:51], scratch[51:]
    packed, own_sem, csend, crecv, ssem, rsem, fsend, frecv, psend, precv, qsend, qrecv, hsend, hrecv = scratch
    d, j, pos, core = place()
    sibling = (pos["y"] * 2 + 1 - core, j)
    following, previous = (d, lax.rem(j + 1, 16)), (d, lax.rem(j + 15, 16))
    column = [(lax.rem(pos["y"] + k // 2, 4) * 2 + lax.rem(core + k, 2), j) for k in range(1, 8)]
    greet(planes(pos, core) + column + [following])
    sent = []
    hops = (2, 1, -1, 0)
    half = 256
    whole = slice(None)
    columns = (slice(0, half), slice(half, 2 * half))

    def go(copy):
        copy.start()
        sent.append(copy)

    def spot(axis, hop):
        return lax.rem(pos[axis] + hop + 4, 4)

    def mine(p, i, which):
        row, count = ROWS[p]
        fixed = {ORDERS[p][1]: spot(ORDERS[p][1], hops[i])}
        return slab(xpart if p < 2 else dpart, fixed, (which, pl.ds(row if p < 2 else 0, count), whole))

    def beside(ref, p, i):
        row, count = ROWS[p]
        return slab(ref, {ORDERS[p][1]: spot(ORDERS[p][1], hops[i])}, (pl.ds(row, count), whole))

    def across(p, i):
        return remote(mine(p, i, 1 - core), beside(cross, p, i), csend.at[p, i], crecv.at[p, i], sibling)

    def own(p, i):
        return pltpu.make_async_copy(mine(p, i, core), beside(sums, p, i), own_sem.at[p, i])

    for i in range(4):
        for p in range(3):
            go(across(p, i))
            own(p, i).start()
    edge_copy = remote(edge, halo, hsend, hrecv, previous)
    go(edge_copy)

    def index_of(fixed, free, values):
        index = [None] * 3
        for a, v in {**fixed, **dict(zip(free, values))}.items():
            index[DIMS[a]] = v
        return tuple(index)

    def add_core(p, i):
        row, count = ROWS[p]
        rows = pl.ds(row, count)
        middle = ORDERS[p][1]
        free = [a for a in "zxy" if a != middle]
        own(p, i).wait()
        across(p, i).wait_recv()

        def one(k, _):
            at = index_of({middle: spot(middle, hops[i])}, free, (lax.div(k, 4), lax.rem(k, 4))) + (rows, whole)
            sums[at] = (sums[at].astype(jnp.float32) + cross[at].astype(jnp.float32)).astype(jnp.bfloat16)
            return 0

        lax.fori_loop(0, 16, one, 0)

    def step(p, slot, axis, fixed, free):
        row, count = ROWS[p]
        rows = pl.ds(row, count)
        right, left = peer(pos, core, axis, 1), peer(pos, core, axis, -1)
        bufs = buffers[(p * 4 + slot) * 4:(p * 4 + slot) * 4 + 4]

        def copy(which):
            hop, cols, device = ((2, columns[0], right), (2, columns[1], left), (1, whole, right), (-1, whole, left))[which]
            source = slab(sums, {**fixed, axis: spot(axis, hop)}, (rows, cols))
            return remote(source, bufs[which], ssem.at[p, slot, which], rsem.at[p, slot, which], device)

        def add(hop, cols, terms):
            def one(k, _):
                at = index_of({**fixed, axis: spot(axis, hop)}, free, (k,)) + (rows, cols)
                total = sums[at].astype(jnp.float32)
                for term in terms:
                    total = total + term[k].astype(jnp.float32)
                sums[at] = total.astype(jnp.bfloat16)
                return 0

            lax.fori_loop(0, 4, one, 0)

        def begin():
            go(copy(0))
            go(copy(1))

        def relay(which):
            copy(which).wait_recv()
            add((1, -1)[which], columns[which], bufs[which:which + 1])
            go(copy(2 + which))

        def finish():
            copy(2).wait_recv()
            copy(3).wait_recv()
            add(0, whole, bufs[2:])

        return begin, relay, finish

    def direct(p, k):
        one, two, three = ORDERS[p]
        a, b = OTHERS[k]
        row, count = ROWS[p]
        source = slab(sums, {one: spot(one, a), two: spot(two, b), three: pos[three]}, (pl.ds(row, count), whole))
        return remote(source, plane[p].at[k], fsend.at[p, k], frecv.at[p, k], peer2(pos, core, (one, two), (a, b)))

    parts = range(3)
    turn = [[k for k, (a, b) in enumerate(OTHERS) if b % 4 == hops[i] % 4] for i in range(4)]
    outer = []
    for p in parts:
        one, two, three = ORDERS[p]
        outer.append([step(p, i, three, {two: spot(two, hops[i])}, [one]) for i in range(4)])
    for i in range(4):
        for p in parts:
            add_core(p, i)
            outer[p][i][0]()
    for i in range(4):
        for which in (0, 1):
            for p in parts:
                outer[p][i][1](which)
    for i in range(4):
        for p in parts:
            outer[p][i][2]()
            for k in turn[i]:
                go(direct(p, k))
    for p in parts:
        row, count = ROWS[p]
        rows = pl.ds(row, count)
        for k in range(15):
            direct(p, k).wait_recv()
        out[rows, :] = sums[pos["z"], pos["x"], pos["y"], rows, :].astype(jnp.float32)

        def one_more(k, _):
            out[rows, :] += plane[p][k].astype(jnp.float32)
            return 0

        lax.fori_loop(0, 15, one_more, 0)

    packed[...] = jnp.zeros((16, 128), jnp.bfloat16)
    rowsum = jnp.concatenate(
        [out[36 + q:37 + q, 128 * s:128 * s + 128] for q in range(3) for s in range(4)] + [jnp.zeros((4, 128), jnp.float32)], axis=0
    )
    packed[...] = rowsum.astype(jnp.bfloat16)
    all_params[pos["z"], pos["x"], pos["y"], core] = packed[...]

    def place_of(hops):
        return all_params.at[lax.rem(pos["z"] + 4 - hops[0], 4), lax.rem(pos["x"] + 4 - hops[1], 4), pos["y"], core]

    def flat(k):
        return remote(place_of((0, 0)), place_of((0, 0)), psend.at[k], precv.at[k], peer2(pos, core, "zx", OTHERS[k]))

    def upright(k):
        ours = all_params.at[:, :, pos["y"], core]
        return remote(ours, ours, qsend.at[k], qrecv.at[k], column[k - 1])

    for k in range(15):
        go(flat(k))
    for k in range(15):
        there = place_of(OTHERS[k])
        remote(there, there, psend.at[k], precv.at[k], peer2(pos, core, "zx", OTHERS[k])).wait_recv()
    for k in range(1, 8):
        go(upright(k))
    for k in range(1, 8):
        y, c = lax.rem(pos["y"] + 4 - k // 2, 4), lax.rem(core + k, 2)
        there = all_params.at[:, :, y, c]
        remote(there, there, qsend.at[k], qrecv.at[k], column[k - 1]).wait_recv()
    edge_copy.wait_recv()
    for copy in sent:
        copy.wait_send()


def reduce_all(xpart, dpart, edge):
    vmem = pl.BlockSpec(memory_space=pltpu.VMEM)
    anyspace = pl.BlockSpec(memory_space=pl.ANY)
    dma = pltpu.SemaphoreType.DMA
    bf16 = jnp.bfloat16
    buffers = []
    for row, count in ROWS:
        buffers += ([pltpu.VMEM((4, count, 256), bf16)] * 2 + [pltpu.VMEM((4, count, 512), bf16)] * 2) * 4
    buffers += [pltpu.VMEM((15, count, 512), bf16) for row, count in ROWS]
    return pl.pallas_call(
        reduce_kernel,
        name="reduce_shards",
        out_shape=[
            jax.ShapeDtypeStruct((80, 512), jnp.float32),
            jax.ShapeDtypeStruct((4, 4, 4, 2, 16, 128), bf16),
            jax.ShapeDtypeStruct(edge.shape, edge.dtype),
        ],
        in_specs=[anyspace] * 3,
        out_specs=[vmem, vmem, anyspace],
        scratch_shapes=[pltpu.VMEM((4, 4, 4, 80, 512), bf16)] * 2 + buffers + [
            pltpu.VMEM((16, 128), bf16),
            dma((3, 4)), dma((3, 4)), dma((3, 4)), dma((3, 4, 4)), dma((3, 4, 4)), dma((3, 15)), dma((3, 15)),
            dma((15,)), dma((15,)), dma((8,)), dma((8,)), dma, dma,
        ],
        compiler_params=pltpu.CompilerParams(
            collective_id=2, has_side_effects=True, vmem_limit_bytes=VMEM_LIMIT
        ),
    )(xpart, dpart, edge)


def spread(rows, columns, row_is_plain):
    index = lax.broadcasted_iota(jnp.int32, (rows, columns), 0 if row_is_plain else 1)
    padded = lax.broadcasted_iota(jnp.int32, (rows, columns), 1 if row_is_plain else 0)
    low = 32 * lax.div(lax.rem(index, 128), 16) + 16 * lax.div(index, 128) + lax.rem(index, 16)
    plain = jnp.where(index < 256, low, index)
    device = lax.div(padded, 48)
    inside = padded - 48 * device
    return jnp.where((inside < 36) & (36 * device + inside == plain), 1.0, 0.0).astype(jnp.bfloat16)


def convolve(x_ref, halo_ref, cw_ref, cb_ref, ext):
    tail = halo_ref[...].astype(jnp.float32)
    ext[0:8, :] = jnp.where(lax.axis_index("seq") == 0, 0.0, tail[8:16])
    ext[8:T + 8, :] = x_ref[...].astype(jnp.float32)

    def part(cols):
        pre = cb_ref[:, cols] + cw_ref[0:1, cols] * ext[5:5 + T, cols]
        for k in range(1, 4):
            pre = pre + cw_ref[k:k + 1, cols] * ext[5 + k:5 + k + T, cols]
        gate = logistic(pre)
        act = pre * gate
        return act.astype(jnp.bfloat16), gate + act * (1.0 - gate)

    return part


def conv_kernel(x_ref, halo_ref, cw_ref, cb_ref, w_ref, xc_ref, low_ref, bc_ref, ext, acc):
    i = pl.program_id(0)

    @pl.when(i == 0)
    def _():
        acc[...] = jnp.zeros(acc.shape, jnp.float32)

    part = convolve(x_ref, halo_ref, cw_ref, cb_ref, ext)
    for half in range(2):
        cols = slice(512 * half, 512 * half + 512)
        xc, _ = part(cols)
        xc_ref[:, cols] = xc
        acc[...] += lax.dot_general(
            xc, w_ref[half].reshape(384, 512), (((1,), (1,)), ((), ())), preferred_element_type=jnp.float32
        )

    @pl.when(i == pl.num_programs(0) - 1)
    def _():
        low_ref[...] = jnp.dot(
            acc[...].astype(jnp.bfloat16), spread(384, 256, False), preferred_element_type=jnp.float32
        ).astype(jnp.bfloat16)
        for n in range(32):
            bc_ref[n] = jnp.broadcast_to(acc[:, 340 + n:341 + n], (T, 128))


def conv_project(x, halo, cw, cb, wg):
    E = x.shape[1]
    nat, row, full = tile_specs(1024)
    S = jax.ShapeDtypeStruct
    return pl.pallas_call(
        conv_kernel, grid=(E // 1024,), name="conv_project",
        in_specs=[nat, row(16), row(4), row(1), pl.BlockSpec((2, 8, 48, 512), lambda i: (i, 0, 0, 0))],
        out_specs=[nat, full(T, 256), full(32, T, 128)],
        out_shape=[S((T, E), jnp.bfloat16), S((T, 256), jnp.bfloat16), S((32, T, 128), jnp.float32)],
        scratch_shapes=[pltpu.VMEM((T + 8, 1024), jnp.float32), pltpu.VMEM((T, 384), jnp.float32)],
        compiler_params=pltpu.CompilerParams(vmem_limit_bytes=VMEM_LIMIT),
    )(x, halo, cw, cb, wg)


def grads_kernel(glow_ref, gbc_ref, gcx_ref, x_ref, halo_ref, cw_ref, cb_ref, w_ref, par_ref, ga_ref,
                 gx_ref, head_ref, tail_ref, part_ref, gproj, turned, ext, wide, gext):
    i = pl.program_id(0)
    f32 = jnp.float32

    @pl.when(i == 0)
    def _():
        plain = jnp.concatenate([glow_ref[...], gbc_ref[...]], axis=1).astype(jnp.bfloat16)
        gproj[...] = jnp.dot(plain, spread(288, 384, True), preferred_element_type=f32).astype(jnp.bfloat16)
        turned[...] = gproj[...].T
        gext[T:T + 8, :] = jnp.zeros((8, gext.shape[1]), f32)

    part = convolve(x_ref, halo_ref, cw_ref, cb_ref, ext)
    for half in range(2):
        cols = slice(512 * half, 512 * half + 512)
        xc, slope = part(cols)
        weights = w_ref[half].reshape(384, 512)
        g_conv = (gcx_ref[:, cols] + jnp.dot(gproj[...], weights, preferred_element_type=f32)) * slope
        gext[0:T, cols] = g_conv
        wide[...] = jnp.dot(turned[...], xc, preferred_element_type=f32)

        def put(r, value):
            wide[48 * (r // 3) + 36 + r % 3:48 * (r // 3) + 37 + r % 3, :] = value

        for k in range(4):
            put(k, jnp.sum(g_conv * ext[5 + k:5 + k + T, cols], axis=0, keepdims=True))
        put(4, jnp.sum(g_conv, axis=0, keepdims=True))
        put(5, par_ref[0:1, cols])
        put(6, par_ref[1:2, cols])
        for n in range(N):
            put(7 + n, jnp.concatenate([ga_ref[n, 4 * half + s:4 * half + s + 1, :] for s in range(4)], axis=1))
        part_ref[half] = wide[...].reshape(8, 48, 512).astype(jnp.bfloat16)
    total = cw_ref[0:1, :] * gext[3:3 + T, :]
    for k in range(1, 4):
        total = total + cw_ref[k:k + 1, :] * gext[3 - k:3 - k + T, :]
    gx_ref[...] = total.astype(jnp.bfloat16)
    head_ref[...] = gext[0:8, :]
    tail_ref[...] = gext[T - 16:T, :]


def weight_grads(glow, gbc, gcx, x, halo, cw, cb, wg, par, ga):
    E = x.shape[1]
    nat, row, full = tile_specs(1024)
    S = jax.ShapeDtypeStruct
    f32 = jnp.float32
    block = pl.BlockSpec((2, 8, 48, 512), lambda i: (i, 0, 0, 0))
    return pl.pallas_call(
        grads_kernel, grid=(E // 1024,), name="weight_grads",
        in_specs=[full(T, 256), full(T, 32), nat, nat, row(16), row(4), row(1), block, row(8),
                  pl.BlockSpec((N, 8, 128), lambda i: (0, i, 0))],
        out_specs=[nat, row(8), row(16), block],
        out_shape=[S((T, E), jnp.bfloat16), S((8, E), f32), S((16, E), f32), S((E // 512, 8, 48, 512), jnp.bfloat16)],
        scratch_shapes=[pltpu.VMEM((T, 384), jnp.bfloat16), pltpu.VMEM((384, T), jnp.bfloat16), pltpu.VMEM((T + 8, 1024), f32),
                        pltpu.VMEM((384, 512), f32),
                        pltpu.VMEM((T + 8, 1024), f32)],
        compiler_params=pltpu.CompilerParams(vmem_limit_bytes=VMEM_LIMIT),
    )(glow, gbc, gcx, x, halo, cw, cb, wg, par, ga)


def last_rows_kernel(gx_ref, tail_ref, edge_ref, cw_ref, out_ref, ext):
    ext[0:16, :] = tail_ref[...]
    ext[16:24, :] = jnp.where(lax.axis_index("seq") == 15, 0.0, edge_ref[...])
    total = cw_ref[0:1, :] * ext[3:19, :]
    for k in range(1, 4):
        total = total + cw_ref[k:k + 1, :] * ext[3 - k:19 - k, :]
    out_ref[...] = total.astype(jnp.bfloat16)


def last_rows(gx, tail, edge, cw):
    E = gx.shape[1]
    row = lambda count: pl.BlockSpec((count, 2048), lambda i: (0, i))
    block = pl.BlockSpec((16, 2048), lambda i: (T // 16 - 1, i))
    return pl.pallas_call(
        last_rows_kernel, grid=(E // 2048,), name="last_rows",
        in_specs=[block, row(16), row(8), row(4)], out_specs=block,
        out_shape=jax.ShapeDtypeStruct((T, E), jnp.bfloat16),
        scratch_shapes=[pltpu.VMEM((24, 2048), jnp.float32)],
        input_output_aliases={0: 0},
        compiler_params=pltpu.CompilerParams(vmem_limit_bytes=VMEM_LIMIT),
    )(gx, tail, edge, cw)


def local(x_branch, z_branch, out_grad, x_weight, dt_weight, conv_weight, conv_bias, dt_bias, a_log, d_skip):
    x, z, g = x_branch[0], z_branch[0], out_grad[0]
    E = x.shape[1]
    shard = jnp.concatenate([x_weight.T, jnp.zeros((12, 512), jnp.bfloat16), dt_weight], axis=0)
    gathered, halo = gather(shard, x, tuple(zip(ORDERS, GATHER_ROWS)), 0)
    wg = gathered.reshape(16, 8, 80, 512)
    a2_wide = -jnp.exp(a_log) * LOG2E
    a2 = a2_wide.reshape(N, E // 128, 128)
    a2_blocks = a2_wide.reshape(N, 16, 4, 128).transpose(1, 0, 2, 3).reshape(16, 64, 128)
    bias = conv_bias[None]
    xc, low, bc = conv_project(x, halo, conv_weight, bias, wg)
    step3, drive3, gs3, sig, ends, tot = local_scan(low, wg, xc, z, g, dt_bias[None], a2, bc)
    carried = carry(ends, tot, a2_blocks)
    mixer_out, grad_z, gcx, gdt, par, ga, glow, gbc = main_scan(
        step3, drive3, gs3, sig, xc, z, g, d_skip[None], a2, bc, carried, wg, low
    )
    gx, head, tail, part = weight_grads(glow, jnp.sum(gbc, axis=2), gcx, x, halo, conv_weight, bias, wg, par, ga)
    reduced, params, edge = reduce_all(part.reshape(4, 4, 4, 2, 48, 512), gdt.reshape(4, 4, 4, 2, 32, 512), head)
    grad_x = last_rows(gx, tail, edge, conv_weight)
    params = params.reshape(16, 8, 16, 128)[:, :, :12].reshape(16, 8, 3, 4, 128)
    params = params.transpose(1, 2, 0, 3, 4).reshape(24, E).astype(jnp.float32)
    return (
        mixer_out[None], grad_x[None], grad_z[None], reduced[:36].T, reduced[48:80],
        params[0:4], params[4], params[5], params[7:23], params[6],
    )


def solution(mesh):
    tokens, weights, whole = P("dp", "seq", None), P("seq", "dp"), P()
    in_specs = (tokens,) * 3 + (weights, P("dp", "seq")) + (whole,) * 5
    out_specs = (tokens,) * 3 + (weights, P("dp", "seq")) + (whole,) * 5
    return jax.shard_map(local, mesh=mesh, in_specs=in_specs, out_specs=out_specs, check_vma=False)
```

```python
import functools

import jax
import jax.numpy as jnp
from jax import lax
from jax.experimental import pallas as pl
from jax.experimental.pallas import tpu as pltpu
from jax.sharding import PartitionSpec as P

T = 128
N = 16
LN2 = 0.6931471805599453
LOG2E = 1.4426950408889634
VMEM_LIMIT = 62 * 2**20
LOCAL_GROUP, LOCAL_UNROLL = 4, 16
SHIPMENTS = ((0, 4), (4, 3), (7, 1))
CHUNKS = 1
FWD_GROUP, FWD_UNROLL = 8, 8
BWD_GROUP, BWD_UNROLL = 8, 8


def logistic(values):
    return 0.5 * jnp.tanh(0.5 * values) + 0.5


def tile_specs(width):
    nat = pl.BlockSpec((T, width), lambda i: (0, i))
    row = lambda count: pl.BlockSpec((count, width), lambda i: (0, i))
    full = lambda *shape: pl.BlockSpec(shape, lambda i: (0,) * len(shape))
    return nat, row, full


def local_scan_kernel(low_ref, wa_ref, wb_ref, x_ref, z_ref, g_ref, bias_ref, a2_ref, bc_ref, rates_ref,
                      step_ref, drive_ref, gs_ref, sig_ref, carried, ends_all, got, back,
                      ssem, rsem, bsend, brecv, own_sem):
    i = pl.program_id(0)
    d, j, _, _ = place()
    others = [lax.rem(j + k, 16) for k in range(1, 16)]

    @pl.when(i == 0)
    def _():
        barrier = pltpu.get_barrier_semaphore()
        for k in others:
            pl.semaphore_signal(barrier, inc=1, device_id=(d, k), device_id_type=MESH)

    low = low_ref[...]
    rows = [ref.reshape(T * 8, 128) for ref in (step_ref, drive_ref, gs_ref)]
    for half in range(2):
        dt = jnp.concatenate([wa_ref[half].reshape(128, 512), wb_ref[half].reshape(128, 512)], axis=0)
        cols = pl.ds(512 * half, 512)
        rate = jnp.dot(low, dt, preferred_element_type=jnp.float32) + bias_ref[:, cols]
        step = jnp.maximum(rate, 0.0) + jnp.log1p(jnp.exp(-jnp.abs(rate)))
        sig_ref[:, cols] = jnp.exp(rate - step)
        z = z_ref[:, cols].astype(jnp.float32)
        gs = g_ref[:, cols].astype(jnp.float32) * (z * logistic(z))
        drive = step * x_ref[:, cols].astype(jnp.float32)
        for s in range(4):
            for ref, value in zip(rows, (step, drive, gs)):
                ref[pl.ds(4 * half + s, T, stride=8), :] = value[:, 128 * s:128 * s + 128]

    zero = jnp.zeros((8, 128), jnp.float32)
    one = jnp.ones((8, 128), jnp.float32)
    ends, lams = [], []
    for first in range(0, N, LOCAL_GROUP):
        group = range(first, first + LOCAL_GROUP)

        def body(k, carry):
            tot, ends, prods, lams = carry
            for unrolled in range(LOCAL_UNROLL):
                t = k * LOCAL_UNROLL + unrolled
                st, dr, gv = step_ref[t], drive_ref[t], gs_ref[t]
                new_ends, new_prods, new_lams = [], [], []
                for q, n in enumerate(group):
                    f = jnp.exp2(st * a2_ref[n])
                    new_ends.append(f * ends[q] + bc_ref[n, pl.ds(t, 1), :] * dr)
                    p = prods[q] * f
                    new_prods.append(p)
                    new_lams.append(lams[q] + p * (bc_ref[N + n, pl.ds(t, 1), :] * gv))
                tot, ends, prods, lams = tot + st, tuple(new_ends), tuple(new_prods), tuple(new_lams)
            return tot, ends, prods, lams

        many = LOCAL_GROUP
        tot, e, _, l = lax.fori_loop(0, T // LOCAL_UNROLL, body, (zero, (zero,) * many, (one,) * many, (zero,) * many))
        ends += e
        lams += l
    high = tot.astype(jnp.bfloat16)
    sums = jnp.concatenate([high.astype(jnp.float32), tot - high.astype(jnp.float32)], axis=0).astype(jnp.bfloat16)
    for n in range(N):
        ends_all[n, i, 0:16, :] = jnp.concatenate([ends[n], lams[n]], axis=0).astype(jnp.bfloat16)
        ends_all[n, i, 16:32, :] = sums

    def chunks(group):
        return pl.ds(SHIPMENTS[group][0], SHIPMENTS[group][1])

    def outgoing(group, to):
        return remote(ends_all.at[to, chunks(group)], got.at[j, chunks(group)], ssem.at[group, to], rsem.at[group, j], (d, to))

    def returned(group, to):
        return remote(back.at[to, chunks(group)], carried.at[j, chunks(group)], bsend.at[group, to], brecv.at[group, j], (d, to))

    def ship(group):
        for to in others:
            outgoing(group, to).start()
        first, count = SHIPMENTS[group]
        for k in range(first, first + count):
            got[j, k] = ends_all[j, k]

    def recur(group):
        for source in others:
            there = got.at[source, chunks(group)]
            remote(there, there, ssem.at[group, source], rsem.at[group, source], (d, source)).wait_recv()
        first, count = SHIPMENTS[group]
        for c in range(first, first + count):
            rates = rates_ref[j, 8 * c:8 * c + 8, :]
            blocks = [got[k, c].astype(jnp.float32) for k in range(16)]
            decays = [jnp.exp2(rates * (block[16:24] + block[24:32])) for block in blocks]
            enter, leave = [jnp.zeros((8, 128), jnp.float32)], [jnp.zeros((8, 128), jnp.float32)]
            for k in range(15):
                enter.append(decays[k] * enter[k] + blocks[k][0:8])
                leave.append(decays[15 - k] * leave[k] + blocks[15 - k][8:16])
            for k in range(16):
                back[k, c] = jnp.concatenate([enter[k], leave[15 - k]], axis=0).astype(jnp.bfloat16)
        for to in others:
            returned(group, to).start()
        pltpu.make_async_copy(back.at[j, chunks(group)], carried.at[j, chunks(group)], own_sem.at[group]).start()

    @pl.when(i == 3)
    def _():
        pl.semaphore_wait(pltpu.get_barrier_semaphore(), 15)
        ship(0)

    @pl.when(i == 5)
    def _():
        recur(0)

    @pl.when(i == 6)
    def _():
        ship(1)

    @pl.when(i == 7)
    def _():
        ship(2)
        recur(1)
        recur(2)
        for group in range(3):
            pltpu.make_async_copy(back.at[j, chunks(group)], carried.at[j, chunks(group)], own_sem.at[group]).wait()
            for k in others:
                there = carried.at[k, chunks(group)]
                remote(there, there, bsend.at[group, k], brecv.at[group, k], (d, k)).wait_recv()
                outgoing(group, k).wait_send()
                returned(group, k).wait_send()


def local_scan(low, wg, x_conv, z, g, bias, a2, bc):
    E = x_conv.shape[1]
    C = E // 1024
    f32 = jnp.float32
    nat, row, full = tile_specs(1024)
    tri = pl.BlockSpec((T, 8, 128), lambda i: (0, i, 0))
    return pl.pallas_call(
        local_scan_kernel, grid=(C,), name="local_scan",
        in_specs=[full(T, 256), pl.BlockSpec((2, 8, 16, 512), lambda i: (i, 0, 3, 0)),
                  pl.BlockSpec((2, 8, 16, 512), lambda i: (i, 0, 4, 0)), nat, nat, nat,
                  row(1), pl.BlockSpec((N, 8, 128), lambda i: (0, i, 0)), full(32, T, 128), full(N, E // 128, 128)],
        out_specs=[tri, tri, tri, nat, pl.BlockSpec(memory_space=pl.ANY)],
        out_shape=[jax.ShapeDtypeStruct((T, E // 128, 128), f32)] * 3 + [
            jax.ShapeDtypeStruct((T, E), f32), jax.ShapeDtypeStruct((16, C, 16, 128), jnp.bfloat16)],
        scratch_shapes=[pltpu.VMEM((16, C, 32, 128), jnp.bfloat16)] * 2 + [pltpu.VMEM((16, C, 16, 128), jnp.bfloat16)]
        + [pltpu.SemaphoreType.DMA((3, 16))] * 4 + [pltpu.SemaphoreType.DMA((3,))],
        compiler_params=pltpu.CompilerParams(collective_id=1, has_side_effects=True, vmem_limit_bytes=VMEM_LIMIT),
    )(low, wg, wg, x_conv, z, g, bias, a2, bc, a2)


def main_scan_kernel(step_ref, drive_ref, gs_ref, sig_ref, x_ref, z_ref, g_ref, dskip_ref, a2_ref, bc_ref, ent_ref, wa_ref, wb_ref, low_ref,
              mix_ref, gz_ref, gcx_ref, gdt_ref, par_ref, ga_ref, glow_ref, gbc_ref,
              es, us, y3, gd3, gr3, accb, accc, alow, turned, both):
    i = pl.program_id(0)
    f32 = jnp.float32
    span = [slice(8 * q, 8 * q + 8) for q in range(CHUNKS)]

    @pl.when(i == 0)
    def _():
        accb[...] = jnp.zeros(accb.shape, f32)
        accc[...] = jnp.zeros(accc.shape, f32)
        alow[...] = jnp.zeros(alow.shape, f32)
        turned[...] = low_ref[...].T

    es[...] = ent_ref[...].astype(f32)

    def state(base, n, q):
        return es[n, q, base:base + 8, :]

    def add(total, term):
        return term if total is None else total + term

    def inputs(t):
        return tuple([ref[t, rows] for rows in span] for ref in (step_ref, drive_ref, gs_ref))

    zero = jnp.zeros((8, 128), f32)
    for first in range(0, N, FWD_GROUP):
        group = range(first, first + FWD_GROUP)

        def forward(k, hs):
            for unrolled in range(FWD_UNROLL):
                t = k * FWD_UNROLL + unrolled
                st, dr, gv = inputs(t)
                ys = [None if first == 0 else y3[t, rows] for rows in span]
                new = []
                for p, n in enumerate(group):
                    b, c = bc_ref[n, pl.ds(t, 1), :], bc_ref[N + n, pl.ds(t, 1), :]
                    total = accc[t, n]
                    for q in range(CHUNKS):
                        u = jnp.exp2(st[q] * a2_ref[n, span[q]]) * hs[p * CHUNKS + q]
                        us[t, n, span[q]] = u
                        h = u + b * dr[q]
                        new.append(h)
                        ys[q] = add(ys[q], c * h)
                        total = total + h * gv[q]
                    accc[t, n] = total
                for q in range(CHUNKS):
                    y3[t, span[q]] = ys[q]
                hs = tuple(new)
            return hs

        lax.fori_loop(0, T // FWD_UNROLL, forward, tuple(state(0, n, q) for n in group for q in range(CHUNKS)))

    for first in range(0, N, BWD_GROUP):
        group = range(first, first + BWD_GROUP)

        def backward(k, carry):
            adj, ra = carry
            for unrolled in range(BWD_UNROLL):
                t = T - 1 - (k * BWD_UNROLL + unrolled)
                st, dr, gv = inputs(t)
                gd = [None if first == 0 else gd3[t, rows] for rows in span]
                gr = [None if first == 0 else gr3[t, rows] for rows in span]
                na, nr = [], []
                for p, n in enumerate(group):
                    b, c = bc_ref[n, pl.ds(t, 1), :], bc_ref[N + n, pl.ds(t, 1), :]
                    total = accb[t, n]
                    for q in range(CHUNKS):
                        rate = a2_ref[n, span[q]]
                        lam = c * gv[q] + adj[p * CHUNKS + q]
                        gd[q] = add(gd[q], lam * b)
                        total = total + lam * dr[q]
                        na.append(jnp.exp2(st[q] * rate) * lam)
                        m = lam * us[t, n, span[q]]
                        gr[q] = add(gr[q], m * rate)
                        nr.append(ra[p * CHUNKS + q] + m * st[q])
                    accb[t, n] = total
                for q in range(CHUNKS):
                    gd3[t, span[q]] = gd[q]
                    gr3[t, span[q]] = gr[q]
                adj, ra = tuple(na), tuple(nr)
            return adj, ra

        _, ra = lax.fori_loop(0, T // BWD_UNROLL, backward, (tuple(state(8, n, q) for n in group for q in range(CHUNKS)), (zero,) * (BWD_GROUP * CHUNKS)))
        for p, n in enumerate(group):
            for q in range(CHUNKS):
                ga_ref[n, span[q]] = ra[p * CHUNKS + q] * a2_ref[n, span[q]] * LN2

    for half in range(2 * CHUNKS):
        dt = jnp.concatenate([wa_ref[half].reshape(128, 512), wb_ref[half].reshape(128, 512)], axis=0)
        gpb = []
        for s in range(4 * half, 4 * half + 4):
            cols = slice(128 * s, 128 * s + 128)
            xw = x_ref[:, cols].astype(f32)
            z = z_ref[:, cols].astype(f32)
            gw = g_ref[:, cols].astype(f32)
            dsk = dskip_ref[:, cols]
            sz = logistic(z)
            act = z * sz
            inner = y3.reshape(T * 8 * CHUNKS, 128)[pl.ds(s, T, stride=8 * CHUNKS), :] + dsk * xw
            mix_ref[:, cols] = (act * inner).astype(jnp.bfloat16)
            gz_ref[:, cols] = (gw * inner * (sz + act * (1.0 - sz))).astype(jnp.bfloat16)
            gsn = gw * act
            gd = gd3.reshape(T * 8 * CHUNKS, 128)[pl.ds(s, T, stride=8 * CHUNKS), :]
            gpre = (gd * xw + gr3.reshape(T * 8 * CHUNKS, 128)[pl.ds(s, T, stride=8 * CHUNKS), :] * LN2) * sig_ref[:, cols]
            gcx_ref[:, cols] = gd * step_ref.reshape(T * 8 * CHUNKS, 128)[pl.ds(s, T, stride=8 * CHUNKS), :] + gsn * dsk
            par_ref[0:1, cols] = jnp.sum(gpre, axis=0, keepdims=True)
            par_ref[1:2, cols] = jnp.sum(gsn * xw, axis=0, keepdims=True)
            gpb.append(gpre.astype(jnp.bfloat16))
        gp = jnp.concatenate(gpb, axis=1)
        alow[...] += lax.dot_general(gp, dt, (((1,), (1,)), ((), ())), preferred_element_type=f32)
        gdt = jnp.dot(turned[...], gp, preferred_element_type=f32).astype(jnp.bfloat16)
        for h in range(2):
            gdt_ref[half, :, 16 * h:16 * h + 16, :] = gdt[128 * h:128 * h + 128].reshape(8, 16, 512)

    @pl.when(i == pl.num_programs(0) - 1)
    def _():
        glow_ref[...] = alow[...]

        def fold(t, _):
            both[t, 0:16, :] = jnp.sum(accb[t], axis=1)
            both[t, 16:32, :] = jnp.sum(accc[t], axis=1)
            return 0
        lax.fori_loop(0, T, fold, 0)
        for n in range(2 * N):
            gbc_ref[:, n:n + 1] = jnp.sum(both.reshape(T * 32, 128)[pl.ds(n, T, stride=32), :], axis=1, keepdims=True)

def main_scan(step3, drive3, gs3, sig, x_conv, z, g, dskip, a2, bc, ent, wg, low):
    E = x_conv.shape[1]
    C = E // (1024 * CHUNKS)
    f32 = jnp.float32
    nat = pl.BlockSpec((T, 1024 * CHUNKS), lambda i: (0, i))
    tri = pl.BlockSpec((T, 8 * CHUNKS, 128), lambda i: (0, i, 0))
    row = lambda count: pl.BlockSpec((count, 1024 * CHUNKS), lambda i: (0, i))
    once = lambda *shape: pl.BlockSpec(shape, lambda i: (0,) * len(shape), pipeline_mode=pl.Buffered(1))
    full = lambda *shape: pl.BlockSpec(shape, lambda i: (0,) * len(shape))
    rate = pl.BlockSpec((N, 8 * CHUNKS, 128), lambda i: (0, i, 0))
    S = jax.ShapeDtypeStruct
    return pl.pallas_call(
        main_scan_kernel, grid=(C,), name="main_scan",
        in_specs=[tri, tri, tri, nat, nat, nat, nat, row(1), rate, once(32, T, 128),
                  pl.BlockSpec((N, CHUNKS, 16, 128), lambda i: (0, i, 0, 0)),
                  pl.BlockSpec((2 * CHUNKS, 8, 16, 512), lambda i: (i, 0, 3, 0)),
                  pl.BlockSpec((2 * CHUNKS, 8, 16, 512), lambda i: (i, 0, 4, 0)), once(T, 256)],
        out_specs=[nat, nat, nat, pl.BlockSpec((2 * CHUNKS, 8, 32, 512), lambda i: (i, 0, 0, 0)),
                   row(8), rate, full(T, 256), full(T, 32)],
        out_shape=[S((T, E), jnp.bfloat16), S((T, E), jnp.bfloat16), S((T, E), f32), S((E // 512, 8, 32, 512), jnp.bfloat16),
                   S((8, E), f32), S((N, E // 128, 128), f32), S((T, 256), f32), S((T, 32), f32)],
        scratch_shapes=[pltpu.VMEM((N, CHUNKS, 16, 128), f32), pltpu.VMEM((T, N, 8 * CHUNKS, 128), f32)]
        + [pltpu.VMEM((T, 8 * CHUNKS, 128), f32)] * 3 + [pltpu.VMEM((T, N, 8, 128), f32)] * 2 + [pltpu.VMEM((T, 256), f32), pltpu.VMEM((256, T), jnp.bfloat16),
           pltpu.VMEM((T, 32, 128), f32)],
        compiler_params=pltpu.CompilerParams(vmem_limit_bytes=VMEM_LIMIT),
    )(step3, drive3, gs3, sig, x_conv, z, g, dskip, a2, bc, ent, wg, wg, low)


MESH = pl.DeviceIdType.MESH
ORDERS = (("x", "y", "z"), ("y", "z", "x"), ("z", "x", "y"))
GATHER_ROWS = ((0, 32), (32, 32), (64, 16))
ROWS = ((0, 32), (32, 16), (48, 32))
DIMS = {"z": 0, "x": 1, "y": 2}


def place():
    d, j = lax.axis_index("dp"), lax.axis_index("seq")
    return d, j, {"z": lax.div(j, 4), "x": lax.rem(j, 4), "y": lax.div(d, 2)}, lax.rem(d, 2)


def peer(pos, core, axis, hop):
    at = dict(pos)
    at[axis] = lax.rem(at[axis] + hop + 4, 4)
    return (at["y"] * 2 + core, at["z"] * 4 + at["x"])


OTHERS = [(a, b) for a in range(4) for b in range(4) if (a, b) != (0, 0)]


def peer2(pos, core, axes, hops):
    at = {a: lax.rem(pos[a] + h, 4) for a, h in zip(axes, hops)}
    at = {**pos, **at}
    return (at["y"] * 2 + core, at["z"] * 4 + at["x"])


def planes(pos, core):
    near = [peer(pos, core, axis, hop) for axis in "xyz" for hop in (1, 2, 3)]
    return near + [peer2(pos, core, axes, (a, b)) for axes in ("xy", "yz", "zx") for a, b in OTHERS if a and b]


def greet(devices):
    barrier = pltpu.get_barrier_semaphore()
    for device in devices:
        pl.semaphore_signal(barrier, inc=1, device_id=device, device_id_type=MESH)
    pl.semaphore_wait(barrier, len(devices))


def remote(src, dst, send_sem, recv_sem, device):
    return pltpu.make_async_remote_copy(
        src_ref=src, dst_ref=dst, send_sem=send_sem, recv_sem=recv_sem, device_id=device, device_id_type=MESH
    )


def slab(ref, fixed, tail):
    index = [slice(None)] * 3
    for axis, value in fixed.items():
        index[DIMS[axis]] = value
    return ref.at[tuple(index) + tail]


def gather_kernel(parts, with_tail, *refs):
    if with_tail:
        shard, tail_ref, out, halo, local_sem, ssem, rsem, fsend, frecv, csend, crecv, hsend, hrecv = refs
    else:
        shard, out, local_sem, ssem, rsem, fsend, frecv, csend, crecv = refs
    d, j, pos, core = place()
    sibling = (pos["y"] * 2 + 1 - core, j)
    following, previous = (d, lax.rem(j + 1, 16)), (d, lax.rem(j + 15, 16))
    greet(planes(pos, core) + [sibling] + ([previous] if with_tail else []))
    sent = []

    def go(copy):
        copy.start()
        sent.append(copy)

    own = out.at[pos["z"], pos["x"], pos["y"], core]
    local = pltpu.make_async_copy(shard, own, local_sem)
    local.start()
    half = out.shape[-1] // 2
    columns = (pl.ds(0, half), pl.ds(half, half))
    whole = slice(None)
    hops = (0, -1, 1, 2)

    def step(p, slot, axis, fixed):
        row, count = parts[p][1]
        rows = pl.ds(row, count)
        right, left = peer(pos, core, axis, 1), peer(pos, core, axis, -1)

        def at(hop, cols=whole, which=core):
            return slab(out, {**fixed, axis: lax.rem(pos[axis] + hop + 4, 4)}, (which, rows, cols))

        def ring(hop, cols, which, device):
            return remote(at(hop, cols), at(hop, cols), ssem.at[p, slot, which], rsem.at[p, slot, which], device)

        def send(which):
            hop, cols, device = ((0, whole, right), (0, whole, left), (-1, columns[0], right), (1, columns[1], left))[which]
            go(ring(hop, cols, which, device))

        def landed(which):
            hop, cols, device = ((-1, whole, right), (1, whole, left), (2, columns[0], right), (2, columns[1], left))[which]
            ring(hop, cols, which, device).wait_recv()

        def across(which):
            there = at(hops[which])
            go(remote(there, there, csend.at[p, slot, which], crecv.at[p, slot, which], sibling))

        def crossed(which):
            there = at(hops[which], whole, 1 - core)
            remote(there, there, csend.at[p, slot, which], crecv.at[p, slot, which], sibling).wait_recv()

        return send, landed, across, crossed

    count = range(len(parts))

    def spot(axis, hop):
        return lax.rem(pos[axis] + hop + 4, 4)

    def direct(p, k):
        (one, two, three), (row, rows) = parts[p]
        device = peer2(pos, core, (one, two), OTHERS[k])
        return remote(shard.at[pl.ds(row, rows), :], own.at[pl.ds(row, rows), :], fsend.at[p, k], frecv.at[p, k], device)

    def arrived(p, k):
        (one, two, three), (row, rows) = parts[p]
        a, b = OTHERS[k]
        there = slab(out, {one: spot(one, -a), two: spot(two, -b), three: pos[three]}, (core, pl.ds(row, rows), whole))
        remote(there, there, fsend.at[p, k], frecv.at[p, k], peer2(pos, core, (one, two), OTHERS[k])).wait_recv()

    third = []
    for p in count:
        one, two, three = parts[p][0]
        third.append([step(p, i, three, {two: spot(two, hops[i])}) for i in range(4)])
    turn = [[k for k, (a, b) in enumerate(OTHERS) if (-b) % 4 == hops[i] % 4] for i in range(4)]
    for i in range(4):
        for k in turn[i]:
            for p in count:
                go(direct(p, k))
    if with_tail:
        tail_copy = remote(tail_ref, halo, hsend, hrecv, following)
        go(tail_copy)
    local.wait()
    for i in range(4):
        for p in count:
            for k in turn[i]:
                arrived(p, k)
            send, _, across, _ = third[p][i]
            send(0)
            send(1)
            across(0)
    for i in range(4):
        for which in (0, 1):
            for p in count:
                send, landed, across, _ = third[p][i]
                landed(which)
                send(2 + which)
                across(1 + which)
    for i in range(4):
        for p in count:
            _, landed, across, _ = third[p][i]
            landed(2)
            landed(3)
            across(3)
    for i in range(4):
        for p in count:
            for which in range(4):
                third[p][i][3](which)
    if with_tail:
        tail_copy.wait_recv()
    for copy in sent:
        copy.wait_send()


def gather(shard, tail, parts, collective_id):
    rows, columns = shard.shape
    count = len(parts)
    anyspace = pl.BlockSpec(memory_space=pl.ANY)
    dma = pltpu.SemaphoreType.DMA
    out_shape = [jax.ShapeDtypeStruct((4, 4, 4, 2, rows, columns), shard.dtype)]
    sems = [dma, dma((count, 4, 4)), dma((count, 4, 4)), dma((count, 15)), dma((count, 15)), dma((count, 4, 4)), dma((count, 4, 4))]
    operands = [shard]
    if tail is not None:
        out_shape.append(jax.ShapeDtypeStruct(tail.shape, tail.dtype))
        sems += [dma, dma]
        operands.append(tail)
    return pl.pallas_call(
        functools.partial(gather_kernel, parts, tail is not None),
        name="gather_shards",
        out_shape=out_shape,
        in_specs=[anyspace] * len(operands),
        out_specs=[anyspace] * len(out_shape),
        scratch_shapes=sems,
        compiler_params=pltpu.CompilerParams(collective_id=collective_id, has_side_effects=True, vmem_limit_bytes=VMEM_LIMIT),
    )(*operands)


def reduce_kernel(xpart, dpart, edge, out, all_params, halo, sums, cross, *scratch):
    buffers, plane, scratch = scratch[:48], scratch[48:51], scratch[51:]
    packed, own_sem, csend, crecv, ssem, rsem, fsend, frecv, psend, precv, qsend, qrecv, hsend, hrecv = scratch
    d, j, pos, core = place()
    sibling = (pos["y"] * 2 + 1 - core, j)
    following, previous = (d, lax.rem(j + 1, 16)), (d, lax.rem(j + 15, 16))
    column = [(lax.rem(pos["y"] + k // 2, 4) * 2 + lax.rem(core + k, 2), j) for k in range(1, 8)]
    greet(planes(pos, core) + column + [following])
    sent = []
    hops = (2, 1, -1, 0)
    half = 256
    whole = slice(None)
    columns = (slice(0, half), slice(half, 2 * half))

    def go(copy):
        copy.start()
        sent.append(copy)

    def spot(axis, hop):
        return lax.rem(pos[axis] + hop + 4, 4)

    def mine(p, i, which):
        row, count = ROWS[p]
        fixed = {ORDERS[p][1]: spot(ORDERS[p][1], hops[i])}
        return slab(xpart if p < 2 else dpart, fixed, (which, pl.ds(row if p < 2 else 0, count), whole))

    def beside(ref, p, i):
        row, count = ROWS[p]
        return slab(ref, {ORDERS[p][1]: spot(ORDERS[p][1], hops[i])}, (pl.ds(row, count), whole))

    def across(p, i):
        return remote(mine(p, i, 1 - core), beside(cross, p, i), csend.at[p, i], crecv.at[p, i], sibling)

    def own(p, i):
        return pltpu.make_async_copy(mine(p, i, core), beside(sums, p, i), own_sem.at[p, i])

    for i in range(4):
        for p in range(3):
            go(across(p, i))
            own(p, i).start()
    edge_copy = remote(edge, halo, hsend, hrecv, previous)
    go(edge_copy)

    def index_of(fixed, free, values):
        index = [None] * 3
        for a, v in {**fixed, **dict(zip(free, values))}.items():
            index[DIMS[a]] = v
        return tuple(index)

    def add_core(p, i):
        row, count = ROWS[p]
        rows = pl.ds(row, count)
        middle = ORDERS[p][1]
        free = [a for a in "zxy" if a != middle]
        own(p, i).wait()
        across(p, i).wait_recv()

        def one(k, _):
            at = index_of({middle: spot(middle, hops[i])}, free, (lax.div(k, 4), lax.rem(k, 4))) + (rows, whole)
            sums[at] = (sums[at].astype(jnp.float32) + cross[at].astype(jnp.float32)).astype(jnp.bfloat16)
            return 0

        lax.fori_loop(0, 16, one, 0)

    def step(p, slot, axis, fixed, free):
        row, count = ROWS[p]
        rows = pl.ds(row, count)
        right, left = peer(pos, core, axis, 1), peer(pos, core, axis, -1)
        bufs = buffers[(p * 4 + slot) * 4:(p * 4 + slot) * 4 + 4]

        def copy(which):
            hop, cols, device = ((2, columns[0], right), (2, columns[1], left), (1, whole, right), (-1, whole, left))[which]
            source = slab(sums, {**fixed, axis: spot(axis, hop)}, (rows, cols))
            return remote(source, bufs[which], ssem.at[p, slot, which], rsem.at[p, slot, which], device)

        def add(hop, cols, terms):
            def one(k, _):
                at = index_of({**fixed, axis: spot(axis, hop)}, free, (k,)) + (rows, cols)
                total = sums[at].astype(jnp.float32)
                for term in terms:
                    total = total + term[k].astype(jnp.float32)
                sums[at] = total.astype(jnp.bfloat16)
                return 0

            lax.fori_loop(0, 4, one, 0)

        def begin():
            go(copy(0))
            go(copy(1))

        def relay(which):
            copy(which).wait_recv()
            add((1, -1)[which], columns[which], bufs[which:which + 1])
            go(copy(2 + which))

        def finish():
            copy(2).wait_recv()
            copy(3).wait_recv()
            add(0, whole, bufs[2:])

        return begin, relay, finish

    def direct(p, k):
        one, two, three = ORDERS[p]
        a, b = OTHERS[k]
        row, count = ROWS[p]
        source = slab(sums, {one: spot(one, a), two: spot(two, b), three: pos[three]}, (pl.ds(row, count), whole))
        return remote(source, plane[p].at[k], fsend.at[p, k], frecv.at[p, k], peer2(pos, core, (one, two), (a, b)))

    parts = range(3)
    turn = [[k for k, (a, b) in enumerate(OTHERS) if b % 4 == hops[i] % 4] for i in range(4)]
    outer = []
    for p in parts:
        one, two, three = ORDERS[p]
        outer.append([step(p, i, three, {two: spot(two, hops[i])}, [one]) for i in range(4)])
    for i in range(4):
        for p in parts:
            add_core(p, i)
            outer[p][i][0]()
    for i in range(4):
        for which in (0, 1):
            for p in parts:
                outer[p][i][1](which)
    for i in range(4):
        for p in parts:
            outer[p][i][2]()
            for k in turn[i]:
                go(direct(p, k))
    for p in parts:
        row, count = ROWS[p]
        rows = pl.ds(row, count)
        for k in range(15):
            direct(p, k).wait_recv()
        out[rows, :] = sums[pos["z"], pos["x"], pos["y"], rows, :].astype(jnp.float32)

        def one_more(k, _):
            out[rows, :] += plane[p][k].astype(jnp.float32)
            return 0

        lax.fori_loop(0, 15, one_more, 0)

    packed[...] = jnp.zeros((16, 128), jnp.bfloat16)
    rowsum = jnp.concatenate(
        [out[36 + q:37 + q, 128 * s:128 * s + 128] for q in range(3) for s in range(4)] + [jnp.zeros((4, 128), jnp.float32)], axis=0
    )
    packed[...] = rowsum.astype(jnp.bfloat16)
    all_params[pos["z"], pos["x"], pos["y"], core] = packed[...]

    def place_of(hops):
        return all_params.at[lax.rem(pos["z"] + 4 - hops[0], 4), lax.rem(pos["x"] + 4 - hops[1], 4), pos["y"], core]

    def flat(k):
        return remote(place_of((0, 0)), place_of((0, 0)), psend.at[k], precv.at[k], peer2(pos, core, "zx", OTHERS[k]))

    def upright(k):
        ours = all_params.at[:, :, pos["y"], core]
        return remote(ours, ours, qsend.at[k], qrecv.at[k], column[k - 1])

    for k in range(15):
        go(flat(k))
    for k in range(15):
        there = place_of(OTHERS[k])
        remote(there, there, psend.at[k], precv.at[k], peer2(pos, core, "zx", OTHERS[k])).wait_recv()
    for k in range(1, 8):
        go(upright(k))
    for k in range(1, 8):
        y, c = lax.rem(pos["y"] + 4 - k // 2, 4), lax.rem(core + k, 2)
        there = all_params.at[:, :, y, c]
        remote(there, there, qsend.at[k], qrecv.at[k], column[k - 1]).wait_recv()
    edge_copy.wait_recv()
    for copy in sent:
        copy.wait_send()


def reduce_all(xpart, dpart, edge):
    vmem = pl.BlockSpec(memory_space=pltpu.VMEM)
    anyspace = pl.BlockSpec(memory_space=pl.ANY)
    dma = pltpu.SemaphoreType.DMA
    bf16 = jnp.bfloat16
    buffers = []
    for row, count in ROWS:
        buffers += ([pltpu.VMEM((4, count, 256), bf16)] * 2 + [pltpu.VMEM((4, count, 512), bf16)] * 2) * 4
    buffers += [pltpu.VMEM((15, count, 512), bf16) for row, count in ROWS]
    return pl.pallas_call(
        reduce_kernel,
        name="reduce_shards",
        out_shape=[
            jax.ShapeDtypeStruct((80, 512), jnp.float32),
            jax.ShapeDtypeStruct((4, 4, 4, 2, 16, 128), bf16),
            jax.ShapeDtypeStruct(edge.shape, edge.dtype),
        ],
        in_specs=[anyspace] * 3,
        out_specs=[vmem, vmem, anyspace],
        scratch_shapes=[pltpu.VMEM((4, 4, 4, 80, 512), bf16)] * 2 + buffers + [
            pltpu.VMEM((16, 128), bf16),
            dma((3, 4)), dma((3, 4)), dma((3, 4)), dma((3, 4, 4)), dma((3, 4, 4)), dma((3, 15)), dma((3, 15)),
            dma((15,)), dma((15,)), dma((8,)), dma((8,)), dma, dma,
        ],
        compiler_params=pltpu.CompilerParams(
            collective_id=2, has_side_effects=True, vmem_limit_bytes=VMEM_LIMIT
        ),
    )(xpart, dpart, edge)


def spread(rows, columns, row_is_plain):
    index = lax.broadcasted_iota(jnp.int32, (rows, columns), 0 if row_is_plain else 1)
    padded = lax.broadcasted_iota(jnp.int32, (rows, columns), 1 if row_is_plain else 0)
    low = 32 * lax.div(lax.rem(index, 128), 16) + 16 * lax.div(index, 128) + lax.rem(index, 16)
    plain = jnp.where(index < 256, low, index)
    device = lax.div(padded, 48)
    inside = padded - 48 * device
    return jnp.where((inside < 36) & (36 * device + inside == plain), 1.0, 0.0).astype(jnp.bfloat16)


HALO = pl.BlockSpec((3, 8, 128), lambda i: (0, i, 0))


def convolve(x_ref, halo_ref, cw_ref, cb_ref, ext):
    first = lax.axis_index("seq") == 0
    for r in range(3):
        for s in range(8):
            ext[5 + r:6 + r, 128 * s:128 * s + 128] = jnp.where(first, 0.0, halo_ref[r, s:s + 1, :])
    ext[8:T + 8, :] = x_ref[...].astype(jnp.float32)

    def part(cols):
        pre = cb_ref[:, cols] + cw_ref[0:1, cols] * ext[5:5 + T, cols]
        for k in range(1, 4):
            pre = pre + cw_ref[k:k + 1, cols] * ext[5 + k:5 + k + T, cols]
        gate = logistic(pre)
        act = pre * gate
        return act.astype(jnp.bfloat16), gate + act * (1.0 - gate)

    return part


def conv_kernel(x_ref, halo_ref, cw_ref, cb_ref, w_ref, xc_ref, low_ref, bc_ref, ext, acc):
    i = pl.program_id(0)

    @pl.when(i == 0)
    def _():
        acc[...] = jnp.zeros(acc.shape, jnp.float32)

    part = convolve(x_ref, halo_ref, cw_ref, cb_ref, ext)
    for half in range(2):
        cols = slice(512 * half, 512 * half + 512)
        xc, _ = part(cols)
        xc_ref[:, cols] = xc
        acc[...] += lax.dot_general(
            xc, w_ref[half].reshape(384, 512), (((1,), (1,)), ((), ())), preferred_element_type=jnp.float32
        )

    @pl.when(i == pl.num_programs(0) - 1)
    def _():
        low_ref[...] = jnp.dot(
            acc[...].astype(jnp.bfloat16), spread(384, 256, False), preferred_element_type=jnp.float32
        ).astype(jnp.bfloat16)
        for n in range(32):
            bc_ref[n] = jnp.broadcast_to(acc[:, 340 + n:341 + n], (T, 128))


def conv_project(x, halo, cw, cb, wg):
    E = x.shape[1]
    nat, row, full = tile_specs(1024)
    S = jax.ShapeDtypeStruct
    return pl.pallas_call(
        conv_kernel, grid=(E // 1024,), name="conv_project",
        in_specs=[nat, HALO, row(4), row(1), pl.BlockSpec((2, 8, 48, 512), lambda i: (i, 0, 0, 0))],
        out_specs=[nat, full(T, 256), full(32, T, 128)],
        out_shape=[S((T, E), jnp.bfloat16), S((T, 256), jnp.bfloat16), S((32, T, 128), jnp.float32)],
        scratch_shapes=[pltpu.VMEM((T + 8, 1024), jnp.float32), pltpu.VMEM((T, 384), jnp.float32)],
        compiler_params=pltpu.CompilerParams(vmem_limit_bytes=VMEM_LIMIT),
    )(x, halo, cw, cb, wg)


def grads_kernel(glow_ref, gbc_ref, gcx_ref, x_ref, halo_ref, cw_ref, cb_ref, w_ref, par_ref, ga_ref,
                 gx_ref, head_ref, tail_ref, part_ref, gproj, turned, ext, wide, gext):
    i = pl.program_id(0)
    f32 = jnp.float32

    @pl.when(i == 0)
    def _():
        plain = jnp.concatenate([glow_ref[...], gbc_ref[...]], axis=1).astype(jnp.bfloat16)
        gproj[...] = jnp.dot(plain, spread(288, 384, True), preferred_element_type=f32).astype(jnp.bfloat16)
        turned[...] = gproj[...].T
        gext[T:T + 8, :] = jnp.zeros((8, gext.shape[1]), f32)

    part = convolve(x_ref, halo_ref, cw_ref, cb_ref, ext)
    for half in range(2):
        cols = slice(512 * half, 512 * half + 512)
        xc, slope = part(cols)
        weights = w_ref[half].reshape(384, 512)
        g_conv = (gcx_ref[:, cols] + jnp.dot(gproj[...], weights, preferred_element_type=f32)) * slope
        gext[0:T, cols] = g_conv
        wide[...] = jnp.dot(turned[...], xc, preferred_element_type=f32)

        def put(r, value):
            wide[48 * (r // 3) + 36 + r % 3:48 * (r // 3) + 37 + r % 3, :] = value

        for k in range(4):
            put(k, jnp.sum(g_conv * ext[5 + k:5 + k + T, cols], axis=0, keepdims=True))
        put(4, jnp.sum(g_conv, axis=0, keepdims=True))
        put(5, par_ref[0:1, cols])
        put(6, par_ref[1:2, cols])
        for n in range(N):
            put(7 + n, jnp.concatenate([ga_ref[n, 4 * half + s:4 * half + s + 1, :] for s in range(4)], axis=1))
        part_ref[half] = wide[...].reshape(8, 48, 512).astype(jnp.bfloat16)
    total = cw_ref[0:1, :] * gext[3:3 + T, :]
    for k in range(1, 4):
        total = total + cw_ref[k:k + 1, :] * gext[3 - k:3 - k + T, :]
    gx_ref[...] = total.astype(jnp.bfloat16)
    for r in range(3):
        for s in range(8):
            head_ref[r, s:s + 1, :] = gext[r:r + 1, 128 * s:128 * s + 128]
    tail_ref[...] = gext[T - 16:T, :]


def weight_grads(glow, gbc, gcx, x, halo, cw, cb, wg, par, ga):
    E = x.shape[1]
    nat, row, full = tile_specs(1024)
    S = jax.ShapeDtypeStruct
    f32 = jnp.float32
    block = pl.BlockSpec((2, 8, 48, 512), lambda i: (i, 0, 0, 0))
    return pl.pallas_call(
        grads_kernel, grid=(E // 1024,), name="weight_grads",
        in_specs=[full(T, 256), full(T, 32), nat, nat, HALO, row(4), row(1), block, row(8),
                  pl.BlockSpec((N, 8, 128), lambda i: (0, i, 0))],
        out_specs=[nat, HALO, row(16), block],
        out_shape=[S((T, E), jnp.bfloat16), S((3, E // 128, 128), f32), S((16, E), f32), S((E // 512, 8, 48, 512), jnp.bfloat16)],
        scratch_shapes=[pltpu.VMEM((T, 384), jnp.bfloat16), pltpu.VMEM((384, T), jnp.bfloat16), pltpu.VMEM((T + 8, 1024), f32),
                        pltpu.VMEM((384, 512), f32),
                        pltpu.VMEM((T + 8, 1024), f32)],
        compiler_params=pltpu.CompilerParams(vmem_limit_bytes=VMEM_LIMIT),
    )(glow, gbc, gcx, x, halo, cw, cb, wg, par, ga)


def last_rows_kernel(gx_ref, tail_ref, edge_ref, cw_ref, out_ref, ext):
    ext[0:16, :] = tail_ref[...]
    last = lax.axis_index("seq") == 15
    for r in range(3):
        for s in range(edge_ref.shape[1]):
            ext[16 + r:17 + r, 128 * s:128 * s + 128] = jnp.where(last, 0.0, edge_ref[r, s:s + 1, :])
    total = cw_ref[0:1, :] * ext[3:19, :]
    for k in range(1, 4):
        total = total + cw_ref[k:k + 1, :] * ext[3 - k:19 - k, :]
    out_ref[...] = total.astype(jnp.bfloat16)


def last_rows(gx, tail, edge, cw):
    E = gx.shape[1]
    full = lambda *shape: pl.BlockSpec(shape, lambda i: (0,) * len(shape))
    block = pl.BlockSpec((16, E), lambda i: (T // 16 - 1, 0))
    return pl.pallas_call(
        last_rows_kernel, grid=(1,), name="last_rows",
        in_specs=[block, full(16, E), full(3, E // 128, 128), full(4, E)], out_specs=block,
        out_shape=jax.ShapeDtypeStruct((T, E), jnp.bfloat16),
        scratch_shapes=[pltpu.VMEM((24, E), jnp.float32)],
        input_output_aliases={0: 0},
        compiler_params=pltpu.CompilerParams(vmem_limit_bytes=VMEM_LIMIT),
    )(gx, tail, edge, cw)


def local(x_branch, z_branch, out_grad, x_weight, dt_weight, conv_weight, conv_bias, dt_bias, a_log, d_skip):
    x, z, g = x_branch[0], z_branch[0], out_grad[0]
    E = x.shape[1]
    shard = jnp.concatenate([x_weight.T, jnp.zeros((12, 512), jnp.bfloat16), dt_weight], axis=0)
    gathered, halo = gather(shard, x[T - 3:].astype(jnp.float32).reshape(3, E // 128, 128), tuple(zip(ORDERS, GATHER_ROWS)), 0)
    wg = gathered.reshape(16, 8, 80, 512)
    a2_wide = -jnp.exp(a_log) * LOG2E
    a2 = a2_wide.reshape(N, E // 128, 128)
    bias = conv_bias[None]
    xc, low, bc = conv_project(x, halo, conv_weight, bias, wg)
    step3, drive3, gs3, sig, carried = local_scan(low, wg, xc, z, g, dt_bias[None], a2, bc)
    mixer_out, grad_z, gcx, gdt, par, ga, glow, gbc = main_scan(
        step3, drive3, gs3, sig, xc, z, g, d_skip[None], a2, bc, carried, wg, low
    )
    gx, head, tail, part = weight_grads(glow, gbc, gcx, x, halo, conv_weight, bias, wg, par, ga)
    reduced, params, edge = reduce_all(part.reshape(4, 4, 4, 2, 48, 512), gdt.reshape(4, 4, 4, 2, 32, 512), head)
    grad_x = last_rows(gx, tail, edge, conv_weight)
    params = params.reshape(16, 8, 16, 128)[:, :, :12].reshape(16, 8, 3, 4, 128)
    params = params.transpose(1, 2, 0, 3, 4).reshape(24, E).astype(jnp.float32)
    return (
        mixer_out[None], grad_x[None], grad_z[None], reduced[:36].T, reduced[48:80],
        params[0:4], params[4], params[5], params[7:23], params[6],
    )


def solution(mesh):
    tokens, weights, whole = P("dp", "seq", None), P("seq", "dp"), P()
    in_specs = (tokens,) * 3 + (weights, P("dp", "seq")) + (whole,) * 5
    out_specs = (tokens,) * 3 + (weights, P("dp", "seq")) + (whole,) * 5
    return jax.shard_map(local, mesh=mesh, in_specs=in_specs, out_specs=out_specs, check_vma=False)
```

```python
import functools

import jax
import jax.numpy as jnp
from jax import lax
from jax.experimental import pallas as pl
from jax.experimental.pallas import tpu as pltpu
from jax.sharding import PartitionSpec as P

T = 128
N = 16
LN2 = 0.6931471805599453
LOG2E = 1.4426950408889634
VMEM_LIMIT = 62 * 2**20
LOCAL_GROUP, LOCAL_UNROLL = 4, 16
SHIPMENTS = ((0, 4), (4, 3), (7, 1))
CHUNKS = 1
FWD_GROUP, FWD_UNROLL = 8, 16
BWD_GROUP, BWD_UNROLL = 8, 16


def logistic(values):
    return 0.5 * jnp.tanh(0.5 * values) + 0.5


def tile_specs(width):
    nat = pl.BlockSpec((T, width), lambda i: (0, i))
    row = lambda count: pl.BlockSpec((count, width), lambda i: (0, i))
    full = lambda *shape: pl.BlockSpec(shape, lambda i: (0,) * len(shape))
    return nat, row, full


def local_scan_kernel(low_ref, wa_ref, wb_ref, x_ref, z_ref, g_ref, bias_ref, a2_ref, bc_ref, rates_ref,
                      step_ref, drive_ref, gs_ref, sig_ref, carried, ends_all, got, back,
                      ssem, rsem, bsend, brecv, own_sem):
    i = pl.program_id(0)
    d, j, _, _ = place()
    others = [lax.rem(j + k, 16) for k in range(1, 16)]

    @pl.when(i == 0)
    def _():
        barrier = pltpu.get_barrier_semaphore()
        for k in others:
            pl.semaphore_signal(barrier, inc=1, device_id=(d, k), device_id_type=MESH)

    low = low_ref[...]
    rows = [ref.reshape(T * 8, 128) for ref in (step_ref, drive_ref, gs_ref)]
    for half in range(2):
        dt = jnp.concatenate([wa_ref[half].reshape(128, 512), wb_ref[half].reshape(128, 512)], axis=0)
        cols = pl.ds(512 * half, 512)
        rate = jnp.dot(low, dt, preferred_element_type=jnp.float32) + bias_ref[:, cols]
        step = jnp.maximum(rate, 0.0) + jnp.log1p(jnp.exp(-jnp.abs(rate)))
        sig_ref[:, cols] = jnp.exp(rate - step)
        z = z_ref[:, cols].astype(jnp.float32)
        gs = g_ref[:, cols].astype(jnp.float32) * (z * logistic(z))
        drive = step * x_ref[:, cols].astype(jnp.float32)
        for s in range(4):
            for ref, value in zip(rows, (step, drive, gs)):
                ref[pl.ds(4 * half + s, T, stride=8), :] = value[:, 128 * s:128 * s + 128]

    zero = jnp.zeros((8, 128), jnp.float32)
    one = jnp.ones((8, 128), jnp.float32)
    ends, lams = [], []
    for first in range(0, N, LOCAL_GROUP):
        group = range(first, first + LOCAL_GROUP)

        def body(k, carry):
            tot, ends, prods, lams = carry
            for unrolled in range(LOCAL_UNROLL):
                t = k * LOCAL_UNROLL + unrolled
                st, dr, gv = step_ref[t], drive_ref[t], gs_ref[t]
                new_ends, new_prods, new_lams = [], [], []
                for q, n in enumerate(group):
                    f = jnp.exp2(st * a2_ref[n])
                    new_ends.append(f * ends[q] + bc_ref[n, pl.ds(t, 1), :] * dr)
                    p = prods[q] * f
                    new_prods.append(p)
                    new_lams.append(lams[q] + p * (bc_ref[N + n, pl.ds(t, 1), :] * gv))
                tot, ends, prods, lams = tot + st, tuple(new_ends), tuple(new_prods), tuple(new_lams)
            return tot, ends, prods, lams

        many = LOCAL_GROUP
        tot, e, _, l = lax.fori_loop(0, T // LOCAL_UNROLL, body, (zero, (zero,) * many, (one,) * many, (zero,) * many))
        ends += e
        lams += l
    high = tot.astype(jnp.bfloat16)
    sums = jnp.concatenate([high.astype(jnp.float32), tot - high.astype(jnp.float32)], axis=0).astype(jnp.bfloat16)
    for n in range(N):
        ends_all[n, i, 0:16, :] = jnp.concatenate([ends[n], lams[n]], axis=0).astype(jnp.bfloat16)
        ends_all[n, i, 16:32, :] = sums

    def chunks(group):
        return pl.ds(SHIPMENTS[group][0], SHIPMENTS[group][1])

    def outgoing(group, to):
        return remote(ends_all.at[to, chunks(group)], got.at[j, chunks(group)], ssem.at[group, to], rsem.at[group, j], (d, to))

    def returned(group, to):
        return remote(back.at[to, chunks(group)], carried.at[j, chunks(group)], bsend.at[group, to], brecv.at[group, j], (d, to))

    def ship(group):
        for to in others:
            outgoing(group, to).start()
        first, count = SHIPMENTS[group]
        for k in range(first, first + count):
            got[j, k] = ends_all[j, k]

    def recur(group):
        for source in others:
            there = got.at[source, chunks(group)]
            remote(there, there, ssem.at[group, source], rsem.at[group, source], (d, source)).wait_recv()
        first, count = SHIPMENTS[group]
        for c in range(first, first + count):
            rates = rates_ref[j, 8 * c:8 * c + 8, :]
            blocks = [got[k, c].astype(jnp.float32) for k in range(16)]
            decays = [jnp.exp2(rates * (block[16:24] + block[24:32])) for block in blocks]
            enter, leave = [jnp.zeros((8, 128), jnp.float32)], [jnp.zeros((8, 128), jnp.float32)]
            for k in range(15):
                enter.append(decays[k] * enter[k] + blocks[k][0:8])
                leave.append(decays[15 - k] * leave[k] + blocks[15 - k][8:16])
            for k in range(16):
                back[k, c] = jnp.concatenate([enter[k], leave[15 - k]], axis=0).astype(jnp.bfloat16)
        for to in others:
            returned(group, to).start()
        pltpu.make_async_copy(back.at[j, chunks(group)], carried.at[j, chunks(group)], own_sem.at[group]).start()

    @pl.when(i == 3)
    def _():
        pl.semaphore_wait(pltpu.get_barrier_semaphore(), 15)
        ship(0)

    @pl.when(i == 5)
    def _():
        recur(0)

    @pl.when(i == 6)
    def _():
        ship(1)

    @pl.when(i == 7)
    def _():
        ship(2)
        recur(1)
        recur(2)
        for group in range(3):
            pltpu.make_async_copy(back.at[j, chunks(group)], carried.at[j, chunks(group)], own_sem.at[group]).wait()
            for k in others:
                there = carried.at[k, chunks(group)]
                remote(there, there, bsend.at[group, k], brecv.at[group, k], (d, k)).wait_recv()
                outgoing(group, k).wait_send()
                returned(group, k).wait_send()


def local_scan(low, wg, x_conv, z, g, bias, a2, bc):
    E = x_conv.shape[1]
    C = E // 1024
    f32 = jnp.float32
    nat, row, full = tile_specs(1024)
    tri = pl.BlockSpec((T, 8, 128), lambda i: (0, i, 0))
    return pl.pallas_call(
        local_scan_kernel, grid=(C,), name="local_scan",
        in_specs=[full(T, 256), pl.BlockSpec((2, 8, 16, 512), lambda i: (i, 0, 3, 0)),
                  pl.BlockSpec((2, 8, 16, 512), lambda i: (i, 0, 4, 0)), nat, nat, nat,
                  row(1), pl.BlockSpec((N, 8, 128), lambda i: (0, i, 0)), full(32, T, 128), full(N, E // 128, 128)],
        out_specs=[tri, tri, tri, nat, pl.BlockSpec(memory_space=pl.ANY)],
        out_shape=[jax.ShapeDtypeStruct((T, E // 128, 128), f32)] * 3 + [
            jax.ShapeDtypeStruct((T, E), f32), jax.ShapeDtypeStruct((16, C, 16, 128), jnp.bfloat16)],
        scratch_shapes=[pltpu.VMEM((16, C, 32, 128), jnp.bfloat16)] * 2 + [pltpu.VMEM((16, C, 16, 128), jnp.bfloat16)]
        + [pltpu.SemaphoreType.DMA((3, 16))] * 4 + [pltpu.SemaphoreType.DMA((3,))],
        compiler_params=pltpu.CompilerParams(collective_id=1, has_side_effects=True, vmem_limit_bytes=VMEM_LIMIT),
    )(low, wg, wg, x_conv, z, g, bias, a2, bc, a2)


def main_scan_kernel(step_ref, drive_ref, gs_ref, sig_ref, x_ref, z_ref, g_ref, dskip_ref, a2_ref, bc_ref, ent_ref, wa_ref, wb_ref, low_ref,
              mix_ref, gz_ref, gcx_ref, gdt_ref, par_ref, ga_ref, glow_ref, gbc_ref,
              es, us, y3, gd3, gr3, accb, accc, alow, turned, both):
    i = pl.program_id(0)
    f32 = jnp.float32
    span = [slice(8 * q, 8 * q + 8) for q in range(CHUNKS)]

    @pl.when(i == 0)
    def _():
        accb[...] = jnp.zeros(accb.shape, f32)
        accc[...] = jnp.zeros(accc.shape, f32)
        alow[...] = jnp.zeros(alow.shape, f32)
        turned[...] = low_ref[...].T

    es[...] = ent_ref[...].astype(f32)

    def state(base, n, q):
        return es[n, q, base:base + 8, :]

    def add(total, term):
        return term if total is None else total + term

    def inputs(t):
        return tuple([ref[t, rows] for rows in span] for ref in (step_ref, drive_ref, gs_ref))

    zero = jnp.zeros((8, 128), f32)
    for first in range(0, N, FWD_GROUP):
        group = range(first, first + FWD_GROUP)

        def forward(k, hs):
            for unrolled in range(FWD_UNROLL):
                t = k * FWD_UNROLL + unrolled
                st, dr, gv = inputs(t)
                ys = [None if first == 0 else y3[t, rows] for rows in span]
                new = []
                for p, n in enumerate(group):
                    b, c = bc_ref[n, pl.ds(t, 1), :], bc_ref[N + n, pl.ds(t, 1), :]
                    total = accc[t, n]
                    for q in range(CHUNKS):
                        u = jnp.exp2(st[q] * a2_ref[n, span[q]]) * hs[p * CHUNKS + q]
                        us[t, n, span[q]] = u
                        h = u + b * dr[q]
                        new.append(h)
                        ys[q] = add(ys[q], c * h)
                        total = total + h * gv[q]
                    accc[t, n] = total
                for q in range(CHUNKS):
                    y3[t, span[q]] = ys[q]
                hs = tuple(new)
            return hs

        lax.fori_loop(0, T // FWD_UNROLL, forward, tuple(state(0, n, q) for n in group for q in range(CHUNKS)))

    for first in range(0, N, BWD_GROUP):
        group = range(first, first + BWD_GROUP)

        def backward(k, carry):
            adj, ra = carry
            for unrolled in range(BWD_UNROLL):
                t = T - 1 - (k * BWD_UNROLL + unrolled)
                st, dr, gv = inputs(t)
                gd = [None if first == 0 else gd3[t, rows] for rows in span]
                gr = [None if first == 0 else gr3[t, rows] for rows in span]
                na, nr = [], []
                for p, n in enumerate(group):
                    b, c = bc_ref[n, pl.ds(t, 1), :], bc_ref[N + n, pl.ds(t, 1), :]
                    total = accb[t, n]
                    for q in range(CHUNKS):
                        rate = a2_ref[n, span[q]]
                        lam = c * gv[q] + adj[p * CHUNKS + q]
                        gd[q] = add(gd[q], lam * b)
                        total = total + lam * dr[q]
                        na.append(jnp.exp2(st[q] * rate) * lam)
                        m = lam * us[t, n, span[q]]
                        gr[q] = add(gr[q], m * rate)
                        nr.append(ra[p * CHUNKS + q] + m * st[q])
                    accb[t, n] = total
                for q in range(CHUNKS):
                    gd3[t, span[q]] = gd[q]
                    gr3[t, span[q]] = gr[q]
                adj, ra = tuple(na), tuple(nr)
            return adj, ra

        _, ra = lax.fori_loop(0, T // BWD_UNROLL, backward, (tuple(state(8, n, q) for n in group for q in range(CHUNKS)), (zero,) * (BWD_GROUP * CHUNKS)))
        for p, n in enumerate(group):
            for q in range(CHUNKS):
                ga_ref[n, span[q]] = ra[p * CHUNKS + q] * a2_ref[n, span[q]] * LN2

    for half in range(2 * CHUNKS):
        dt = jnp.concatenate([wa_ref[half].reshape(128, 512), wb_ref[half].reshape(128, 512)], axis=0)
        gpb = []
        for s in range(4 * half, 4 * half + 4):
            cols = slice(128 * s, 128 * s + 128)
            xw = x_ref[:, cols].astype(f32)
            z = z_ref[:, cols].astype(f32)
            gw = g_ref[:, cols].astype(f32)
            dsk = dskip_ref[:, cols]
            sz = logistic(z)
            act = z * sz
            inner = y3.reshape(T * 8 * CHUNKS, 128)[pl.ds(s, T, stride=8 * CHUNKS), :] + dsk * xw
            mix_ref[:, cols] = (act * inner).astype(jnp.bfloat16)
            gz_ref[:, cols] = (gw * inner * (sz + act * (1.0 - sz))).astype(jnp.bfloat16)
            gsn = gw * act
            gd = gd3.reshape(T * 8 * CHUNKS, 128)[pl.ds(s, T, stride=8 * CHUNKS), :]
            gpre = (gd * xw + gr3.reshape(T * 8 * CHUNKS, 128)[pl.ds(s, T, stride=8 * CHUNKS), :] * LN2) * sig_ref[:, cols]
            gcx_ref[:, cols] = gd * step_ref.reshape(T * 8 * CHUNKS, 128)[pl.ds(s, T, stride=8 * CHUNKS), :] + gsn * dsk
            par_ref[0:1, cols] = jnp.sum(gpre, axis=0, keepdims=True)
            par_ref[1:2, cols] = jnp.sum(gsn * xw, axis=0, keepdims=True)
            gpb.append(gpre.astype(jnp.bfloat16))
        gp = jnp.concatenate(gpb, axis=1)
        alow[...] += lax.dot_general(gp, dt, (((1,), (1,)), ((), ())), preferred_element_type=f32)
        gdt = jnp.dot(turned[...], gp, preferred_element_type=f32).astype(jnp.bfloat16)
        for h in range(2):
            gdt_ref[half, :, 16 * h:16 * h + 16, :] = gdt[128 * h:128 * h + 128].reshape(8, 16, 512)

    @pl.when(i == pl.num_programs(0) - 1)
    def _():
        glow_ref[...] = alow[...]

        def fold(t, _):
            both[t, 0:16, :] = jnp.sum(accb[t], axis=1)
            both[t, 16:32, :] = jnp.sum(accc[t], axis=1)
            return 0
        lax.fori_loop(0, T, fold, 0)
        for n in range(2 * N):
            gbc_ref[:, n:n + 1] = jnp.sum(both.reshape(T * 32, 128)[pl.ds(n, T, stride=32), :], axis=1, keepdims=True)

def main_scan(step3, drive3, gs3, sig, x_conv, z, g, dskip, a2, bc, ent, wg, low):
    E = x_conv.shape[1]
    C = E // (1024 * CHUNKS)
    f32 = jnp.float32
    nat = pl.BlockSpec((T, 1024 * CHUNKS), lambda i: (0, i))
    tri = pl.BlockSpec((T, 8 * CHUNKS, 128), lambda i: (0, i, 0))
    row = lambda count: pl.BlockSpec((count, 1024 * CHUNKS), lambda i: (0, i))
    once = lambda *shape: pl.BlockSpec(shape, lambda i: (0,) * len(shape), pipeline_mode=pl.Buffered(1))
    full = lambda *shape: pl.BlockSpec(shape, lambda i: (0,) * len(shape))
    rate = pl.BlockSpec((N, 8 * CHUNKS, 128), lambda i: (0, i, 0))
    S = jax.ShapeDtypeStruct
    return pl.pallas_call(
        main_scan_kernel, grid=(C,), name="main_scan",
        in_specs=[tri, tri, tri, nat, nat, nat, nat, row(1), rate, once(32, T, 128),
                  pl.BlockSpec((N, CHUNKS, 16, 128), lambda i: (0, i, 0, 0)),
                  pl.BlockSpec((2 * CHUNKS, 8, 16, 512), lambda i: (i, 0, 3, 0)),
                  pl.BlockSpec((2 * CHUNKS, 8, 16, 512), lambda i: (i, 0, 4, 0)), once(T, 256)],
        out_specs=[nat, nat, nat, pl.BlockSpec((2 * CHUNKS, 8, 32, 512), lambda i: (i, 0, 0, 0)),
                   row(8), rate, full(T, 256), full(T, 32)],
        out_shape=[S((T, E), jnp.bfloat16), S((T, E), jnp.bfloat16), S((T, E), f32), S((E // 512, 8, 32, 512), jnp.bfloat16),
                   S((8, E), f32), S((N, E // 128, 128), f32), S((T, 256), f32), S((T, 32), f32)],
        scratch_shapes=[pltpu.VMEM((N, CHUNKS, 16, 128), f32), pltpu.VMEM((T, N, 8 * CHUNKS, 128), f32)]
        + [pltpu.VMEM((T, 8 * CHUNKS, 128), f32)] * 3 + [pltpu.VMEM((T, N, 8, 128), f32)] * 2 + [pltpu.VMEM((T, 256), f32), pltpu.VMEM((256, T), jnp.bfloat16),
           pltpu.VMEM((T, 32, 128), f32)],
        compiler_params=pltpu.CompilerParams(vmem_limit_bytes=VMEM_LIMIT),
    )(step3, drive3, gs3, sig, x_conv, z, g, dskip, a2, bc, ent, wg, wg, low)


MESH = pl.DeviceIdType.MESH
ORDERS = (("x", "y", "z"), ("y", "z", "x"), ("z", "x", "y"))
GATHER_ROWS = ((0, 32), (32, 32), (64, 16))
ROWS = ((0, 32), (32, 16), (48, 32))
DIMS = {"z": 0, "x": 1, "y": 2}


def place():
    d, j = lax.axis_index("dp"), lax.axis_index("seq")
    return d, j, {"z": lax.div(j, 4), "x": lax.rem(j, 4), "y": lax.div(d, 2)}, lax.rem(d, 2)


def peer(pos, core, axis, hop):
    at = dict(pos)
    at[axis] = lax.rem(at[axis] + hop + 4, 4)
    return (at["y"] * 2 + core, at["z"] * 4 + at["x"])


OTHERS = [(a, b) for a in range(4) for b in range(4) if (a, b) != (0, 0)]


def peer2(pos, core, axes, hops):
    at = {a: lax.rem(pos[a] + h, 4) for a, h in zip(axes, hops)}
    at = {**pos, **at}
    return (at["y"] * 2 + core, at["z"] * 4 + at["x"])


def planes(pos, core):
    near = [peer(pos, core, axis, hop) for axis in "xyz" for hop in (1, 2, 3)]
    return near + [peer2(pos, core, axes, (a, b)) for axes in ("xy", "yz", "zx") for a, b in OTHERS if a and b]


def greet(devices):
    barrier = pltpu.get_barrier_semaphore()
    for device in devices:
        pl.semaphore_signal(barrier, inc=1, device_id=device, device_id_type=MESH)
    pl.semaphore_wait(barrier, len(devices))


def remote(src, dst, send_sem, recv_sem, device):
    return pltpu.make_async_remote_copy(
        src_ref=src, dst_ref=dst, send_sem=send_sem, recv_sem=recv_sem, device_id=device, device_id_type=MESH
    )


def slab(ref, fixed, tail):
    index = [slice(None)] * 3
    for axis, value in fixed.items():
        index[DIMS[axis]] = value
    return ref.at[tuple(index) + tail]


def gather_kernel(parts, with_tail, *refs):
    if with_tail:
        shard, tail_ref, out, halo, local_sem, ssem, rsem, fsend, frecv, csend, crecv, hsend, hrecv = refs
    else:
        shard, out, local_sem, ssem, rsem, fsend, frecv, csend, crecv = refs
    d, j, pos, core = place()
    sibling = (pos["y"] * 2 + 1 - core, j)
    following, previous = (d, lax.rem(j + 1, 16)), (d, lax.rem(j + 15, 16))
    greet(planes(pos, core) + [sibling] + ([previous] if with_tail else []))
    sent = []

    def go(copy):
        copy.start()
        sent.append(copy)

    own = out.at[pos["z"], pos["x"], pos["y"], core]
    local = pltpu.make_async_copy(shard, own, local_sem)
    local.start()
    half = out.shape[-1] // 2
    columns = (pl.ds(0, half), pl.ds(half, half))
    whole = slice(None)
    hops = (0, -1, 1, 2)

    def step(p, slot, axis, fixed):
        row, count = parts[p][1]
        rows = pl.ds(row, count)
        right, left = peer(pos, core, axis, 1), peer(pos, core, axis, -1)

        def at(hop, cols=whole, which=core):
            return slab(out, {**fixed, axis: lax.rem(pos[axis] + hop + 4, 4)}, (which, rows, cols))

        def ring(hop, cols, which, device):
            return remote(at(hop, cols), at(hop, cols), ssem.at[p, slot, which], rsem.at[p, slot, which], device)

        def send(which):
            hop, cols, device = ((0, whole, right), (0, whole, left), (-1, columns[0], right), (1, columns[1], left))[which]
            go(ring(hop, cols, which, device))

        def landed(which):
            hop, cols, device = ((-1, whole, right), (1, whole, left), (2, columns[0], right), (2, columns[1], left))[which]
            ring(hop, cols, which, device).wait_recv()

        def across(which):
            there = at(hops[which])
            go(remote(there, there, csend.at[p, slot, which], crecv.at[p, slot, which], sibling))

        def crossed(which):
            there = at(hops[which], whole, 1 - core)
            remote(there, there, csend.at[p, slot, which], crecv.at[p, slot, which], sibling).wait_recv()

        return send, landed, across, crossed

    count = range(len(parts))

    def spot(axis, hop):
        return lax.rem(pos[axis] + hop + 4, 4)

    def direct(p, k):
        (one, two, three), (row, rows) = parts[p]
        device = peer2(pos, core, (one, two), OTHERS[k])
        return remote(shard.at[pl.ds(row, rows), :], own.at[pl.ds(row, rows), :], fsend.at[p, k], frecv.at[p, k], device)

    def arrived(p, k):
        (one, two, three), (row, rows) = parts[p]
        a, b = OTHERS[k]
        there = slab(out, {one: spot(one, -a), two: spot(two, -b), three: pos[three]}, (core, pl.ds(row, rows), whole))
        remote(there, there, fsend.at[p, k], frecv.at[p, k], peer2(pos, core, (one, two), OTHERS[k])).wait_recv()

    third = []
    for p in count:
        one, two, three = parts[p][0]
        third.append([step(p, i, three, {two: spot(two, hops[i])}) for i in range(4)])
    turn = [[k for k, (a, b) in enumerate(OTHERS) if (-b) % 4 == hops[i] % 4] for i in range(4)]
    for i in range(4):
        for k in turn[i]:
            for p in count:
                go(direct(p, k))
    if with_tail:
        tail_copy = remote(tail_ref, halo, hsend, hrecv, following)
        go(tail_copy)
    local.wait()
    for i in range(4):
        for p in count:
            for k in turn[i]:
                arrived(p, k)
            send, _, across, _ = third[p][i]
            send(0)
            send(1)
            across(0)
    for i in range(4):
        for which in (0, 1):
            for p in count:
                send, landed, across, _ = third[p][i]
                landed(which)
                send(2 + which)
                across(1 + which)
    for i in range(4):
        for p in count:
            _, landed, across, _ = third[p][i]
            landed(2)
            landed(3)
            across(3)
    for i in range(4):
        for p in count:
            for which in range(4):
                third[p][i][3](which)
    if with_tail:
        tail_copy.wait_recv()
    for copy in sent:
        copy.wait_send()


def gather(shard, tail, parts, collective_id):
    rows, columns = shard.shape
    count = len(parts)
    anyspace = pl.BlockSpec(memory_space=pl.ANY)
    dma = pltpu.SemaphoreType.DMA
    out_shape = [jax.ShapeDtypeStruct((4, 4, 4, 2, rows, columns), shard.dtype)]
    sems = [dma, dma((count, 4, 4)), dma((count, 4, 4)), dma((count, 15)), dma((count, 15)), dma((count, 4, 4)), dma((count, 4, 4))]
    operands = [shard]
    if tail is not None:
        out_shape.append(jax.ShapeDtypeStruct(tail.shape, tail.dtype))
        sems += [dma, dma]
        operands.append(tail)
    return pl.pallas_call(
        functools.partial(gather_kernel, parts, tail is not None),
        name="gather_shards",
        out_shape=out_shape,
        in_specs=[anyspace] * len(operands),
        out_specs=[anyspace] * len(out_shape),
        scratch_shapes=sems,
        compiler_params=pltpu.CompilerParams(collective_id=collective_id, has_side_effects=True, vmem_limit_bytes=VMEM_LIMIT),
    )(*operands)


def reduce_kernel(xpart, dpart, edge, out, all_params, halo, sums, cross, *scratch):
    buffers, plane, scratch = scratch[:48], scratch[48:51], scratch[51:]
    own_sem, csend, crecv, ssem, rsem, fsend, frecv, psend, precv, qsend, qrecv, hsend, hrecv = scratch
    d, j, pos, core = place()
    sibling = (pos["y"] * 2 + 1 - core, j)
    following, previous = (d, lax.rem(j + 1, 16)), (d, lax.rem(j + 15, 16))
    greet(planes(pos, core) + [sibling, following])
    sent = []
    hops = (2, 1, -1, 0)
    half = 256
    whole = slice(None)
    columns = (slice(0, half), slice(half, 2 * half))

    def go(copy):
        copy.start()
        sent.append(copy)

    def spot(axis, hop):
        return lax.rem(pos[axis] + hop + 4, 4)

    def mine(p, i, which):
        row, count = ROWS[p]
        fixed = {ORDERS[p][1]: spot(ORDERS[p][1], hops[i])}
        return slab(xpart if p < 2 else dpart, fixed, (which, pl.ds(row if p < 2 else 0, count), whole))

    def beside(ref, p, i):
        row, count = ROWS[p]
        return slab(ref, {ORDERS[p][1]: spot(ORDERS[p][1], hops[i])}, (pl.ds(row, count), whole))

    def across(p, i):
        return remote(mine(p, i, 1 - core), beside(cross, p, i), csend.at[p, i], crecv.at[p, i], sibling)

    def own(p, i):
        return pltpu.make_async_copy(mine(p, i, core), beside(sums, p, i), own_sem.at[p, i])

    for i in range(4):
        for p in range(3):
            go(across(p, i))
            own(p, i).start()
    edge_copy = remote(edge, halo, hsend, hrecv, previous)
    go(edge_copy)

    def index_of(fixed, free, values):
        index = [None] * 3
        for a, v in {**fixed, **dict(zip(free, values))}.items():
            index[DIMS[a]] = v
        return tuple(index)

    def add_core(p, i):
        row, count = ROWS[p]
        rows = pl.ds(row, count)
        middle = ORDERS[p][1]
        free = [a for a in "zxy" if a != middle]
        own(p, i).wait()
        across(p, i).wait_recv()

        def one(k, _):
            at = index_of({middle: spot(middle, hops[i])}, free, (lax.div(k, 4), lax.rem(k, 4))) + (rows, whole)
            sums[at] = (sums[at].astype(jnp.float32) + cross[at].astype(jnp.float32)).astype(jnp.bfloat16)
            return 0

        lax.fori_loop(0, 16, one, 0)

    def step(p, slot, axis, fixed, free):
        row, count = ROWS[p]
        rows = pl.ds(row, count)
        right, left = peer(pos, core, axis, 1), peer(pos, core, axis, -1)
        bufs = buffers[(p * 4 + slot) * 4:(p * 4 + slot) * 4 + 4]

        def copy(which):
            hop, cols, device = ((2, columns[0], right), (2, columns[1], left), (1, whole, right), (-1, whole, left))[which]
            source = slab(sums, {**fixed, axis: spot(axis, hop)}, (rows, cols))
            return remote(source, bufs[which], ssem.at[p, slot, which], rsem.at[p, slot, which], device)

        def add(hop, cols, terms):
            def one(k, _):
                at = index_of({**fixed, axis: spot(axis, hop)}, free, (k,)) + (rows, cols)
                total = sums[at].astype(jnp.float32)
                for term in terms:
                    total = total + term[k].astype(jnp.float32)
                sums[at] = total.astype(jnp.bfloat16)
                return 0

            lax.fori_loop(0, 4, one, 0)

        def begin():
            go(copy(0))
            go(copy(1))

        def relay(which):
            copy(which).wait_recv()
            add((1, -1)[which], columns[which], bufs[which:which + 1])
            go(copy(2 + which))

        def finish():
            copy(2).wait_recv()
            copy(3).wait_recv()
            add(0, whole, bufs[2:])

        return begin, relay, finish

    def direct(p, k):
        one, two, three = ORDERS[p]
        a, b = OTHERS[k]
        row, count = ROWS[p]
        source = slab(sums, {one: spot(one, a), two: spot(two, b), three: pos[three]}, (pl.ds(row, count), whole))
        return remote(source, plane[p].at[k], fsend.at[p, k], frecv.at[p, k], peer2(pos, core, (one, two), (a, b)))

    parts = range(3)
    turn = [[k for k, (a, b) in enumerate(OTHERS) if b % 4 == hops[i] % 4] for i in range(4)]
    outer = []
    for p in parts:
        one, two, three = ORDERS[p]
        outer.append([step(p, i, three, {two: spot(two, hops[i])}, [one]) for i in range(4)])
    def relays(p, i):
        for which in (0, 1):
            outer[p][i][1](which)

    def finish(p):
        for i in range(4):
            outer[p][i][2]()
            for k in turn[i]:
                go(direct(p, k))

    def total(p):
        row, count = ROWS[p]
        rows = pl.ds(row, count)
        for k in range(15):
            direct(p, k).wait_recv()
        out[rows, :] = sums[pos["z"], pos["x"], pos["y"], rows, :].astype(jnp.float32)

        def one_more(k, _):
            out[rows, :] += plane[p][k].astype(jnp.float32)
            return 0

        lax.fori_loop(0, 15, one_more, 0)

    def place_of(hops):
        return all_params.at[lax.rem(pos["z"] + 4 - hops[0], 4), lax.rem(pos["x"] + 4 - hops[1], 4), pos["y"], core]

    def flat(k):
        return remote(place_of((0, 0)), place_of((0, 0)), psend.at[k], precv.at[k], peer2(pos, core, "zx", OTHERS[k]))

    def upright(hop):
        ours = all_params.at[:, :, pos["y"], core]
        return remote(ours, ours, qsend.at[hop], qrecv.at[hop], peer(pos, core, "y", hop))

    for i in range(4):
        for p in (1, 0, 2):
            add_core(p, i)
            outer[p][i][0]()
    for i in range(2):
        relays(1, 2 * i)
        for p in (0, 2):
            relays(p, i)
        relays(1, 2 * i + 1)
    finish(1)
    for p in (0, 2):
        relays(p, 2)
    total(1)

    rowsum = jnp.concatenate(
        [out[36 + q:37 + q, 128 * s:128 * s + 128] for q in range(3) for s in range(4)] + [jnp.zeros((4, 128), jnp.float32)], axis=0
    )
    all_params[pos["z"], pos["x"], pos["y"], core] = rowsum.astype(jnp.bfloat16)
    for k in range(15):
        go(flat(k))
    for p in (0, 2):
        relays(p, 3)
    for p in (0, 2):
        finish(p)
    for k in range(15):
        there = place_of(OTHERS[k])
        remote(there, there, psend.at[k], precv.at[k], peer2(pos, core, "zx", OTHERS[k])).wait_recv()
    for hop in (1, 2, 3):
        go(upright(hop))
    total(0)
    for hop in (1, 2, 3):
        there = all_params.at[:, :, lax.rem(pos["y"] + 4 - hop, 4), core]
        remote(there, there, qsend.at[hop], qrecv.at[hop], peer(pos, core, "y", hop)).wait_recv()
    ours, theirs = all_params.at[:, :, :, core], all_params.at[:, :, :, 1 - core]
    go(remote(ours, ours, qsend.at[0], qrecv.at[0], sibling))
    total(2)
    remote(theirs, theirs, qsend.at[0], qrecv.at[0], sibling).wait_recv()
    edge_copy.wait_recv()
    for copy in sent:
        copy.wait_send()


def reduce_all(xpart, dpart, edge):
    vmem = pl.BlockSpec(memory_space=pltpu.VMEM)
    anyspace = pl.BlockSpec(memory_space=pl.ANY)
    dma = pltpu.SemaphoreType.DMA
    bf16 = jnp.bfloat16
    buffers = []
    for row, count in ROWS:
        buffers += ([pltpu.VMEM((4, count, 256), bf16)] * 2 + [pltpu.VMEM((4, count, 512), bf16)] * 2) * 4
    buffers += [pltpu.VMEM((15, count, 512), bf16) for row, count in ROWS]
    return pl.pallas_call(
        reduce_kernel,
        name="reduce_shards",
        out_shape=[
            jax.ShapeDtypeStruct((80, 512), jnp.float32),
            jax.ShapeDtypeStruct((4, 4, 4, 2, 16, 128), bf16),
            jax.ShapeDtypeStruct(edge.shape, edge.dtype),
        ],
        in_specs=[anyspace] * 3,
        out_specs=[vmem, vmem, anyspace],
        scratch_shapes=[pltpu.VMEM((4, 4, 4, 80, 512), bf16)] * 2 + buffers + [
            dma((3, 4)), dma((3, 4)), dma((3, 4)), dma((3, 4, 4)), dma((3, 4, 4)), dma((3, 15)), dma((3, 15)),
            dma((15,)), dma((15,)), dma((4,)), dma((4,)), dma, dma,
        ],
        compiler_params=pltpu.CompilerParams(
            collective_id=2, has_side_effects=True, vmem_limit_bytes=VMEM_LIMIT
        ),
    )(xpart, dpart, edge)


def spread(rows, columns, row_is_plain):
    index = lax.broadcasted_iota(jnp.int32, (rows, columns), 0 if row_is_plain else 1)
    padded = lax.broadcasted_iota(jnp.int32, (rows, columns), 1 if row_is_plain else 0)
    low = 32 * lax.div(lax.rem(index, 128), 16) + 16 * lax.div(index, 128) + lax.rem(index, 16)
    plain = jnp.where(index < 256, low, index)
    device = lax.div(padded, 48)
    inside = padded - 48 * device
    return jnp.where((inside < 36) & (36 * device + inside == plain), 1.0, 0.0).astype(jnp.bfloat16)


HALO = pl.BlockSpec((3, 8, 128), lambda i: (0, i, 0))


def convolve(x_ref, halo_ref, cw_ref, cb_ref, ext):
    first = lax.axis_index("seq") == 0
    for r in range(3):
        for s in range(8):
            ext[5 + r:6 + r, 128 * s:128 * s + 128] = jnp.where(first, 0.0, halo_ref[r, s:s + 1, :])
    ext[8:T + 8, :] = x_ref[...].astype(jnp.float32)

    def part(cols):
        pre = cb_ref[:, cols] + cw_ref[0:1, cols] * ext[5:5 + T, cols]
        for k in range(1, 4):
            pre = pre + cw_ref[k:k + 1, cols] * ext[5 + k:5 + k + T, cols]
        gate = logistic(pre)
        act = pre * gate
        return act.astype(jnp.bfloat16), gate + act * (1.0 - gate)

    return part


def conv_kernel(x_ref, halo_ref, cw_ref, cb_ref, w_ref, xc_ref, low_ref, bc_ref, ext, acc):
    i = pl.program_id(0)

    @pl.when(i == 0)
    def _():
        acc[...] = jnp.zeros(acc.shape, jnp.float32)

    part = convolve(x_ref, halo_ref, cw_ref, cb_ref, ext)
    for half in range(2):
        cols = slice(512 * half, 512 * half + 512)
        xc, _ = part(cols)
        xc_ref[:, cols] = xc
        acc[...] += lax.dot_general(
            xc, w_ref[half].reshape(384, 512), (((1,), (1,)), ((), ())), preferred_element_type=jnp.float32
        )

    @pl.when(i == pl.num_programs(0) - 1)
    def _():
        low_ref[...] = jnp.dot(
            acc[...].astype(jnp.bfloat16), spread(384, 256, False), preferred_element_type=jnp.float32
        ).astype(jnp.bfloat16)
        for n in range(32):
            bc_ref[n] = jnp.broadcast_to(acc[:, 340 + n:341 + n], (T, 128))


def conv_project(x, halo, cw, cb, wg):
    E = x.shape[1]
    nat, row, full = tile_specs(1024)
    S = jax.ShapeDtypeStruct
    return pl.pallas_call(
        conv_kernel, grid=(E // 1024,), name="conv_project",
        in_specs=[nat, HALO, row(4), row(1), pl.BlockSpec((2, 8, 48, 512), lambda i: (i, 0, 0, 0))],
        out_specs=[nat, full(T, 256), full(32, T, 128)],
        out_shape=[S((T, E), jnp.bfloat16), S((T, 256), jnp.bfloat16), S((32, T, 128), jnp.float32)],
        scratch_shapes=[pltpu.VMEM((T + 8, 1024), jnp.float32), pltpu.VMEM((T, 384), jnp.float32)],
        compiler_params=pltpu.CompilerParams(vmem_limit_bytes=VMEM_LIMIT),
    )(x, halo, cw, cb, wg)


def grads_kernel(glow_ref, gbc_ref, gcx_ref, x_ref, halo_ref, cw_ref, cb_ref, w_ref, par_ref, ga_ref,
                 gx_ref, head_ref, tail_ref, part_ref, gproj, turned, ext, wide, gext):
    i = pl.program_id(0)
    f32 = jnp.float32

    @pl.when(i == 0)
    def _():
        plain = jnp.concatenate([glow_ref[...], gbc_ref[...]], axis=1).astype(jnp.bfloat16)
        gproj[...] = jnp.dot(plain, spread(288, 384, True), preferred_element_type=f32).astype(jnp.bfloat16)
        turned[...] = gproj[...].T
        gext[T:T + 8, :] = jnp.zeros((8, gext.shape[1]), f32)

    part = convolve(x_ref, halo_ref, cw_ref, cb_ref, ext)
    for half in range(2):
        cols = slice(512 * half, 512 * half + 512)
        xc, slope = part(cols)
        weights = w_ref[half].reshape(384, 512)
        g_conv = (gcx_ref[:, cols] + jnp.dot(gproj[...], weights, preferred_element_type=f32)) * slope
        gext[0:T, cols] = g_conv
        wide[...] = jnp.dot(turned[...], xc, preferred_element_type=f32)

        def put(r, value):
            wide[48 * (r // 3) + 36 + r % 3:48 * (r // 3) + 37 + r % 3, :] = value

        for k in range(4):
            put(k, jnp.sum(g_conv * ext[5 + k:5 + k + T, cols], axis=0, keepdims=True))
        put(4, jnp.sum(g_conv, axis=0, keepdims=True))
        put(5, par_ref[0:1, cols])
        put(6, par_ref[1:2, cols])
        for n in range(N):
            put(7 + n, jnp.concatenate([ga_ref[n, 4 * half + s:4 * half + s + 1, :] for s in range(4)], axis=1))
        part_ref[half] = wide[...].reshape(8, 48, 512).astype(jnp.bfloat16)
    total = cw_ref[0:1, :] * gext[3:3 + T, :]
    for k in range(1, 4):
        total = total + cw_ref[k:k + 1, :] * gext[3 - k:3 - k + T, :]
    gx_ref[...] = total.astype(jnp.bfloat16)
    for r in range(3):
        for s in range(8):
            head_ref[r, s:s + 1, :] = gext[r:r + 1, 128 * s:128 * s + 128]
    tail_ref[...] = gext[T - 16:T, :]


def weight_grads(glow, gbc, gcx, x, halo, cw, cb, wg, par, ga):
    E = x.shape[1]
    nat, row, full = tile_specs(1024)
    S = jax.ShapeDtypeStruct
    f32 = jnp.float32
    block = pl.BlockSpec((2, 8, 48, 512), lambda i: (i, 0, 0, 0))
    return pl.pallas_call(
        grads_kernel, grid=(E // 1024,), name="weight_grads",
        in_specs=[full(T, 256), full(T, 32), nat, nat, HALO, row(4), row(1), block, row(8),
                  pl.BlockSpec((N, 8, 128), lambda i: (0, i, 0))],
        out_specs=[nat, HALO, row(16), block],
        out_shape=[S((T, E), jnp.bfloat16), S((3, E // 128, 128), f32), S((16, E), f32), S((E // 512, 8, 48, 512), jnp.bfloat16)],
        scratch_shapes=[pltpu.VMEM((T, 384), jnp.bfloat16), pltpu.VMEM((384, T), jnp.bfloat16), pltpu.VMEM((T + 8, 1024), f32),
                        pltpu.VMEM((384, 512), f32),
                        pltpu.VMEM((T + 8, 1024), f32)],
        compiler_params=pltpu.CompilerParams(vmem_limit_bytes=VMEM_LIMIT),
    )(glow, gbc, gcx, x, halo, cw, cb, wg, par, ga)


def last_rows_kernel(gx_ref, tail_ref, edge_ref, cw_ref, out_ref, ext):
    ext[0:16, :] = tail_ref[...]
    last = lax.axis_index("seq") == 15
    for r in range(3):
        for s in range(edge_ref.shape[1]):
            ext[16 + r:17 + r, 128 * s:128 * s + 128] = jnp.where(last, 0.0, edge_ref[r, s:s + 1, :])
    total = cw_ref[0:1, :] * ext[3:19, :]
    for k in range(1, 4):
        total = total + cw_ref[k:k + 1, :] * ext[3 - k:19 - k, :]
    out_ref[...] = total.astype(jnp.bfloat16)


def last_rows(gx, tail, edge, cw):
    E = gx.shape[1]
    full = lambda *shape: pl.BlockSpec(shape, lambda i: (0,) * len(shape))
    block = pl.BlockSpec((16, E), lambda i: (T // 16 - 1, 0))
    return pl.pallas_call(
        last_rows_kernel, grid=(1,), name="last_rows",
        in_specs=[block, full(16, E), full(3, E // 128, 128), full(4, E)], out_specs=block,
        out_shape=jax.ShapeDtypeStruct((T, E), jnp.bfloat16),
        scratch_shapes=[pltpu.VMEM((24, E), jnp.float32)],
        input_output_aliases={0: 0},
        compiler_params=pltpu.CompilerParams(vmem_limit_bytes=VMEM_LIMIT),
    )(gx, tail, edge, cw)


def local(x_branch, z_branch, out_grad, x_weight, dt_weight, conv_weight, conv_bias, dt_bias, a_log, d_skip):
    x, z, g = x_branch[0], z_branch[0], out_grad[0]
    E = x.shape[1]
    shard = jnp.concatenate([x_weight.T, jnp.zeros((12, 512), jnp.bfloat16), dt_weight], axis=0)
    gathered, halo = gather(shard, x[T - 3:].astype(jnp.float32).reshape(3, E // 128, 128), tuple(zip(ORDERS, GATHER_ROWS)), 0)
    wg = gathered.reshape(16, 8, 80, 512)
    a2_wide = -jnp.exp(a_log) * LOG2E
    a2 = a2_wide.reshape(N, E // 128, 128)
    bias = conv_bias[None]
    xc, low, bc = conv_project(x, halo, conv_weight, bias, wg)
    step3, drive3, gs3, sig, carried = local_scan(low, wg, xc, z, g, dt_bias[None], a2, bc)
    mixer_out, grad_z, gcx, gdt, par, ga, glow, gbc = main_scan(
        step3, drive3, gs3, sig, xc, z, g, d_skip[None], a2, bc, carried, wg, low
    )
    gx, head, tail, part = weight_grads(glow, gbc, gcx, x, halo, conv_weight, bias, wg, par, ga)
    reduced, params, edge = reduce_all(part.reshape(4, 4, 4, 2, 48, 512), gdt.reshape(4, 4, 4, 2, 32, 512), head)
    grad_x = last_rows(gx, tail, edge, conv_weight)
    params = params.reshape(16, 8, 16, 128)[:, :, :12].reshape(16, 8, 3, 4, 128)
    params = params.transpose(1, 2, 0, 3, 4).reshape(24, E).astype(jnp.float32)
    return (
        mixer_out[None], grad_x[None], grad_z[None], reduced[:36].T, reduced[48:80],
        params[0:4], params[4], params[5], params[7:23], params[6],
    )


def solution(mesh):
    tokens, weights, whole = P("dp", "seq", None), P("seq", "dp"), P()
    in_specs = (tokens,) * 3 + (weights, P("dp", "seq")) + (whole,) * 5
    out_specs = (tokens,) * 3 + (weights, P("dp", "seq")) + (whole,) * 5
    return jax.shard_map(local, mesh=mesh, in_specs=in_specs, out_specs=out_specs, check_vma=False)
```

```python
import functools

import jax
import jax.numpy as jnp
from jax import lax
from jax.experimental import pallas as pl
from jax.experimental.pallas import tpu as pltpu
from jax.sharding import PartitionSpec as P

T = 128
N = 16
LN2 = 0.6931471805599453
LOG2E = 1.4426950408889634
VMEM_LIMIT = 62 * 2**20
LOCAL_GROUP, LOCAL_UNROLL = 4, 16
SHIPMENTS = ((0, 4), (4, 3), (7, 1))
CHUNKS = 1
FWD_GROUP, FWD_UNROLL = 16, 16
BWD_GROUP, BWD_UNROLL = 16, 16


def logistic(values):
    return 0.5 * jnp.tanh(0.5 * values) + 0.5


def tile_specs(width):
    nat = pl.BlockSpec((T, width), lambda i: (0, i))
    row = lambda count: pl.BlockSpec((count, width), lambda i: (0, i))
    full = lambda *shape: pl.BlockSpec(shape, lambda i: (0,) * len(shape))
    return nat, row, full


def local_scan_kernel(low_ref, wa_ref, wb_ref, x_ref, z_ref, g_ref, bias_ref, a2_ref, bc_ref, rates_ref,
                      step_ref, drive_ref, gs_ref, sig_ref, carried, ends_all, got, back,
                      ssem, rsem, bsend, brecv, own_sem):
    i = pl.program_id(0)
    d, j, _, _ = place()
    others = [lax.rem(j + k, 16) for k in range(1, 16)]

    @pl.when(i == 0)
    def _():
        barrier = pltpu.get_barrier_semaphore()
        for k in others:
            pl.semaphore_signal(barrier, inc=1, device_id=(d, k), device_id_type=MESH)

    low = low_ref[...]
    rows = [ref.reshape(T * 8, 128) for ref in (step_ref, drive_ref, gs_ref)]
    for half in range(2):
        dt = jnp.concatenate([wa_ref[half].reshape(128, 512), wb_ref[half].reshape(128, 512)], axis=0)
        cols = pl.ds(512 * half, 512)
        rate = jnp.dot(low, dt, preferred_element_type=jnp.float32) + bias_ref[:, cols]
        step = jnp.maximum(rate, 0.0) + jnp.log1p(jnp.exp(-jnp.abs(rate)))
        sig_ref[:, cols] = jnp.exp(rate - step)
        z = z_ref[:, cols].astype(jnp.float32)
        gs = g_ref[:, cols].astype(jnp.float32) * (z * logistic(z))
        drive = step * x_ref[:, cols].astype(jnp.float32)
        for s in range(4):
            for ref, value in zip(rows, (step, drive, gs)):
                ref[pl.ds(4 * half + s, T, stride=8), :] = value[:, 128 * s:128 * s + 128]

    zero = jnp.zeros((8, 128), jnp.float32)
    one = jnp.ones((8, 128), jnp.float32)
    ends, lams = [], []
    for first in range(0, N, LOCAL_GROUP):
        group = range(first, first + LOCAL_GROUP)

        def body(k, carry):
            tot, ends, prods, lams = carry
            for unrolled in range(LOCAL_UNROLL):
                t = k * LOCAL_UNROLL + unrolled
                st, dr, gv = step_ref[t], drive_ref[t], gs_ref[t]
                new_ends, new_prods, new_lams = [], [], []
                for q, n in enumerate(group):
                    f = jnp.exp2(st * a2_ref[n])
                    new_ends.append(f * ends[q] + bc_ref[n, pl.ds(t, 1), :] * dr)
                    p = prods[q] * f
                    new_prods.append(p)
                    new_lams.append(lams[q] + p * (bc_ref[N + n, pl.ds(t, 1), :] * gv))
                tot, ends, prods, lams = tot + st, tuple(new_ends), tuple(new_prods), tuple(new_lams)
            return tot, ends, prods, lams

        many = LOCAL_GROUP
        tot, e, _, l = lax.fori_loop(0, T // LOCAL_UNROLL, body, (zero, (zero,) * many, (one,) * many, (zero,) * many))
        ends += e
        lams += l
    high = tot.astype(jnp.bfloat16)
    sums = jnp.concatenate([high.astype(jnp.float32), tot - high.astype(jnp.float32)], axis=0).astype(jnp.bfloat16)
    for n in range(N):
        ends_all[n, i, 0:16, :] = jnp.concatenate([ends[n], lams[n]], axis=0).astype(jnp.bfloat16)
        ends_all[n, i, 16:32, :] = sums

    def chunks(group):
        return pl.ds(SHIPMENTS[group][0], SHIPMENTS[group][1])

    def outgoing(group, to):
        return remote(ends_all.at[to, chunks(group)], got.at[j, chunks(group)], ssem.at[group, to], rsem.at[group, j], (d, to))

    def returned(group, to):
        return remote(back.at[to, chunks(group)], carried.at[j, chunks(group)], bsend.at[group, to], brecv.at[group, j], (d, to))

    def ship(group):
        for to in others:
            outgoing(group, to).start()
        first, count = SHIPMENTS[group]
        for k in range(first, first + count):
            got[j, k] = ends_all[j, k]

    def recur(group):
        for source in others:
            there = got.at[source, chunks(group)]
            remote(there, there, ssem.at[group, source], rsem.at[group, source], (d, source)).wait_recv()
        first, count = SHIPMENTS[group]
        for c in range(first, first + count):
            rates = rates_ref[j, 8 * c:8 * c + 8, :]
            blocks = [got[k, c].astype(jnp.float32) for k in range(16)]
            decays = [jnp.exp2(rates * (block[16:24] + block[24:32])) for block in blocks]
            enter, leave = [jnp.zeros((8, 128), jnp.float32)], [jnp.zeros((8, 128), jnp.float32)]
            for k in range(15):
                enter.append(decays[k] * enter[k] + blocks[k][0:8])
                leave.append(decays[15 - k] * leave[k] + blocks[15 - k][8:16])
            for k in range(16):
                back[k, c] = jnp.concatenate([enter[k], leave[15 - k]], axis=0).astype(jnp.bfloat16)
        for to in others:
            returned(group, to).start()
        pltpu.make_async_copy(back.at[j, chunks(group)], carried.at[j, chunks(group)], own_sem.at[group]).start()

    @pl.when(i == 3)
    def _():
        pl.semaphore_wait(pltpu.get_barrier_semaphore(), 15)
        ship(0)

    @pl.when(i == 5)
    def _():
        recur(0)

    @pl.when(i == 6)
    def _():
        ship(1)

    @pl.when(i == 7)
    def _():
        ship(2)
        recur(1)
        recur(2)
        for group in range(3):
            pltpu.make_async_copy(back.at[j, chunks(group)], carried.at[j, chunks(group)], own_sem.at[group]).wait()
            for k in others:
                there = carried.at[k, chunks(group)]
                remote(there, there, bsend.at[group, k], brecv.at[group, k], (d, k)).wait_recv()
                outgoing(group, k).wait_send()
                returned(group, k).wait_send()


def local_scan(low, wg, x_conv, z, g, bias, a2, bc):
    E = x_conv.shape[1]
    C = E // 1024
    f32 = jnp.float32
    nat, row, full = tile_specs(1024)
    tri = pl.BlockSpec((T, 8, 128), lambda i: (0, i, 0))
    return pl.pallas_call(
        local_scan_kernel, grid=(C,), name="local_scan",
        in_specs=[full(T, 256), pl.BlockSpec((2, 8, 16, 512), lambda i: (i, 0, 3, 0)),
                  pl.BlockSpec((2, 8, 16, 512), lambda i: (i, 0, 4, 0)), nat, nat, nat,
                  row(1), pl.BlockSpec((N, 8, 128), lambda i: (0, i, 0)), full(32, T, 128), full(N, E // 128, 128)],
        out_specs=[tri, tri, tri, nat, pl.BlockSpec(memory_space=pl.ANY)],
        out_shape=[jax.ShapeDtypeStruct((T, E // 128, 128), f32)] * 3 + [
            jax.ShapeDtypeStruct((T, E), f32), jax.ShapeDtypeStruct((16, C, 16, 128), jnp.bfloat16)],
        scratch_shapes=[pltpu.VMEM((16, C, 32, 128), jnp.bfloat16)] * 2 + [pltpu.VMEM((16, C, 16, 128), jnp.bfloat16)]
        + [pltpu.SemaphoreType.DMA((3, 16))] * 4 + [pltpu.SemaphoreType.DMA((3,))],
        compiler_params=pltpu.CompilerParams(collective_id=1, has_side_effects=True, vmem_limit_bytes=VMEM_LIMIT),
    )(low, wg, wg, x_conv, z, g, bias, a2, bc, a2)


def main_scan_kernel(step_ref, drive_ref, gs_ref, sig_ref, x_ref, z_ref, g_ref, dskip_ref, a2_ref, bc_ref, ent_ref, wa_ref, wb_ref, low_ref,
              mix_ref, gz_ref, gcx_ref, gdt_ref, par_ref, ga_ref, glow_ref, gbc_ref,
              es, us, y3, gd3, gr3, accb, accc, alow, turned, both):
    i = pl.program_id(0)
    f32 = jnp.float32
    span = [slice(8 * q, 8 * q + 8) for q in range(CHUNKS)]

    @pl.when(i == 0)
    def _():
        accb[...] = jnp.zeros(accb.shape, f32)
        accc[...] = jnp.zeros(accc.shape, f32)
        alow[...] = jnp.zeros(alow.shape, f32)
        turned[...] = low_ref[...].T

    es[...] = ent_ref[...].astype(f32)

    def state(base, n, q):
        return es[n, q, base:base + 8, :]

    def add(total, term):
        return term if total is None else total + term

    def inputs(t):
        return tuple([ref[t, rows] for rows in span] for ref in (step_ref, drive_ref, gs_ref))

    zero = jnp.zeros((8, 128), f32)
    for first in range(0, N, FWD_GROUP):
        group = range(first, first + FWD_GROUP)

        def forward(k, hs):
            for unrolled in range(FWD_UNROLL):
                t = k * FWD_UNROLL + unrolled
                st, dr, gv = inputs(t)
                ys = [None if first == 0 else y3[t, rows] for rows in span]
                new = []
                for p, n in enumerate(group):
                    b, c = bc_ref[n, pl.ds(t, 1), :], bc_ref[N + n, pl.ds(t, 1), :]
                    total = accc[t, n]
                    for q in range(CHUNKS):
                        u = jnp.exp2(st[q] * a2_ref[n, span[q]]) * hs[p * CHUNKS + q]
                        us[t, n, span[q]] = u
                        h = u + b * dr[q]
                        new.append(h)
                        ys[q] = add(ys[q], c * h)
                        total = total + h * gv[q]
                    accc[t, n] = total
                for q in range(CHUNKS):
                    y3[t, span[q]] = ys[q]
                hs = tuple(new)
            return hs

        lax.fori_loop(0, T // FWD_UNROLL, forward, tuple(state(0, n, q) for n in group for q in range(CHUNKS)))

    for first in range(0, N, BWD_GROUP):
        group = range(first, first + BWD_GROUP)

        def backward(k, carry):
            adj, ra = carry
            for unrolled in range(BWD_UNROLL):
                t = T - 1 - (k * BWD_UNROLL + unrolled)
                st, dr, gv = inputs(t)
                gd = [None if first == 0 else gd3[t, rows] for rows in span]
                gr = [None if first == 0 else gr3[t, rows] for rows in span]
                na, nr = [], []
                for p, n in enumerate(group):
                    b, c = bc_ref[n, pl.ds(t, 1), :], bc_ref[N + n, pl.ds(t, 1), :]
                    total = accb[t, n]
                    for q in range(CHUNKS):
                        rate = a2_ref[n, span[q]]
                        lam = c * gv[q] + adj[p * CHUNKS + q]
                        gd[q] = add(gd[q], lam * b)
                        total = total + lam * dr[q]
                        na.append(jnp.exp2(st[q] * rate) * lam)
                        m = lam * us[t, n, span[q]]
                        gr[q] = add(gr[q], m * rate)
                        nr.append(ra[p * CHUNKS + q] + m * st[q])
                    accb[t, n] = total
                for q in range(CHUNKS):
                    gd3[t, span[q]] = gd[q]
                    gr3[t, span[q]] = gr[q]
                adj, ra = tuple(na), tuple(nr)
            return adj, ra

        _, ra = lax.fori_loop(0, T // BWD_UNROLL, backward, (tuple(state(8, n, q) for n in group for q in range(CHUNKS)), (zero,) * (BWD_GROUP * CHUNKS)))
        for p, n in enumerate(group):
            for q in range(CHUNKS):
                ga_ref[n, span[q]] = ra[p * CHUNKS + q] * a2_ref[n, span[q]] * LN2

    for half in range(2 * CHUNKS):
        dt = jnp.concatenate([wa_ref[half].reshape(128, 512), wb_ref[half].reshape(128, 512)], axis=0)
        gpb = []
        for s in range(4 * half, 4 * half + 4):
            cols = slice(128 * s, 128 * s + 128)
            xw = x_ref[:, cols].astype(f32)
            z = z_ref[:, cols].astype(f32)
            gw = g_ref[:, cols].astype(f32)
            dsk = dskip_ref[:, cols]
            sz = logistic(z)
            act = z * sz
            inner = y3.reshape(T * 8 * CHUNKS, 128)[pl.ds(s, T, stride=8 * CHUNKS), :] + dsk * xw
            mix_ref[:, cols] = (act * inner).astype(jnp.bfloat16)
            gz_ref[:, cols] = (gw * inner * (sz + act * (1.0 - sz))).astype(jnp.bfloat16)
            gsn = gw * act
            gd = gd3.reshape(T * 8 * CHUNKS, 128)[pl.ds(s, T, stride=8 * CHUNKS), :]
            gpre = (gd * xw + gr3.reshape(T * 8 * CHUNKS, 128)[pl.ds(s, T, stride=8 * CHUNKS), :] * LN2) * sig_ref[:, cols]
            gcx_ref[:, cols] = gd * step_ref.reshape(T * 8 * CHUNKS, 128)[pl.ds(s, T, stride=8 * CHUNKS), :] + gsn * dsk
            par_ref[0:1, cols] = jnp.sum(gpre, axis=0, keepdims=True)
            par_ref[1:2, cols] = jnp.sum(gsn * xw, axis=0, keepdims=True)
            gpb.append(gpre.astype(jnp.bfloat16))
        gp = jnp.concatenate(gpb, axis=1)
        alow[...] += lax.dot_general(gp, dt, (((1,), (1,)), ((), ())), preferred_element_type=f32)
        gdt = jnp.dot(turned[...], gp, preferred_element_type=f32).astype(jnp.bfloat16)
        for h in range(2):
            gdt_ref[half, :, 16 * h:16 * h + 16, :] = gdt[128 * h:128 * h + 128].reshape(8, 16, 512)

    @pl.when(i == pl.num_programs(0) - 1)
    def _():
        glow_ref[...] = alow[...]

        def fold(t, _):
            both[t, 0:16, :] = jnp.sum(accb[t], axis=1)
            both[t, 16:32, :] = jnp.sum(accc[t], axis=1)
            return 0
        lax.fori_loop(0, T, fold, 0)
        for n in range(2 * N):
            gbc_ref[:, n:n + 1] = jnp.sum(both.reshape(T * 32, 128)[pl.ds(n, T, stride=32), :], axis=1, keepdims=True)

def main_scan(step3, drive3, gs3, sig, x_conv, z, g, dskip, a2, bc, ent, wg, low):
    E = x_conv.shape[1]
    C = E // (1024 * CHUNKS)
    f32 = jnp.float32
    nat = pl.BlockSpec((T, 1024 * CHUNKS), lambda i: (0, i))
    tri = pl.BlockSpec((T, 8 * CHUNKS, 128), lambda i: (0, i, 0))
    row = lambda count: pl.BlockSpec((count, 1024 * CHUNKS), lambda i: (0, i))
    once = lambda *shape: pl.BlockSpec(shape, lambda i: (0,) * len(shape), pipeline_mode=pl.Buffered(1))
    full = lambda *shape: pl.BlockSpec(shape, lambda i: (0,) * len(shape))
    rate = pl.BlockSpec((N, 8 * CHUNKS, 128), lambda i: (0, i, 0))
    S = jax.ShapeDtypeStruct
    return pl.pallas_call(
        main_scan_kernel, grid=(C,), name="main_scan",
        in_specs=[tri, tri, tri, nat, nat, nat, nat, row(1), rate, once(32, T, 128),
                  pl.BlockSpec((N, CHUNKS, 16, 128), lambda i: (0, i, 0, 0)),
                  pl.BlockSpec((2 * CHUNKS, 8, 16, 512), lambda i: (i, 0, 3, 0)),
                  pl.BlockSpec((2 * CHUNKS, 8, 16, 512), lambda i: (i, 0, 4, 0)), once(T, 256)],
        out_specs=[nat, nat, nat, pl.BlockSpec((2 * CHUNKS, 8, 32, 512), lambda i: (i, 0, 0, 0)),
                   row(8), rate, full(T, 256), full(T, 32)],
        out_shape=[S((T, E), jnp.bfloat16), S((T, E), jnp.bfloat16), S((T, E), f32), S((E // 512, 8, 32, 512), jnp.bfloat16),
                   S((8, E), f32), S((N, E // 128, 128), f32), S((T, 256), f32), S((T, 32), f32)],
        scratch_shapes=[pltpu.VMEM((N, CHUNKS, 16, 128), f32), pltpu.VMEM((T, N, 8 * CHUNKS, 128), f32)]
        + [pltpu.VMEM((T, 8 * CHUNKS, 128), f32)] * 3 + [pltpu.VMEM((T, N, 8, 128), f32)] * 2 + [pltpu.VMEM((T, 256), f32), pltpu.VMEM((256, T), jnp.bfloat16),
           pltpu.VMEM((T, 32, 128), f32)],
        compiler_params=pltpu.CompilerParams(vmem_limit_bytes=VMEM_LIMIT),
    )(step3, drive3, gs3, sig, x_conv, z, g, dskip, a2, bc, ent, wg, wg, low)


MESH = pl.DeviceIdType.MESH
ORDERS = (("x", "y", "z"), ("y", "z", "x"), ("z", "x", "y"))
GATHER_ROWS = ((0, 32), (32, 32), (64, 16))
ROWS = ((0, 32), (32, 16), (48, 32))
DIMS = {"z": 0, "x": 1, "y": 2}


def place():
    d, j = lax.axis_index("dp"), lax.axis_index("seq")
    return d, j, {"z": lax.div(j, 4), "x": lax.rem(j, 4), "y": lax.div(d, 2)}, lax.rem(d, 2)


def peer(pos, core, axis, hop):
    at = dict(pos)
    at[axis] = lax.rem(at[axis] + hop + 4, 4)
    return (at["y"] * 2 + core, at["z"] * 4 + at["x"])


OTHERS = [(a, b) for a in range(4) for b in range(4) if (a, b) != (0, 0)]


def peer2(pos, core, axes, hops):
    at = {a: lax.rem(pos[a] + h, 4) for a, h in zip(axes, hops)}
    at = {**pos, **at}
    return (at["y"] * 2 + core, at["z"] * 4 + at["x"])


def planes(pos, core):
    near = [peer(pos, core, axis, hop) for axis in "xyz" for hop in (1, 2, 3)]
    return near + [peer2(pos, core, axes, (a, b)) for axes in ("xy", "yz", "zx") for a, b in OTHERS if a and b]


def greet(devices):
    barrier = pltpu.get_barrier_semaphore()
    for device in devices:
        pl.semaphore_signal(barrier, inc=1, device_id=device, device_id_type=MESH)
    pl.semaphore_wait(barrier, len(devices))


def remote(src, dst, send_sem, recv_sem, device):
    return pltpu.make_async_remote_copy(
        src_ref=src, dst_ref=dst, send_sem=send_sem, recv_sem=recv_sem, device_id=device, device_id_type=MESH
    )


def slab(ref, fixed, tail):
    index = [slice(None)] * 3
    for axis, value in fixed.items():
        index[DIMS[axis]] = value
    return ref.at[tuple(index) + tail]


def gather_kernel(parts, with_tail, *refs):
    if with_tail:
        shard, tail_ref, out, halo, local_sem, ssem, rsem, fsend, frecv, csend, crecv, hsend, hrecv = refs
    else:
        shard, out, local_sem, ssem, rsem, fsend, frecv, csend, crecv = refs
    d, j, pos, core = place()
    sibling = (pos["y"] * 2 + 1 - core, j)
    following, previous = (d, lax.rem(j + 1, 16)), (d, lax.rem(j + 15, 16))
    greet(planes(pos, core) + [sibling] + ([previous] if with_tail else []))
    sent = []

    def go(copy):
        copy.start()
        sent.append(copy)

    own = out.at[pos["z"], pos["x"], pos["y"], core]
    local = pltpu.make_async_copy(shard, own, local_sem)
    local.start()
    half = out.shape[-1] // 2
    columns = (pl.ds(0, half), pl.ds(half, half))
    whole = slice(None)
    hops = (0, -1, 1, 2)

    def step(p, slot, axis, fixed):
        row, count = parts[p][1]
        rows = pl.ds(row, count)
        right, left = peer(pos, core, axis, 1), peer(pos, core, axis, -1)

        def at(hop, cols=whole, which=core):
            return slab(out, {**fixed, axis: lax.rem(pos[axis] + hop + 4, 4)}, (which, rows, cols))

        def ring(hop, cols, which, device):
            return remote(at(hop, cols), at(hop, cols), ssem.at[p, slot, which], rsem.at[p, slot, which], device)

        def send(which):
            hop, cols, device = ((0, whole, right), (0, whole, left), (-1, columns[0], right), (1, columns[1], left))[which]
            go(ring(hop, cols, which, device))

        def landed(which):
            hop, cols, device = ((-1, whole, right), (1, whole, left), (2, columns[0], right), (2, columns[1], left))[which]
            ring(hop, cols, which, device).wait_recv()

        def across(which):
            there = at(hops[which])
            go(remote(there, there, csend.at[p, slot, which], crecv.at[p, slot, which], sibling))

        def crossed(which):
            there = at(hops[which], whole, 1 - core)
            remote(there, there, csend.at[p, slot, which], crecv.at[p, slot, which], sibling).wait_recv()

        return send, landed, across, crossed

    count = range(len(parts))

    def spot(axis, hop):
        return lax.rem(pos[axis] + hop + 4, 4)

    def direct(p, k):
        (one, two, three), (row, rows) = parts[p]
        device = peer2(pos, core, (one, two), OTHERS[k])
        return remote(shard.at[pl.ds(row, rows), :], own.at[pl.ds(row, rows), :], fsend.at[p, k], frecv.at[p, k], device)

    def arrived(p, k):
        (one, two, three), (row, rows) = parts[p]
        a, b = OTHERS[k]
        there = slab(out, {one: spot(one, -a), two: spot(two, -b), three: pos[three]}, (core, pl.ds(row, rows), whole))
        remote(there, there, fsend.at[p, k], frecv.at[p, k], peer2(pos, core, (one, two), OTHERS[k])).wait_recv()

    third = []
    for p in count:
        one, two, three = parts[p][0]
        third.append([step(p, i, three, {two: spot(two, hops[i])}) for i in range(4)])
    turn = [[k for k, (a, b) in enumerate(OTHERS) if (-b) % 4 == hops[i] % 4] for i in range(4)]
    for i in range(4):
        for k in turn[i]:
            for p in count:
                go(direct(p, k))
    if with_tail:
        tail_copy = remote(tail_ref, halo, hsend, hrecv, following)
        go(tail_copy)
    local.wait()
    for i in range(4):
        for p in count:
            for k in turn[i]:
                arrived(p, k)
            send, _, across, _ = third[p][i]
            send(0)
            send(1)
            across(0)
    for i in range(4):
        for which in (0, 1):
            for p in count:
                send, landed, across, _ = third[p][i]
                landed(which)
                send(2 + which)
                across(1 + which)
    for i in range(4):
        for p in count:
            _, landed, across, _ = third[p][i]
            landed(2)
            landed(3)
            across(3)
    for i in range(4):
        for p in count:
            for which in range(4):
                third[p][i][3](which)
    if with_tail:
        tail_copy.wait_recv()
    for copy in sent:
        copy.wait_send()


def gather(shard, tail, parts, collective_id):
    rows, columns = shard.shape
    count = len(parts)
    anyspace = pl.BlockSpec(memory_space=pl.ANY)
    dma = pltpu.SemaphoreType.DMA
    out_shape = [jax.ShapeDtypeStruct((4, 4, 4, 2, rows, columns), shard.dtype)]
    sems = [dma, dma((count, 4, 4)), dma((count, 4, 4)), dma((count, 15)), dma((count, 15)), dma((count, 4, 4)), dma((count, 4, 4))]
    operands = [shard]
    if tail is not None:
        out_shape.append(jax.ShapeDtypeStruct(tail.shape, tail.dtype))
        sems += [dma, dma]
        operands.append(tail)
    return pl.pallas_call(
        functools.partial(gather_kernel, parts, tail is not None),
        name="gather_shards",
        out_shape=out_shape,
        in_specs=[anyspace] * len(operands),
        out_specs=[anyspace] * len(out_shape),
        scratch_shapes=sems,
        compiler_params=pltpu.CompilerParams(collective_id=collective_id, has_side_effects=True, vmem_limit_bytes=VMEM_LIMIT),
    )(*operands)


def reduce_kernel(xpart, dpart, edge, out, all_params, halo, sums, cross, *scratch):
    buffers, plane, scratch = scratch[:48], scratch[48:51], scratch[51:]
    own_sem, csend, crecv, ssem, rsem, fsend, frecv, psend, precv, qsend, qrecv, hsend, hrecv = scratch
    d, j, pos, core = place()
    sibling = (pos["y"] * 2 + 1 - core, j)
    following, previous = (d, lax.rem(j + 1, 16)), (d, lax.rem(j + 15, 16))
    greet(planes(pos, core) + [sibling, following])
    sent = []
    hops = (2, 1, -1, 0)
    half = 256
    whole = slice(None)
    columns = (slice(0, half), slice(half, 2 * half))

    def go(copy):
        copy.start()
        sent.append(copy)

    def spot(axis, hop):
        return lax.rem(pos[axis] + hop + 4, 4)

    def mine(p, i, which):
        row, count = ROWS[p]
        fixed = {ORDERS[p][1]: spot(ORDERS[p][1], hops[i])}
        return slab(xpart if p < 2 else dpart, fixed, (which, pl.ds(row if p < 2 else 0, count), whole))

    def beside(ref, p, i):
        row, count = ROWS[p]
        return slab(ref, {ORDERS[p][1]: spot(ORDERS[p][1], hops[i])}, (pl.ds(row, count), whole))

    def across(p, i):
        return remote(mine(p, i, 1 - core), beside(cross, p, i), csend.at[p, i], crecv.at[p, i], sibling)

    def own(p, i):
        return pltpu.make_async_copy(mine(p, i, core), beside(sums, p, i), own_sem.at[p, i])

    for i in range(4):
        for p in range(3):
            go(across(p, i))
            own(p, i).start()
    edge_copy = remote(edge, halo, hsend, hrecv, previous)
    go(edge_copy)

    def index_of(fixed, free, values):
        index = [None] * 3
        for a, v in {**fixed, **dict(zip(free, values))}.items():
            index[DIMS[a]] = v
        return tuple(index)

    def add_core(p, i):
        row, count = ROWS[p]
        rows = pl.ds(row, count)
        middle = ORDERS[p][1]
        free = [a for a in "zxy" if a != middle]
        own(p, i).wait()
        across(p, i).wait_recv()

        def one(k, _):
            at = index_of({middle: spot(middle, hops[i])}, free, (lax.div(k, 4), lax.rem(k, 4))) + (rows, whole)
            sums[at] = (sums[at].astype(jnp.float32) + cross[at].astype(jnp.float32)).astype(jnp.bfloat16)
            return 0

        lax.fori_loop(0, 16, one, 0)

    def step(p, slot, axis, fixed, free):
        row, count = ROWS[p]
        rows = pl.ds(row, count)
        right, left = peer(pos, core, axis, 1), peer(pos, core, axis, -1)
        bufs = buffers[(p * 4 + slot) * 4:(p * 4 + slot) * 4 + 4]

        def copy(which):
            hop, cols, device = ((2, columns[0], right), (2, columns[1], left), (1, whole, right), (-1, whole, left))[which]
            source = slab(sums, {**fixed, axis: spot(axis, hop)}, (rows, cols))
            return remote(source, bufs[which], ssem.at[p, slot, which], rsem.at[p, slot, which], device)

        def add(hop, cols, terms):
            def one(k, _):
                at = index_of({**fixed, axis: spot(axis, hop)}, free, (k,)) + (rows, cols)
                total = sums[at].astype(jnp.float32)
                for term in terms:
                    total = total + term[k].astype(jnp.float32)
                sums[at] = total.astype(jnp.bfloat16)
                return 0

            lax.fori_loop(0, 4, one, 0)

        def begin():
            go(copy(0))
            go(copy(1))

        def relay(which):
            copy(which).wait_recv()
            add((1, -1)[which], columns[which], bufs[which:which + 1])
            go(copy(2 + which))

        def finish():
            copy(2).wait_recv()
            copy(3).wait_recv()
            add(0, whole, bufs[2:])

        return begin, relay, finish

    def direct(p, k):
        one, two, three = ORDERS[p]
        a, b = OTHERS[k]
        row, count = ROWS[p]
        source = slab(sums, {one: spot(one, a), two: spot(two, b), three: pos[three]}, (pl.ds(row, count), whole))
        return remote(source, plane[p].at[k], fsend.at[p, k], frecv.at[p, k], peer2(pos, core, (one, two), (a, b)))

    parts = range(3)
    turn = [[k for k, (a, b) in enumerate(OTHERS) if b % 4 == hops[i] % 4] for i in range(4)]
    outer = []
    for p in parts:
        one, two, three = ORDERS[p]
        outer.append([step(p, i, three, {two: spot(two, hops[i])}, [one]) for i in range(4)])
    def relays(p, i):
        for which in (0, 1):
            outer[p][i][1](which)

    def finish(p):
        for i in range(4):
            outer[p][i][2]()
            for k in turn[i]:
                go(direct(p, k))

    def total(p):
        row, count = ROWS[p]
        rows = pl.ds(row, count)
        for k in range(15):
            direct(p, k).wait_recv()
        out[rows, :] = sums[pos["z"], pos["x"], pos["y"], rows, :].astype(jnp.float32)

        def one_more(k, _):
            out[rows, :] += plane[p][k].astype(jnp.float32)
            return 0

        lax.fori_loop(0, 15, one_more, 0)

    def place_of(hops):
        return all_params.at[lax.rem(pos["z"] + 4 - hops[0], 4), lax.rem(pos["x"] + 4 - hops[1], 4), pos["y"], core]

    def flat(k):
        return remote(place_of((0, 0)), place_of((0, 0)), psend.at[k], precv.at[k], peer2(pos, core, "zx", OTHERS[k]))

    def upright(hop):
        ours = all_params.at[:, :, pos["y"], core]
        return remote(ours, ours, qsend.at[hop], qrecv.at[hop], peer(pos, core, "y", hop))

    for i in range(4):
        for p in (1, 0, 2):
            add_core(p, i)
            outer[p][i][0]()
    for i in range(2):
        relays(1, 2 * i)
        for p in (0, 2):
            relays(p, i)
        relays(1, 2 * i + 1)
    finish(1)
    for p in (0, 2):
        relays(p, 2)
    total(1)

    rowsum = jnp.concatenate(
        [out[36 + q:37 + q, 128 * s:128 * s + 128] for q in range(3) for s in range(4)] + [jnp.zeros((4, 128), jnp.float32)], axis=0
    )
    all_params[pos["z"], pos["x"], pos["y"], core] = rowsum.astype(jnp.bfloat16)
    for k in range(15):
        go(flat(k))
    for p in (0, 2):
        relays(p, 3)
    for p in (0, 2):
        finish(p)
    for k in range(15):
        there = place_of(OTHERS[k])
        remote(there, there, psend.at[k], precv.at[k], peer2(pos, core, "zx", OTHERS[k])).wait_recv()
    for hop in (1, 2, 3):
        go(upright(hop))
    total(0)
    for hop in (1, 2, 3):
        there = all_params.at[:, :, lax.rem(pos["y"] + 4 - hop, 4), core]
        remote(there, there, qsend.at[hop], qrecv.at[hop], peer(pos, core, "y", hop)).wait_recv()
    ours, theirs = all_params.at[:, :, :, core], all_params.at[:, :, :, 1 - core]
    go(remote(ours, ours, qsend.at[0], qrecv.at[0], sibling))
    total(2)
    remote(theirs, theirs, qsend.at[0], qrecv.at[0], sibling).wait_recv()
    edge_copy.wait_recv()
    for copy in sent:
        copy.wait_send()


def reduce_all(xpart, dpart, edge):
    vmem = pl.BlockSpec(memory_space=pltpu.VMEM)
    anyspace = pl.BlockSpec(memory_space=pl.ANY)
    dma = pltpu.SemaphoreType.DMA
    bf16 = jnp.bfloat16
    buffers = []
    for row, count in ROWS:
        buffers += ([pltpu.VMEM((4, count, 256), bf16)] * 2 + [pltpu.VMEM((4, count, 512), bf16)] * 2) * 4
    buffers += [pltpu.VMEM((15, count, 512), bf16) for row, count in ROWS]
    return pl.pallas_call(
        reduce_kernel,
        name="reduce_shards",
        out_shape=[
            jax.ShapeDtypeStruct((80, 512), jnp.float32),
            jax.ShapeDtypeStruct((4, 4, 4, 2, 16, 128), bf16),
            jax.ShapeDtypeStruct(edge.shape, edge.dtype),
        ],
        in_specs=[anyspace] * 3,
        out_specs=[vmem, vmem, anyspace],
        scratch_shapes=[pltpu.VMEM((4, 4, 4, 80, 512), bf16)] * 2 + buffers + [
            dma((3, 4)), dma((3, 4)), dma((3, 4)), dma((3, 4, 4)), dma((3, 4, 4)), dma((3, 15)), dma((3, 15)),
            dma((15,)), dma((15,)), dma((4,)), dma((4,)), dma, dma,
        ],
        compiler_params=pltpu.CompilerParams(
            collective_id=2, has_side_effects=True, vmem_limit_bytes=VMEM_LIMIT
        ),
    )(xpart, dpart, edge)


def spread(rows, columns, row_is_plain):
    index = lax.broadcasted_iota(jnp.int32, (rows, columns), 0 if row_is_plain else 1)
    padded = lax.broadcasted_iota(jnp.int32, (rows, columns), 1 if row_is_plain else 0)
    low = 32 * lax.div(lax.rem(index, 128), 16) + 16 * lax.div(index, 128) + lax.rem(index, 16)
    plain = jnp.where(index < 256, low, index)
    device = lax.div(padded, 48)
    inside = padded - 48 * device
    return jnp.where((inside < 36) & (36 * device + inside == plain), 1.0, 0.0).astype(jnp.bfloat16)


HALO = pl.BlockSpec((3, 8, 128), lambda i: (0, i, 0))


def convolve(x_ref, halo_ref, cw_ref, cb_ref, ext):
    first = lax.axis_index("seq") == 0
    for r in range(3):
        for s in range(8):
            ext[5 + r:6 + r, 128 * s:128 * s + 128] = jnp.where(first, 0.0, halo_ref[r, s:s + 1, :])
    ext[8:T + 8, :] = x_ref[...].astype(jnp.float32)

    def part(cols):
        pre = cb_ref[:, cols] + cw_ref[0:1, cols] * ext[5:5 + T, cols]
        for k in range(1, 4):
            pre = pre + cw_ref[k:k + 1, cols] * ext[5 + k:5 + k + T, cols]
        gate = logistic(pre)
        act = pre * gate
        return act.astype(jnp.bfloat16), gate + act * (1.0 - gate)

    return part


def conv_kernel(x_ref, halo_ref, cw_ref, cb_ref, w_ref, xc_ref, low_ref, bc_ref, ext, acc):
    i = pl.program_id(0)

    @pl.when(i == 0)
    def _():
        acc[...] = jnp.zeros(acc.shape, jnp.float32)

    part = convolve(x_ref, halo_ref, cw_ref, cb_ref, ext)
    for half in range(2):
        cols = slice(512 * half, 512 * half + 512)
        xc, _ = part(cols)
        xc_ref[:, cols] = xc
        acc[...] += lax.dot_general(
            xc, w_ref[half].reshape(384, 512), (((1,), (1,)), ((), ())), preferred_element_type=jnp.float32
        )

    @pl.when(i == pl.num_programs(0) - 1)
    def _():
        low_ref[...] = jnp.dot(
            acc[...].astype(jnp.bfloat16), spread(384, 256, False), preferred_element_type=jnp.float32
        ).astype(jnp.bfloat16)
        for n in range(32):
            bc_ref[n] = jnp.broadcast_to(acc[:, 340 + n:341 + n], (T, 128))


def conv_project(x, halo, cw, cb, wg):
    E = x.shape[1]
    nat, row, full = tile_specs(1024)
    S = jax.ShapeDtypeStruct
    return pl.pallas_call(
        conv_kernel, grid=(E // 1024,), name="conv_project",
        in_specs=[nat, HALO, row(4), row(1), pl.BlockSpec((2, 8, 48, 512), lambda i: (i, 0, 0, 0))],
        out_specs=[nat, full(T, 256), full(32, T, 128)],
        out_shape=[S((T, E), jnp.bfloat16), S((T, 256), jnp.bfloat16), S((32, T, 128), jnp.float32)],
        scratch_shapes=[pltpu.VMEM((T + 8, 1024), jnp.float32), pltpu.VMEM((T, 384), jnp.float32)],
        compiler_params=pltpu.CompilerParams(vmem_limit_bytes=VMEM_LIMIT),
    )(x, halo, cw, cb, wg)


def grads_kernel(glow_ref, gbc_ref, gcx_ref, x_ref, halo_ref, cw_ref, cb_ref, w_ref, par_ref, ga_ref,
                 gx_ref, head_ref, tail_ref, part_ref, gproj, turned, ext, wide, gext):
    i = pl.program_id(0)
    f32 = jnp.float32

    @pl.when(i == 0)
    def _():
        plain = jnp.concatenate([glow_ref[...], gbc_ref[...]], axis=1).astype(jnp.bfloat16)
        gproj[...] = jnp.dot(plain, spread(288, 384, True), preferred_element_type=f32).astype(jnp.bfloat16)
        turned[...] = gproj[...].T
        gext[T:T + 8, :] = jnp.zeros((8, gext.shape[1]), f32)

    part = convolve(x_ref, halo_ref, cw_ref, cb_ref, ext)
    for half in range(2):
        cols = slice(512 * half, 512 * half + 512)
        xc, slope = part(cols)
        weights = w_ref[half].reshape(384, 512)
        g_conv = (gcx_ref[:, cols] + jnp.dot(gproj[...], weights, preferred_element_type=f32)) * slope
        gext[0:T, cols] = g_conv
        wide[...] = jnp.dot(turned[...], xc, preferred_element_type=f32)

        def put(r, value):
            wide[48 * (r // 3) + 36 + r % 3:48 * (r // 3) + 37 + r % 3, :] = value

        for k in range(4):
            put(k, jnp.sum(g_conv * ext[5 + k:5 + k + T, cols], axis=0, keepdims=True))
        put(4, jnp.sum(g_conv, axis=0, keepdims=True))
        put(5, par_ref[0:1, cols])
        put(6, par_ref[1:2, cols])
        for n in range(N):
            put(7 + n, jnp.concatenate([ga_ref[n, 4 * half + s:4 * half + s + 1, :] for s in range(4)], axis=1))
        part_ref[half] = wide[...].reshape(8, 48, 512).astype(jnp.bfloat16)
    total = cw_ref[0:1, :] * gext[3:3 + T, :]
    for k in range(1, 4):
        total = total + cw_ref[k:k + 1, :] * gext[3 - k:3 - k + T, :]
    gx_ref[...] = total.astype(jnp.bfloat16)
    for r in range(3):
        for s in range(8):
            head_ref[r, s:s + 1, :] = gext[r:r + 1, 128 * s:128 * s + 128]
    tail_ref[...] = gext[T - 16:T, :]


def weight_grads(glow, gbc, gcx, x, halo, cw, cb, wg, par, ga):
    E = x.shape[1]
    nat, row, full = tile_specs(1024)
    S = jax.ShapeDtypeStruct
    f32 = jnp.float32
    block = pl.BlockSpec((2, 8, 48, 512), lambda i: (i, 0, 0, 0))
    return pl.pallas_call(
        grads_kernel, grid=(E // 1024,), name="weight_grads",
        in_specs=[full(T, 256), full(T, 32), nat, nat, HALO, row(4), row(1), block, row(8),
                  pl.BlockSpec((N, 8, 128), lambda i: (0, i, 0))],
        out_specs=[nat, HALO, row(16), block],
        out_shape=[S((T, E), jnp.bfloat16), S((3, E // 128, 128), f32), S((16, E), f32), S((E // 512, 8, 48, 512), jnp.bfloat16)],
        scratch_shapes=[pltpu.VMEM((T, 384), jnp.bfloat16), pltpu.VMEM((384, T), jnp.bfloat16), pltpu.VMEM((T + 8, 1024), f32),
                        pltpu.VMEM((384, 512), f32),
                        pltpu.VMEM((T + 8, 1024), f32)],
        compiler_params=pltpu.CompilerParams(vmem_limit_bytes=VMEM_LIMIT),
    )(glow, gbc, gcx, x, halo, cw, cb, wg, par, ga)


def last_rows_kernel(gx_ref, tail_ref, edge_ref, cw_ref, out_ref, ext):
    ext[0:16, :] = tail_ref[...]
    last = lax.axis_index("seq") == 15
    for r in range(3):
        for s in range(edge_ref.shape[1]):
            ext[16 + r:17 + r, 128 * s:128 * s + 128] = jnp.where(last, 0.0, edge_ref[r, s:s + 1, :])
    total = cw_ref[0:1, :] * ext[3:19, :]
    for k in range(1, 4):
        total = total + cw_ref[k:k + 1, :] * ext[3 - k:19 - k, :]
    out_ref[...] = total.astype(jnp.bfloat16)


def last_rows(gx, tail, edge, cw):
    E = gx.shape[1]
    full = lambda *shape: pl.BlockSpec(shape, lambda i: (0,) * len(shape))
    block = pl.BlockSpec((16, E), lambda i: (T // 16 - 1, 0))
    return pl.pallas_call(
        last_rows_kernel, grid=(1,), name="last_rows",
        in_specs=[block, full(16, E), full(3, E // 128, 128), full(4, E)], out_specs=block,
        out_shape=jax.ShapeDtypeStruct((T, E), jnp.bfloat16),
        scratch_shapes=[pltpu.VMEM((24, E), jnp.float32)],
        input_output_aliases={0: 0},
        compiler_params=pltpu.CompilerParams(vmem_limit_bytes=VMEM_LIMIT),
    )(gx, tail, edge, cw)


def local(x_branch, z_branch, out_grad, x_weight, dt_weight, conv_weight, conv_bias, dt_bias, a_log, d_skip):
    x, z, g = x_branch[0], z_branch[0], out_grad[0]
    E = x.shape[1]
    shard = jnp.concatenate([x_weight.T, jnp.zeros((12, 512), jnp.bfloat16), dt_weight], axis=0)
    gathered, halo = gather(shard, x[T - 3:].astype(jnp.float32).reshape(3, E // 128, 128), tuple(zip(ORDERS, GATHER_ROWS)), 0)
    wg = gathered.reshape(16, 8, 80, 512)
    a2_wide = -jnp.exp(a_log) * LOG2E
    a2 = a2_wide.reshape(N, E // 128, 128)
    bias = conv_bias[None]
    xc, low, bc = conv_project(x, halo, conv_weight, bias, wg)
    step3, drive3, gs3, sig, carried = local_scan(low, wg, xc, z, g, dt_bias[None], a2, bc)
    mixer_out, grad_z, gcx, gdt, par, ga, glow, gbc = main_scan(
        step3, drive3, gs3, sig, xc, z, g, d_skip[None], a2, bc, carried, wg, low
    )
    gx, head, tail, part = weight_grads(glow, gbc, gcx, x, halo, conv_weight, bias, wg, par, ga)
    reduced, params, edge = reduce_all(part.reshape(4, 4, 4, 2, 48, 512), gdt.reshape(4, 4, 4, 2, 32, 512), head)
    grad_x = last_rows(gx, tail, edge, conv_weight)
    params = params.reshape(16, 8, 16, 128)[:, :, :12].reshape(16, 8, 3, 4, 128)
    params = params.transpose(1, 2, 0, 3, 4).reshape(24, E).astype(jnp.float32)
    return (
        mixer_out[None], grad_x[None], grad_z[None], reduced[:36].T, reduced[48:80],
        params[0:4], params[4], params[5], params[7:23], params[6],
    )


def solution(mesh):
    tokens, weights, whole = P("dp", "seq", None), P("seq", "dp"), P()
    in_specs = (tokens,) * 3 + (weights, P("dp", "seq")) + (whole,) * 5
    out_specs = (tokens,) * 3 + (weights, P("dp", "seq")) + (whole,) * 5
    return jax.shard_map(local, mesh=mesh, in_specs=in_specs, out_specs=out_specs, check_vma=False)
```
